32 devices in a mesh: walk: 8 (over z, x), pt: 4 (over y, core).
Axes of the slice: x: 2, y: 2, z: 4, core: 2. Of those that a mesh axis runs over, the one named last changes fastest.
Arguments:
- bra_orbitals: bfloat16 [8, 1536, 160], P('walk'), may hold values from -6 to 6
- ket_orbitals: bfloat16 [8, 1536, 160], P('walk'), may hold values from -6 to 6
- collocation: bfloat16 [12288, 1536], P('pt'), may hold values from -0.15625 to 0.15625
- kernel: bfloat16 [12288, 12288], P('pt', 'walk'), as said below
- walker_weight: float32 [8], P('walk'), may hold values from 0.3 to 3
- walker_group: int32 [8], P('walk'), may hold values from 0 to 19
- group_occupied: int32 [20], replicated, may hold values from 80 to 160, as said below
Outputs:
- gradient: float32 [12288, 1536], P('pt', 'walk')
The draws below stay inside these ranges and needn't reach their ends.
Inputs may be any that keep to these rules, and one draw needn't show every extreme that they name: kernel is symmetric. `group_occupied`: some group has exactly 160 occupied orbitals.
All inputs are finite; a program needn't handle non-finite values.
Results may differ from the reference program's by a relative error of at most 0.0064.
Values may be sent and summed in bfloat16 or wider, within the bound.
No kernel may reach another device: no remote copies, remote signals or barrier semaphores. Data moves between devices by JAX's collectives and lax.ppermute only.
A program may use at most 192 MiB of HBM per device.

```python
import math
import jax
import jax.numpy as jnp
from jax import lax

M = 1536
NOCC = 160
P_SIZE = 12288
GROUPS = 20
WALKERS = 8
N_PT = 4


def draw_kernel(key, part):
    values = jax.random.normal(key, (P_SIZE, P_SIZE), jnp.float32)
    factor = 1.0 / math.sqrt(2.0 * P_SIZE * NOCC)
    return ((values + values.T) * factor).astype(jnp.bfloat16)


def draw_group_occupied(key, part):
    counts = jax.random.randint(key, (GROUPS,), NOCC // 2, NOCC + 1, dtype=jnp.int32)
    chosen = jax.random.randint(jax.random.fold_in(key, 7), (), 0, GROUPS, dtype=jnp.int32)
    positions = jnp.arange(GROUPS, dtype=jnp.int32)
    return jnp.where(positions == chosen, NOCC, counts).astype(jnp.int32)


def with_ends(values, stream_key, smallest, top_value):
    longest = values.shape.index(max(values.shape))
    spots = []
    for shift in (0, 1):
        where = [jax.random.randint(jax.random.fold_in(stream_key, axis), (), 0, length) for axis, length in enumerate(values.shape)]
        where[longest] = (where[longest] + shift) % values.shape[longest]
        spots.append(tuple(where))
    return values.at[spots[0]].set(smallest).at[spots[1]].set(top_value)


def shard_levels(stream_key, shape, cuts, least, largest):
    def one(dim, blocks):
        heights = jax.random.uniform(jax.random.fold_in(jax.random.fold_in(stream_key, 6), dim), (blocks,), jnp.float32, least / len(cuts), largest / len(cuts))
        return jnp.repeat(jnp.exp(heights), shape[dim] // blocks).reshape((-1,) + (1,) * (len(shape) - dim - 1))

    loudness = one(*cuts[0])
    for cut in cuts[1:]:
        loudness = loudness * one(*cut)
    return loudness


def bell_draw(key, shape, spread, bound, shards=(), kind=jnp.bfloat16):
    values = spread * jax.random.normal(key, shape, jnp.float32)
    if shards:
        values = values * shard_levels(key, shape, shards, -0.22, 0.18)
    return jnp.clip(values, -bound, bound).astype(kind)


def setup_inputs(seed: int = 0) -> dict:
    streams_of = jax.random.split(jax.random.key(seed), 8)
    bra_orbitals = bell_draw(streams_of[0], (WALKERS, M, NOCC), 1.0, 6.0, ((0, 8),))
    ket_orbitals = bell_draw(streams_of[1], (WALKERS, M, NOCC), 1.0, 6.0, ((0, 8),))
    collocation = bell_draw(streams_of[2], (P_SIZE, M), M ** -0.5, 0.15625, ((0, 4),))
    kernel = draw_kernel(jax.random.fold_in(streams_of[7], 71), 0)
    walker_weight = jnp.clip(jnp.exp(math.log(3.0) - 2.3025851 * jax.random.uniform(streams_of[4], (WALKERS,), jnp.float32) ** shard_levels(streams_of[4], (WALKERS,), ((0, 8),), -0.2, 0.2)), 0.3, 3.0)
    walker_group = with_ends(jax.random.randint(streams_of[5], (WALKERS,), 0, GROUPS), jax.random.fold_in(streams_of[5], 1), 0, GROUPS - 1).astype(jnp.int32)
    group_occupied = draw_group_occupied(jax.random.fold_in(streams_of[7], 71), 0)
    return {"bra_orbitals": bra_orbitals, "ket_orbitals": ket_orbitals, "collocation": collocation, "kernel": kernel, "walker_weight": walker_weight, "walker_group": walker_group, "group_occupied": group_occupied}


def reference(bra_orbitals, ket_orbitals, collocation, kernel, walker_weight, walker_group, group_occupied):
    occupied = group_occupied[walker_group]
    masks = (jnp.arange(NOCC, dtype=jnp.int32)[None, :] < occupied[:, None]).astype(jnp.bfloat16)
    shares = walker_weight / jnp.sum(walker_weight)
    block_rows = P_SIZE // N_PT

    def one_walker(totals, inputs):
        bra_raw, ket_raw, mask_row, share_one = inputs
        left_bra = bra_raw * mask_row[None, :]
        right_ket = ket_raw * mask_row[None, :]
        lefts = jnp.dot(collocation, left_bra, preferred_element_type=jnp.float32).astype(jnp.bfloat16)
        rights = jnp.dot(collocation, right_ket, preferred_element_type=jnp.float32).astype(jnp.bfloat16)

        def block(begin):
            left_rows = lax.dynamic_slice_in_dim(lefts, begin, block_rows, 0)
            right_rows = lax.dynamic_slice_in_dim(rights, begin, block_rows, 0)
            kernel_rows = lax.dynamic_slice_in_dim(kernel, begin, block_rows, 0).astype(jnp.float32)
            green_t = jnp.dot(right_rows, lefts.T, preferred_element_type=jnp.float32)
            green = jnp.dot(left_rows, rights.T, preferred_element_type=jnp.float32)
            hadamard_t = (kernel_rows * green_t).astype(jnp.bfloat16)
            hadamard = (kernel_rows * green).astype(jnp.bfloat16)
            grad_left = (2.0 * jnp.dot(hadamard_t, rights, preferred_element_type=jnp.float32)).astype(jnp.bfloat16)
            grad_right = (2.0 * jnp.dot(hadamard, lefts, preferred_element_type=jnp.float32)).astype(jnp.bfloat16)
            return jnp.dot(grad_left, left_bra.T, preferred_element_type=jnp.float32) + jnp.dot(grad_right, right_ket.T, preferred_element_type=jnp.float32)

        starts = jnp.arange(N_PT, dtype=jnp.int32) * block_rows
        term = lax.map(block, starts).reshape(P_SIZE, M)
        return totals + share_one * term, None

    start_total = jnp.zeros((P_SIZE, M), jnp.float32)
    result, unused = lax.scan(one_walker, start_total, (bra_orbitals, ket_orbitals, masks, shares))
    return result
```

```python
import functools

import jax
import jax.numpy as jnp
from jax import lax
from jax.experimental import pallas as pl
from jax.experimental.pallas import tpu as pltpu
from jax.sharding import PartitionSpec as P

F32 = jnp.float32
BF16 = jnp.bfloat16
BOTH = ("walk", "pt")


def largest_tile(size, limit):
    tile = limit
    while size % tile:
        tile //= 2
    return tile


def pair_kernel(tile_b, share_ref, kt_ref, lrp_ref, lrq_ref, out_ref):
    occ = lrp_ref.shape[0] // 2
    rows, size_b = kt_ref.shape[0], lrp_ref.shape[1]
    tile_a = lrq_ref.shape[1]
    scale = 2.0 * share_ref[pl.program_id(0)]
    begin = pl.multiple_of(pl.program_id(1) * tile_a, tile_a)
    left_a = lrq_ref[:occ, :].T
    right_a = lrq_ref[occ:, :].T
    nt = (((1,), (1,)), ((), ()))
    total_l = jnp.zeros((tile_a, occ), F32)
    total_r = jnp.zeros((tile_a, occ), F32)
    for at in range(0, size_b, tile_b):
        left_t = lrp_ref[:occ, at : at + tile_b]
        right_t = lrp_ref[occ:, at : at + tile_b]
        kern = kt_ref[pl.ds(begin, tile_a), at : at + tile_b].astype(F32)
        green_t = jnp.dot(right_a, left_t, preferred_element_type=F32)
        had_t = (kern * green_t).astype(BF16)
        green = jnp.dot(left_a, right_t, preferred_element_type=F32)
        had = (kern * green).astype(BF16)
        total_l += lax.dot_general(had_t, right_t, nt, preferred_element_type=F32)
        total_r += lax.dot_general(had, left_t, nt, preferred_element_type=F32)
    out_ref[:occ, :] = (total_l * scale).astype(BF16).T
    out_ref[occ:, :] = (total_r * scale).astype(BF16).T


def pair_gradients(share, kernel_t, lrp, lrq, walkers):
    size_a, size_b = kernel_t.shape
    width = lrp.shape[0] // walkers
    tile_a = largest_tile(size_a, 512)
    tile_b = largest_tile(size_b, 512)
    return pl.pallas_call(
        functools.partial(pair_kernel, tile_b),
        out_shape=jax.ShapeDtypeStruct((lrp.shape[0], size_a), BF16),
        grid_spec=pltpu.PrefetchScalarGridSpec(
            num_scalar_prefetch=1,
            grid=(walkers, size_a // tile_a),
            in_specs=[
                pl.BlockSpec((size_a, size_b), lambda w, a, s: (0, 0), pipeline_mode=pl.Buffered(1)),
                pl.BlockSpec((width, size_b), lambda w, a, s: (w, 0)),
                pl.BlockSpec((width, tile_a), lambda w, a, s: (w, a)),
            ],
            out_specs=pl.BlockSpec((width, tile_a), lambda w, a, s: (w, a)),
        ),
        compiler_params=pltpu.CompilerParams(vmem_limit_bytes=56 * 1024 * 1024),
        cost_estimate=pl.CostEstimate(
            flops=2 * 4 * lrp.shape[0] // 2 * size_a * size_b,
            bytes_accessed=2 * (size_a * size_b + 2 * lrp.size + 2 * lrq.size),
            transcendentals=0,
        ),
    )(share, kernel_t, lrp, lrq)


def send(x, axes, pairs):
    return lax.ppermute(x, axes, pairs)


def gather_ring(own, count):
    z_size = count // 2
    walk = range(count)
    mine = [own]
    for r in range(1, z_size):
        mine.append(send(own, "walk", [(j, (j - 2 * r) % count) for j in walk]))
    across = [send(part, "walk", [(j, j ^ 1) for j in walk]) for part in mine]
    slots = []
    for part in [p for pair in zip(mine, across) for p in pair]:
        other = send(part, "pt", [(i, i ^ 1) for i in range(4)])
        slots += [part, other]
    return jnp.concatenate(slots, axis=0)


def on_device(nw, npt, bra_orbitals, ket_orbitals, collocation, kernel, walker_weight, walker_group, group_occupied):
    group_count = group_occupied.shape[0]
    local, size_m, occ = bra_orbitals.shape
    walkers = nw * local
    size_b, size_a = kernel.shape
    me_w, me_p = lax.axis_index("walk"), lax.axis_index("pt")
    fast = nw == 8 and npt == 4 and local == 1 and size_b == 2 * size_a and size_m % nw == 0

    matches = walker_group[:, None] == jnp.arange(group_count, dtype=jnp.int32)[None, :]
    occupied = jnp.sum(jnp.where(matches, group_occupied[None, :], 0), axis=1)
    masks = (jnp.arange(occ, dtype=jnp.int32)[None, :] < occupied[:, None]).astype(BF16)
    bra_t = jnp.swapaxes(bra_orbitals * masks[:, None, :], 1, 2)
    ket_t = jnp.swapaxes(ket_orbitals * masks[:, None, :], 1, 2)
    weights = lax.all_gather(walker_weight, "walk", axis=0, tiled=True)
    shares = weights / jnp.sum(weights)
    kernel_t = kernel.T

    if fast:
        parity = me_p % 2
        own = jnp.where(parity == 0, bra_t[0], ket_t[0])
        orbitals = gather_ring(own, nw)
        slot = jnp.arange(walkers, dtype=jnp.int32)
        shares = shares[((me_w // 2 + slot // 2) % (nw // 2)) * 2 + (me_w + slot) % 2]
        z = me_w // 2
        rows = lax.dynamic_slice_in_dim(collocation, (me_w % 2) * size_a, size_a, 0)
        far = send(rows, BOTH, [(j * npt + j // 2, j * npt + (j // 2 ^ 2)) for j in range(nw)])
        near = jnp.where(me_p == z, rows, far)
        swap = [(j * npt + (j // 2 ^ s), j * npt + (j // 2 ^ s ^ 1)) for j in range(nw) for s in (0, 2)]
        col_q = jnp.where(parity == z % 2, near, send(near, BOTH, swap))
    else:
        both = jnp.concatenate([bra_t, ket_t], axis=1).reshape(local * 2 * occ, size_m)
        orbitals = lax.all_gather(both, "walk", axis=0, tiled=True)
        owner = (me_w * size_a) // size_b
        all_rows = lax.all_gather(collocation, "pt", axis=0, tiled=True)
        col_q = lax.dynamic_slice_in_dim(all_rows, me_w * size_a, size_a, 0)

    nt = (((1,), (1,)), ((), ()))
    lrp = lax.dot_general(orbitals, collocation, nt, preferred_element_type=F32).astype(BF16)
    lrq = lax.dot_general(orbitals, col_q, nt, preferred_element_type=F32).astype(BF16)
    grads = pair_gradients(shares, kernel_t, lrp, lrq, walkers)
    tn = (((0,), (0,)), ((), ()))
    part = lax.dot_general(orbitals, grads, tn, preferred_element_type=F32)

    if fast:
        half, quarter, eighth = size_m // 2, size_m // 4, size_m // 8
        y = me_p // 2
        part = part.astype(BF16)
        give = lax.dynamic_slice_in_dim(part, (1 - parity) * half, half, 0)
        keep = lax.dynamic_slice_in_dim(part, parity * half, half, 0)
        got = send(give, "pt", [(i, i ^ 1) for i in range(npt)])
        part = (keep.astype(F32) + got.astype(F32)).astype(BF16)
        give = lax.dynamic_slice_in_dim(part, (1 - y) * quarter, quarter, 0)
        keep = lax.dynamic_slice_in_dim(part, y * quarter, quarter, 0)
        got = send(give, "pt", [(i, i ^ 2) for i in range(npt)])
        part = (keep.astype(F32) + got.astype(F32)).astype(BF16)
        x = me_w % 2
        landed = []
        for t in (0, 1):
            piece = lax.dynamic_slice_in_dim(part, (x ^ t) * eighth, eighth, 0)
            pairs = []
            for j in range(nw):
                for i in range(npt):
                    quarter_of = 2 * (i % 2) + i // 2
                    pairs.append((j * npt + i, (2 * quarter_of + (j % 2 ^ t)) * npt + j // 2))
            landed.append(send(piece, BOTH, pairs))
        first = jnp.where(x == 0, landed[0], landed[1])
        second = jnp.where(x == 0, landed[1], landed[0])
        return jnp.concatenate([first, second], axis=1).astype(F32).T
    part = lax.psum(part, "pt")
    part = jnp.where(owner == me_p, part, 0.0)
    wide = jnp.zeros((size_m, size_b), F32)
    wide = lax.dynamic_update_slice_in_dim(wide, part, (me_w * size_a) % size_b, 1)
    return lax.psum_scatter(wide, "walk", scatter_dimension=0, tiled=True).T


def solution(mesh):
    in_specs = (
        P("walk", None, None),
        P("walk", None, None),
        P("pt", None),
        P("pt", "walk"),
        P("walk"),
        P("walk"),
        P(),
    )
    out_specs = P("pt", "walk")
    body = functools.partial(on_device, mesh.shape["walk"], mesh.shape["pt"])
    return jax.shard_map(body, mesh=mesh, in_specs=in_specs, out_specs=out_specs, check_vma=False)
```

```python
import functools

import jax
import jax.numpy as jnp
from jax import lax
from jax.experimental import pallas as pl
from jax.experimental.pallas import tpu as pltpu
from jax.sharding import PartitionSpec as P

F32 = jnp.float32
BF16 = jnp.bfloat16
BOTH = ("walk", "pt")
NT = (((1,), (1,)), ((), ()))
TN = (((0,), (0,)), ((), ()))
VMEM_LIMIT = 56 * 1024 * 1024


def tile_of(size, limit):
    return next(t for t in range(min(size, limit), 0, -128) if size % t == 0)


def dot(a, b, dims=(((1,), (0,)), ((), ()))):
    return lax.dot_general(a, b, dims, preferred_element_type=F32)


def cost(flops, nbytes):
    return pl.CostEstimate(flops=flops, bytes_accessed=nbytes, transcendentals=0)


def turn_kernel(in_ref, out_ref):
    out_ref[...] = in_ref[...].T


def turned(block):
    rows, cols = block.shape
    tr, tc = tile_of(rows, 512), tile_of(cols, 512)
    return pl.pallas_call(
        turn_kernel,
        out_shape=jax.ShapeDtypeStruct((cols, rows), block.dtype),
        grid=(cols // tc, rows // tr),
        in_specs=[pl.BlockSpec((tr, tc), lambda c, r: (r, c))],
        out_specs=pl.BlockSpec((tc, tr), lambda c, r: (c, r)),
        compiler_params=pltpu.CompilerParams(vmem_limit_bytes=VMEM_LIMIT),
        cost_estimate=cost(0, 4 * rows * cols),
    )(block)


def columns_kernel(count, *refs):
    items, col_ref, out_ref, stack = refs[:count], refs[count], refs[count + 1], refs[count + 2]
    width = items[0].shape[0]

    @pl.when(pl.program_id(0) == 0)
    def _():
        for s in range(count):
            stack[s * width : (s + 1) * width, :] = items[s][...]

    out_ref[...] = dot(stack[...], col_ref[...], NT).astype(BF16)


def project_columns(items, col):
    count, (width, size_m), size = len(items), items[0].shape, col.shape[0]
    tile = tile_of(size, 512)
    return pl.pallas_call(
        functools.partial(columns_kernel, count),
        out_shape=jax.ShapeDtypeStruct((count * width, size), BF16),
        grid=(size // tile,),
        in_specs=[pl.BlockSpec((width, size_m), lambda b: (0, 0))] * count
        + [pl.BlockSpec((tile, size_m), lambda b: (b, 0))],
        out_specs=pl.BlockSpec((count * width, tile), lambda b: (0, b)),
        scratch_shapes=[pltpu.VMEM((count * width, size_m), BF16)],
        compiler_params=pltpu.CompilerParams(vmem_limit_bytes=VMEM_LIMIT),
        cost_estimate=cost(2 * count * width * size_m * size, 2 * size_m * size),
    )(*items, col)


def rows_kernel(count, *refs):
    items, col_ref, out_ref = refs[:count], refs[count], refs[count + 1]
    occ = items[0].shape[0] // 2
    for s in range(count):
        for side in (0, 1):
            out_ref[2 * s + side] = dot(col_ref[...], items[s][side * occ : (side + 1) * occ, :], NT).astype(BF16)


def project_rows(items, col):
    count, (width, size_m), size = len(items), items[0].shape, col.shape[0]
    tile = tile_of(size, 384)
    return pl.pallas_call(
        functools.partial(rows_kernel, count),
        out_shape=jax.ShapeDtypeStruct((2 * count, size, width // 2), BF16),
        grid=(size // tile,),
        in_specs=[pl.BlockSpec((width, size_m), lambda b: (0, 0))] * count
        + [pl.BlockSpec((tile, size_m), lambda b: (b, 0))],
        out_specs=pl.BlockSpec((2 * count, tile, width // 2), lambda b: (0, b, 0)),
        compiler_params=pltpu.CompilerParams(vmem_limit_bytes=VMEM_LIMIT),
        cost_estimate=cost(2 * count * width * size_m * size, 2 * size_m * size),
    )(*items, col)


def pair_kernel(parts, groups, sub, share_ref, *refs):
    kts, refs = refs[:parts], refs[parts:]
    lrps, refs = refs[: parts * groups], refs[parts * groups :]
    lrqs, out_ref, totals = refs[:groups], refs[groups], refs[groups + 1]
    item, step = pl.program_id(0), pl.program_id(1)
    occ = lrps[0].shape[0] // 2
    tile = kts[0].shape[1]

    @pl.when(step == 0)
    def _():
        totals[...] = jnp.zeros_like(totals)

    for g in range(groups):
        sum_l, sum_r = totals[2 * g], totals[2 * g + 1]
        left_a, right_a = lrqs[g][0], lrqs[g][1]
        for h in range(parts):
            for at in range(0, tile, sub):
                left_t = lrps[g * parts + h][:occ, at : at + sub]
                right_t = lrps[g * parts + h][occ:, at : at + sub]
                kern = kts[h][:, at : at + sub]
                had_t = kern * dot(right_a, left_t).astype(BF16)
                had = kern * dot(left_a, right_t).astype(BF16)
                sum_l += dot(had_t, right_t, NT)
                sum_r += dot(had, left_t, NT)
        totals[2 * g], totals[2 * g + 1] = sum_l, sum_r

    @pl.when(step == pl.num_programs(1) - 1)
    def _():
        for g in range(groups):
            scale = 2.0 * share_ref[g * pl.num_programs(0) + item]
            for side in (0, 1):
                out_ref[g, 0, side * occ : (side + 1) * occ, :] = (totals[2 * g + side] * scale).astype(BF16).T


def pair_gradients(share, kts, row_at, lrps, lrqs):
    parts, groups = len(kts), len(lrqs)
    size_b = kts[0].shape[1]
    sides, chunk, occ = lrqs[0].shape
    count, width = sides // 2, 2 * occ
    tile = tile_of(size_b, 1024 // groups)
    sub = tile_of(tile, 512)
    at = row_at // chunk
    return pl.pallas_call(
        functools.partial(pair_kernel, parts, groups, sub),
        out_shape=jax.ShapeDtypeStruct((groups, count, width, chunk), BF16),
        grid_spec=pltpu.PrefetchScalarGridSpec(
            num_scalar_prefetch=1,
            grid=(count, size_b // tile),
            in_specs=[pl.BlockSpec((chunk, tile), lambda w, b, s: (at, b))] * parts
            + [pl.BlockSpec((width, tile), lambda w, b, s: (w, b))] * (parts * groups)
            + [pl.BlockSpec((2, chunk, occ), lambda w, b, s: (w, 0, 0))] * groups,
            out_specs=pl.BlockSpec((groups, 1, width, chunk), lambda w, b, s: (0, w, 0, 0)),
            scratch_shapes=[pltpu.VMEM((2 * groups, chunk, occ), F32)],
        ),
        compiler_params=pltpu.CompilerParams(vmem_limit_bytes=VMEM_LIMIT),
        cost_estimate=cost(
            2 * 4 * groups * count * 256 * chunk * size_b * parts, 2 * groups * count * chunk * size_b * parts
        ),
    )(share, *kts, *[x for group in lrps for x in group], *lrqs)


def send(x, axes, pairs):
    return lax.ppermute(x, axes, pairs)


def masked_orbitals(bra_orbitals, ket_orbitals, walker_group, group_occupied):
    group_count, occ = group_occupied.shape[0], bra_orbitals.shape[2]
    matches = walker_group[:, None] == jnp.arange(group_count, dtype=jnp.int32)[None, :]
    occupied = jnp.sum(jnp.where(matches, group_occupied[None, :], 0), axis=1)
    masks = (jnp.arange(occ, dtype=jnp.int32)[None, :] < occupied[:, None]).astype(BF16)
    bra_t = jnp.swapaxes(bra_orbitals * masks[:, None, :], 1, 2)
    ket_t = jnp.swapaxes(ket_orbitals * masks[:, None, :], 1, 2)
    return jnp.concatenate([bra_t, ket_t], axis=1)


def on_device_8x4(own, collocation, kernel, walker_weight):
    nw, npt = 8, 4
    size_b, size_a = kernel.shape
    size_m = collocation.shape[1]
    me_w, me_p = lax.axis_index("walk"), lax.axis_index("pt")
    z, x, y, core = me_w // 2, me_w % 2, me_p // 2, me_p % 2

    def put(j, i):
        return j * npt + i

    swap_core = [(i, i ^ 1) for i in range(npt)]
    order = (0, 1, 3, 2)
    found = [own]
    for r in order[1:]:
        pairs = [(put(j, i), put((j - 2 * r) % nw, i)) for j in range(nw) for i in (0, 2)]
        found.append(send(own, BOTH, pairs))
    to_side = [(put(j, i), put(j ^ 1, i + 1)) for j in range(nw) for i in (0, 2)]
    items = [jnp.where(core == 0, part, send(part, BOTH, to_side)) for part in found]

    chunks = [(0, size_a // 2), (size_a // 2, size_a // 2)]
    cols_q = []
    for begin, chunk in chunks:
        rows = lax.dynamic_slice_in_dim(collocation, x * size_a + begin, chunk, 0)
        far = send(rows, BOTH, [(put(j, j // 2), put(j, j // 2 ^ 2)) for j in range(nw)])
        near = jnp.where(me_p == z, rows, far)
        pairs = [(put(j, j // 2 ^ s), put(j, j // 2 ^ s ^ 1)) for j in range(nw) for s in (0, 2)]
        cols_q.append(jnp.where(core == z % 2, near, send(near, BOTH, pairs)))

    kernel_t = turned(kernel)
    col_other = send(collocation, "pt", swap_core)
    kernel_t_other = send(kernel_t, "pt", swap_core)
    kts = [kernel_t, kernel_t_other]

    weights = walker_weight.reshape(1, 1)
    weights = jnp.concatenate([weights, send(weights, "walk", [(j, j ^ 1) for j in range(nw)])], axis=1)
    for r in (1, 2):
        pairs = [(j, (j - 2 * r) % nw) for j in range(nw)]
        weights = jnp.concatenate([weights, send(weights, "walk", pairs)], axis=0)
    share_table = weights / jnp.sum(weights)
    shares = jnp.stack([jnp.where(core == 0, share_table[r, 0], share_table[r, 1]) for r in order])

    pairs_of = [items[:2], items[2:]]
    lrps = [[project_columns(two, collocation), project_columns(two, col_other)] for two in pairs_of]

    stacked = jnp.concatenate(items, axis=0)
    half, quarter, eighth = size_m // 2, size_m // 4, size_m // 8
    give_items = lax.dynamic_slice_in_dim(stacked, (1 - core) * half, half, 1)
    keep_items = lax.dynamic_slice_in_dim(stacked, core * half, half, 1)

    landed = []
    for c, (begin, chunk) in enumerate(chunks):
        lrqs = [project_rows(two, cols_q[c]) for two in pairs_of]
        if c == 0:
            grads = jnp.concatenate(
                [pair_gradients(shares[2 * g : 2 * g + 2], kts, begin, [lrps[g]], [lrqs[g]]) for g in (0, 1)]
            )
        else:
            grads = pair_gradients(shares, kts, begin, lrps, lrqs)
        grads = grads.reshape(stacked.shape[0], chunk)
        got = send(dot(give_items, grads, TN).astype(BF16), "pt", swap_core)
        part = dot(keep_items, grads, TN) + got.astype(F32)
        give = lax.dynamic_slice_in_dim(part, (1 - y) * quarter, quarter, 0).astype(BF16)
        keep = lax.dynamic_slice_in_dim(part, y * quarter, quarter, 0)
        got = send(give, "pt", [(i, i ^ 2) for i in range(npt)])
        part = (keep + got.astype(F32)).astype(BF16)
        came = []
        for t in (0, 1):
            piece = lax.dynamic_slice_in_dim(part, (x ^ t) * eighth, eighth, 0)
            pairs = []
            for j in range(nw):
                for i in range(npt):
                    quarter_of = 2 * (i % 2) + i // 2
                    pairs.append((put(j, i), put(2 * quarter_of + (j % 2 ^ t), j // 2)))
            came.append(send(piece, BOTH, pairs))
        landed.append(came)
    first = jnp.concatenate([jnp.where(x == 0, came[0], came[1]) for came in landed], axis=1)
    second = jnp.concatenate([jnp.where(x == 0, came[1], came[0]) for came in landed], axis=1)
    return jnp.concatenate([first, second], axis=1).astype(F32).T


def on_device_any(nw, own, collocation, kernel, walker_weight):
    size_b, size_a = kernel.shape
    local, size_m = walker_weight.shape[0], collocation.shape[1]
    width = own.shape[0] // local
    me_w, me_p = lax.axis_index("walk"), lax.axis_index("pt")
    weights = lax.all_gather(walker_weight, "walk", axis=0, tiled=True)
    orbitals = lax.all_gather(own, "walk", axis=0, tiled=True)
    all_rows = lax.all_gather(collocation, "pt", axis=0, tiled=True)
    col_q = lax.dynamic_slice_in_dim(all_rows, me_w * size_a, size_a, 0)
    items = [orbitals[s * width : (s + 1) * width] for s in range(nw * local)]
    lrp = dot(orbitals, collocation, NT).astype(BF16)
    lrq = project_rows(items, col_q)
    grads = pair_gradients(weights / jnp.sum(weights), [turned(kernel)], 0, [[lrp]], [lrq])
    part = lax.psum(dot(orbitals, grads.reshape(orbitals.shape[0], size_a), TN), "pt")
    part = jnp.where((me_w * size_a) // size_b == me_p, part, 0.0)
    wide = lax.dynamic_update_slice_in_dim(jnp.zeros((size_m, size_b), F32), part, (me_w * size_a) % size_b, 1)
    return lax.psum_scatter(wide, "walk", scatter_dimension=0, tiled=True).T


def on_device(
    nw, npt, bra_orbitals, ket_orbitals, collocation, kernel, walker_weight, walker_group, group_occupied
):
    own = masked_orbitals(bra_orbitals, ket_orbitals, walker_group, group_occupied)
    own = own.reshape(-1, own.shape[2])
    if (nw, npt, walker_weight.shape[0]) == (8, 4, 1) and kernel.shape[0] == 2 * kernel.shape[1]:
        return on_device_8x4(own, collocation, kernel, walker_weight)
    return on_device_any(nw, own, collocation, kernel, walker_weight)


def solution(mesh):
    in_specs = (
        P("walk", None, None),
        P("walk", None, None),
        P("pt", None),
        P("pt", "walk"),
        P("walk"),
        P("walk"),
        P(),
    )
    out_specs = P("pt", "walk")
    body = functools.partial(on_device, mesh.shape["walk"], mesh.shape["pt"])
    return jax.shard_map(body, mesh=mesh, in_specs=in_specs, out_specs=out_specs, check_vma=False)
```

```python
import functools

import jax
import jax.numpy as jnp
from jax import lax
from jax.experimental import pallas as pl
from jax.experimental.pallas import tpu as pltpu
from jax.sharding import PartitionSpec as P

F32 = jnp.float32
BF16 = jnp.bfloat16
BOTH = ("walk", "pt")
NT = (((1,), (1,)), ((), ()))
TN = (((0,), (0,)), ((), ()))
VMEM_LIMIT = 56 * 1024 * 1024


def tile_of(size, limit):
    return next(t for t in range(min(size, limit), 0, -128) if size % t == 0)


def dot(a, b, dims=(((1,), (0,)), ((), ()))):
    return lax.dot_general(a, b, dims, preferred_element_type=F32)


def cost(flops, nbytes):
    return pl.CostEstimate(flops=flops, bytes_accessed=nbytes, transcendentals=0)


def turn_kernel(in_ref, out_ref):
    out_ref[...] = in_ref[...].T


def turned(block):
    rows, cols = block.shape
    tr, tc = tile_of(rows, 512), tile_of(cols, 512)
    return pl.pallas_call(
        turn_kernel,
        out_shape=jax.ShapeDtypeStruct((cols, rows), block.dtype),
        grid=(cols // tc, rows // tr),
        in_specs=[pl.BlockSpec((tr, tc), lambda c, r: (r, c))],
        out_specs=pl.BlockSpec((tc, tr), lambda c, r: (c, r)),
        compiler_params=pltpu.CompilerParams(vmem_limit_bytes=VMEM_LIMIT),
        cost_estimate=cost(0, 10 * rows * cols),
    )(block)


def pack_kernel(group_ref, occupied_ref, side_ref, weight_ref, bra_ref, ket_ref, own_ref, half_ref):
    occ = bra_ref.shape[0]
    used = occupied_ref[group_ref[0]]
    kept = lax.broadcasted_iota(jnp.int32, bra_ref.shape, 0) < used
    bra_t = jnp.where(kept, bra_ref[...].astype(F32), 0.0).astype(BF16)
    ket_t = jnp.where(kept, ket_ref[...].astype(F32), 0.0).astype(BF16)
    own_ref[:occ, :] = bra_t
    own_ref[occ:, :] = ket_t

    @pl.when(side_ref[0] == 0)
    def _():
        half_ref[:occ, :] = bra_t

    @pl.when(side_ref[0] != 0)
    def _():
        half_ref[:occ, :] = ket_t

    shape = (half_ref.shape[0] - occ, half_ref.shape[1])
    row = lax.broadcasted_iota(jnp.int32, shape, 0)
    rest, rows = jnp.full(shape, weight_ref[0], F32), jnp.zeros(shape, F32)
    for part in range(3):
        near = rest.astype(BF16).astype(F32)
        rows = jnp.where(row == part, near, rows)
        rest = rest - near
    half_ref[occ:, :] = rows.astype(BF16)


def packed(bra, ket, group, occupied, side, weight):
    occ, size_m = bra.shape
    smem = pl.BlockSpec(memory_space=pltpu.SMEM)
    return pl.pallas_call(
        pack_kernel,
        out_shape=[
            jax.ShapeDtypeStruct((2 * occ, size_m), BF16),
            jax.ShapeDtypeStruct((occ + 16, size_m), BF16),
        ],
        in_specs=[smem] * 4 + [pl.BlockSpec(memory_space=pltpu.VMEM)] * 2,
        compiler_params=pltpu.CompilerParams(vmem_limit_bytes=VMEM_LIMIT),
        cost_estimate=cost(0, 12 * size_m * occ),
    )(group, occupied, side, weight, bra, ket)


def columns_kernel(count, rows_each, waits, *refs):
    items, col_ref, refs = refs[:count], refs[count], refs[count + 1 + waits :]
    out_ref, stack = refs[0], refs[-1]

    @pl.when(pl.program_id(0) == 0)
    def _():
        at = 0
        for ref, rows in zip(items, rows_each):
            stack[at : at + rows, :] = ref[:rows, :]
            at += rows
        if len(refs) > 2:
            refs[1][...] = stack[...]

    out_ref[...] = dot(stack[...], col_ref[...], NT).astype(BF16)


def project(items, rows_each, col, keep_stack, after=()):
    count, size_m, size, total = len(items), col.shape[1], col.shape[0], sum(rows_each)
    tile = tile_of(size, 512)
    return pl.pallas_call(
        functools.partial(columns_kernel, count, tuple(rows_each), len(after)),
        out_shape=[
            jax.ShapeDtypeStruct((total, size), BF16),
            jax.ShapeDtypeStruct((total, size_m), BF16),
        ][: 1 + keep_stack],
        grid=(size // tile,),
        in_specs=[pl.BlockSpec(x.shape, lambda b: (0, 0), pipeline_mode=pl.Buffered(1)) for x in items]
        + [pl.BlockSpec((tile, size_m), lambda b: (b, 0))]
        + [pl.BlockSpec(memory_space=pl.ANY)] * len(after),
        out_specs=[
            pl.BlockSpec((total, tile), lambda b: (0, b)),
            pl.BlockSpec((total, size_m), lambda b: (0, 0), pipeline_mode=pl.Buffered(1)),
        ][: 1 + keep_stack],
        scratch_shapes=[pltpu.VMEM((total, size_m), BF16)],
        compiler_params=pltpu.CompilerParams(vmem_limit_bytes=VMEM_LIMIT),
        cost_estimate=cost(2 * total * size_m * size + 2 * 2 * 640 * size_m * size, 2 * size_m * size),
    )(*items, col, *after)


def pair_kernel(parts, groups, sub, waits, share_ref, *refs):
    kts, refs = refs[:parts], refs[parts:]
    lrps, refs = refs[: parts * groups], refs[parts * groups :]
    lrqs, refs = refs[:groups], refs[groups + waits :]
    out_ref, sides_a, totals = refs
    item, step = pl.program_id(0), pl.program_id(1)
    occ = lrps[0].shape[0] // 2
    tile = kts[0].shape[1]

    @pl.when(step == 0)
    def _():
        totals[...] = jnp.zeros_like(totals)
        for g in range(groups):
            for side in (0, 1):
                sides_a[2 * g + side] = lrqs[g][side * occ : (side + 1) * occ, :].T

    for g in range(groups):
        sum_l, sum_r = totals[2 * g], totals[2 * g + 1]
        left_a, right_a = sides_a[2 * g], sides_a[2 * g + 1]
        for h in range(parts):
            for at in range(0, tile, sub):
                left_t = lrps[g * parts + h][:occ, at : at + sub]
                right_t = lrps[g * parts + h][occ:, at : at + sub]
                kern = kts[h][:, at : at + sub]
                had_t = kern * dot(right_a, left_t).astype(BF16)
                had = kern * dot(left_a, right_t).astype(BF16)
                sum_l += dot(had_t, right_t, NT)
                sum_r += dot(had, left_t, NT)
        totals[2 * g], totals[2 * g + 1] = sum_l, sum_r

    @pl.when(step == pl.num_programs(1) - 1)
    def _():
        for g in range(groups):
            scale = 2.0 * share_ref[g * pl.num_programs(0) + item]
            for side in (0, 1):
                out_ref[g, 0, side * occ : (side + 1) * occ, :] = (totals[2 * g + side] * scale).astype(BF16).T


def pair_gradients(share, kts, row_at, lrps, lrqs, after=()):
    parts, groups, count = len(kts), len(lrqs), share.shape[0] // len(lrqs)
    size_b = kts[0].shape[1]
    width, chunk = lrqs[0].shape[0] // count, lrqs[0].shape[1]
    occ = width // 2
    tile = tile_of(size_b, 1024 // groups)
    sub = tile_of(tile, 512)
    at = row_at // chunk
    return pl.pallas_call(
        functools.partial(pair_kernel, parts, groups, sub, len(after)),
        out_shape=jax.ShapeDtypeStruct((groups, count, width, chunk), BF16),
        grid_spec=pltpu.PrefetchScalarGridSpec(
            num_scalar_prefetch=1,
            grid=(count, size_b // tile),
            in_specs=[pl.BlockSpec((chunk, tile), lambda w, b, s: (at, b))] * parts
            + [pl.BlockSpec((width, tile), lambda w, b, s: (w, b))] * (parts * groups)
            + [pl.BlockSpec((width, chunk), lambda w, b, s: (w, 0))] * groups
            + [pl.BlockSpec(memory_space=pl.ANY)] * len(after),
            out_specs=pl.BlockSpec((groups, 1, width, chunk), lambda w, b, s: (0, w, 0, 0)),
            scratch_shapes=[
                pltpu.VMEM((2 * groups, chunk, occ), BF16),
                pltpu.VMEM((2 * groups, chunk, occ), F32),
            ],
        ),
        compiler_params=pltpu.CompilerParams(vmem_limit_bytes=VMEM_LIMIT),
        cost_estimate=cost(
            2 * 4 * groups * count * 256 * chunk * size_b * parts, 2 * groups * count * chunk * size_b * parts
        ),
    )(share, *kts, *[x for group in lrps for x in group], *lrqs, *after)


def send(x, axes, pairs):
    return lax.ppermute(x, axes, pairs)


def masked_orbitals(bra_orbitals, ket_orbitals, walker_group, group_occupied):
    group_count, occ = group_occupied.shape[0], bra_orbitals.shape[2]
    matches = walker_group[:, None] == jnp.arange(group_count, dtype=jnp.int32)[None, :]
    occupied = jnp.sum(jnp.where(matches, group_occupied[None, :], 0), axis=1)
    masks = (jnp.arange(occ, dtype=jnp.int32)[None, :] < occupied[:, None]).astype(BF16)
    bra_t = jnp.swapaxes(bra_orbitals * masks[:, None, :], 1, 2)
    ket_t = jnp.swapaxes(ket_orbitals * masks[:, None, :], 1, 2)
    return jnp.concatenate([bra_t, ket_t], axis=1)


def on_device_8x4(bra, ket, collocation, kernel, walker_weight, walker_group, group_occupied):
    nw, npt = 8, 4
    size_b, size_a = kernel.shape
    occ, size_m = bra.shape
    width = 2 * occ
    me_w, me_p = lax.axis_index("walk"), lax.axis_index("pt")
    z, x, y, core = me_w // 2, me_w % 2, me_p // 2, me_p % 2

    def put(j, i):
        return j * npt + i

    def across(part):
        return send(part, "walk", [(j, j ^ 1) for j in range(nw)])

    def along(part, r):
        return send(part, "walk", [(j, (j - 2 * r) % nw) for j in range(nw)])

    def other(part):
        return send(part, "pt", [(i, i ^ 1) for i in range(npt)])

    def columns_q(begin, chunk):
        rows = lax.dynamic_slice_in_dim(collocation, x * size_a + begin, chunk, 0)
        far = send(rows, BOTH, [(put(j, j // 2), put(j, j // 2 ^ 2)) for j in range(nw)])
        near = jnp.where(me_p == z, rows, far)
        pairs = [(put(j, j // 2 ^ s), put(j, j // 2 ^ s ^ 1)) for j in range(nw) for s in (0, 2)]
        return jnp.where(core == z % 2, near, send(near, BOTH, pairs))

    def weight_of(part):
        return jnp.sum(part[occ : occ + 3, 0].astype(F32))

    chunks = [(0, 2 * size_a // 3), (2 * size_a // 3, size_a // 3)]
    own, half = packed(bra, ket, walker_group, group_occupied, core.reshape(1), walker_weight)
    cols_q = [columns_q(*chunk) for chunk in chunks]
    z1, z3, x0 = along(half, 1), along(half, 3), across(half)
    z2 = along(half, 2)
    x1, x3, x2 = across(z1), across(z3), across(z2)
    groups = [[own, x0, other(x0)], [h for part in (z1, z3, x1, x3, z2, x2) for h in (part, other(part))]]
    rows_each = [[width, occ, occ], [occ] * 12]
    weights = [
        jnp.stack([walker_weight[0], weight_of(x0)]),
        jnp.stack([weight_of(part) for part in (z1, z3, x1, x3, z2, x2)]),
    ]
    total = jnp.sum(weights[0]) + jnp.sum(weights[1])

    kts = [turned(kernel)]

    def gradients(g, c, lrp, after=()):
        (lrq,) = project(groups[g], rows_each[g], cols_q[c], False)
        return pair_gradients(weights[g], kts, chunks[c][0], [[lrp]], [lrq], after).reshape(sum(rows_each[g]), -1)

    lrp_0, stack_0 = project(groups[0], rows_each[0], collocation, True)
    first_grads = gradients(0, 0, lrp_0)
    lrp_1, stack_1 = project(groups[1], rows_each[1], collocation, True, (first_grads,))

    half_m, quarter, eighth = size_m // 2, size_m // 4, size_m // 8
    landed, after = [], ()
    for c in range(len(chunks)):
        grads_0 = first_grads if c == 0 else gradients(0, c, lrp_0, after)
        grads_1 = gradients(1, c, lrp_1, after)
        part = dot(stack_0, grads_0, TN) + dot(stack_1, grads_1, TN)
        give = lax.dynamic_slice_in_dim(part, (1 - core) * half_m, half_m, 0).astype(BF16)
        keep = lax.dynamic_slice_in_dim(part, core * half_m, half_m, 0)
        part = keep + other(give).astype(F32)
        give = lax.dynamic_slice_in_dim(part, (1 - y) * quarter, quarter, 0).astype(BF16)
        keep = lax.dynamic_slice_in_dim(part, y * quarter, quarter, 0)
        after = (give,)
        got = send(give, "pt", [(i, i ^ 2) for i in range(npt)])
        part = (keep + got.astype(F32)).astype(BF16)
        came = []
        for t in (0, 1):
            piece = lax.dynamic_slice_in_dim(part, (x ^ t) * eighth, eighth, 0)
            pairs = []
            for j in range(nw):
                for i in range(npt):
                    quarter_of = 2 * (i % 2) + i // 2
                    pairs.append((put(j, i), put(2 * quarter_of + (j % 2 ^ t), j // 2)))
            came.append(send(piece, BOTH, pairs))
        landed.append(came)
    first = jnp.concatenate([jnp.where(x == 0, came[0], came[1]) for came in landed], axis=1)
    second = jnp.concatenate([jnp.where(x == 0, came[1], came[0]) for came in landed], axis=1)
    return (jnp.concatenate([first, second], axis=1).astype(F32) / total).T


def on_device_any(nw, own, collocation, kernel, walker_weight):
    size_b, size_a = kernel.shape
    local, size_m = walker_weight.shape[0], collocation.shape[1]
    me_w, me_p = lax.axis_index("walk"), lax.axis_index("pt")
    weights = lax.all_gather(walker_weight, "walk", axis=0, tiled=True)
    orbitals = lax.all_gather(own, "walk", axis=0, tiled=True)
    all_rows = lax.all_gather(collocation, "pt", axis=0, tiled=True)
    col_q = lax.dynamic_slice_in_dim(all_rows, me_w * size_a, size_a, 0)
    lrp = dot(orbitals, collocation, NT).astype(BF16)
    lrq = dot(orbitals, col_q, NT).astype(BF16)
    grads = pair_gradients(weights / jnp.sum(weights), [turned(kernel)], 0, [[lrp]], [lrq])
    part = lax.psum(dot(orbitals, grads.reshape(orbitals.shape[0], size_a), TN), "pt")
    part = jnp.where((me_w * size_a) // size_b == me_p, part, 0.0)
    wide = lax.dynamic_update_slice_in_dim(jnp.zeros((size_m, size_b), F32), part, (me_w * size_a) % size_b, 1)
    return lax.psum_scatter(wide, "walk", scatter_dimension=0, tiled=True).T


def on_device(
    nw, npt, bra_orbitals, ket_orbitals, collocation, kernel, walker_weight, walker_group, group_occupied
):
    if (nw, npt, walker_weight.shape[0]) == (8, 4, 1) and kernel.shape[0] == 2 * kernel.shape[1]:
        bra, ket = bra_orbitals[0].T, ket_orbitals[0].T
        return on_device_8x4(bra, ket, collocation, kernel, walker_weight, walker_group, group_occupied)
    own = masked_orbitals(bra_orbitals, ket_orbitals, walker_group, group_occupied)
    return on_device_any(nw, own.reshape(-1, own.shape[2]), collocation, kernel, walker_weight)


def solution(mesh):
    in_specs = (
        P("walk", None, None),
        P("walk", None, None),
        P("pt", None),
        P("pt", "walk"),
        P("walk"),
        P("walk"),
        P(),
    )
    out_specs = P("pt", "walk")
    body = functools.partial(on_device, mesh.shape["walk"], mesh.shape["pt"])
    return jax.shard_map(body, mesh=mesh, in_specs=in_specs, out_specs=out_specs, check_vma=False)
```

```python
import functools

import jax
import jax.numpy as jnp
from jax import lax
from jax.experimental import pallas as pl
from jax.experimental.pallas import tpu as pltpu
from jax.sharding import PartitionSpec as P

F32 = jnp.float32
BF16 = jnp.bfloat16
BOTH = ("walk", "pt")
NT = (((1,), (1,)), ((), ()))
VMEM_LIMIT = 56 * 1024 * 1024


def tile_of(size, limit):
    return next(t for t in range(min(size, limit), 0, -128) if size % t == 0)


def dot(a, b, dims=(((1,), (0,)), ((), ()))):
    return lax.dot_general(a, b, dims, preferred_element_type=F32)


def cost(flops, nbytes):
    return pl.CostEstimate(flops=flops, bytes_accessed=nbytes, transcendentals=0)


def turn_kernel(in_ref, out_ref):
    out_ref[...] = in_ref[...].T


def turned(block):
    rows, cols = block.shape
    tr, tc = tile_of(rows, 512), tile_of(cols, 512)
    return pl.pallas_call(
        turn_kernel,
        out_shape=jax.ShapeDtypeStruct((cols, rows), block.dtype),
        grid=(cols // tc, rows // tr),
        in_specs=[pl.BlockSpec((tr, tc), lambda c, r: (r, c))],
        out_specs=pl.BlockSpec((tc, tr), lambda c, r: (c, r)),
        compiler_params=pltpu.CompilerParams(vmem_limit_bytes=VMEM_LIMIT),
        cost_estimate=cost(0, 10 * rows * cols),
    )(block)


def pack_kernel(group_ref, occupied_ref, side_ref, weight_ref, bra_ref, ket_ref, own_ref, half_ref):
    occ = bra_ref.shape[0]
    used = occupied_ref[group_ref[0]]
    kept = lax.broadcasted_iota(jnp.int32, bra_ref.shape, 0) < used
    bra_t = jnp.where(kept, bra_ref[...].astype(F32), 0.0).astype(BF16)
    ket_t = jnp.where(kept, ket_ref[...].astype(F32), 0.0).astype(BF16)
    own_ref[:occ, :] = bra_t
    own_ref[occ : 2 * occ, :] = ket_t

    @pl.when(side_ref[0] == 0)
    def _():
        half_ref[:occ, :] = bra_t

    @pl.when(side_ref[0] != 0)
    def _():
        half_ref[:occ, :] = ket_t

    shape = (half_ref.shape[0] - occ, half_ref.shape[1])
    row = lax.broadcasted_iota(jnp.int32, shape, 0)
    rest, rows = jnp.full(shape, weight_ref[0], F32), jnp.zeros(shape, F32)
    for part in range(3):
        near = rest.astype(BF16).astype(F32)
        rows = jnp.where(row == part, near, rows)
        rest = rest - near
    half_ref[occ:, :] = rows.astype(BF16)
    own_ref[2 * occ :, :] = rows.astype(BF16)


def packed(bra, ket, group, occupied, side, weight):
    occ, size_m = bra.shape
    smem = pl.BlockSpec(memory_space=pltpu.SMEM)
    return pl.pallas_call(
        pack_kernel,
        out_shape=[
            jax.ShapeDtypeStruct((2 * occ + 16, size_m), BF16),
            jax.ShapeDtypeStruct((occ + 16, size_m), BF16),
        ],
        in_specs=[smem] * 4 + [pl.BlockSpec(memory_space=pltpu.VMEM)] * 2,
        compiler_params=pltpu.CompilerParams(vmem_limit_bytes=VMEM_LIMIT),
        cost_estimate=cost(0, 12 * size_m * occ),
    )(group, occupied, side, weight, bra, ket)


def project_kernel(rows_each, waits, *refs):
    count = len(rows_each)
    items, col_ref = refs[:count], refs[count]
    out_ref, stack_out, weight_out, stack = refs[count + 1 + waits :]
    occ = min(rows_each)

    @pl.when(pl.program_id(0) == 0)
    def _():
        at = 0
        weight_out[...] = jnp.zeros_like(weight_out)
        for ref, rows in zip(items, rows_each):
            stack[at : at + rows, :] = ref[:rows, :]
            if at % (2 * occ) == 0:
                s = at // (2 * occ)
                weight_out[s : s + 1, :] = jnp.sum(ref[rows : rows + 16, :128].astype(F32), axis=0, keepdims=True)
            at += rows
        stack_out[...] = stack[...]

    out_ref[...] = dot(stack[...], col_ref[...], NT).astype(BF16)


def project(items, rows_each, col, groups, index, before=(), after=()):
    size_m, size, total = col.shape[1], col.shape[0], sum(rows_each)
    tile = tile_of(size, 512)
    hbm, waits = pl.BlockSpec(memory_space=pl.ANY), (*before, *after)
    return pl.pallas_call(
        functools.partial(project_kernel, tuple(rows_each), len(waits)),
        out_shape=[
            jax.ShapeDtypeStruct((groups * total, size), BF16),
            jax.ShapeDtypeStruct((groups * total, size_m), BF16),
            jax.ShapeDtypeStruct((groups * 8, 128), F32),
        ],
        grid=(size // tile,),
        in_specs=[pl.BlockSpec(x.shape, lambda b: (0, 0), pipeline_mode=pl.Buffered(1)) for x in items]
        + [pl.BlockSpec((tile, size_m), lambda b: (b, 0))]
        + [hbm] * len(waits),
        out_specs=[
            pl.BlockSpec((total, tile), lambda b: (index, b)),
            pl.BlockSpec((total, size_m), lambda b: (index, 0), pipeline_mode=pl.Buffered(1)),
            pl.BlockSpec((8, 128), lambda b: (index, 0)),
        ],
        scratch_shapes=[pltpu.VMEM((total, size_m), BF16)],
        input_output_aliases={len(items) + 1 + n: n for n in range(len(before))},
        compiler_params=pltpu.CompilerParams(vmem_limit_bytes=VMEM_LIMIT),
        cost_estimate=cost(2 * (total + 640) * size_m * size, 2 * size_m * size),
    )(*items, col, *waits)


def pair_kernel(sub, first, waits, weight_ref, kt_ref, lrp_ref, lrq_ref, *refs):
    out_ref, sides, totals = refs[waits:]
    occ = sides.shape[2]
    count = sides.shape[0] // 2
    for n in range(2 * count):
        sides[n] = lrq_ref[:, n * occ : (n + 1) * occ]
    totals[...] = jnp.zeros_like(totals)

    def columns(t, carry):
        at = pl.ds(pl.multiple_of(t * sub, sub), sub)
        kern = kt_ref[:, at]
        for n in range(count):
            left_t = lrp_ref[2 * n * occ : (2 * n + 1) * occ, at]
            right_t = lrp_ref[(2 * n + 1) * occ : (2 * n + 2) * occ, at]
            had_t = kern * dot(sides[2 * n + 1], left_t).astype(BF16)
            had = kern * dot(sides[2 * n], right_t).astype(BF16)
            totals[2 * n] += dot(had_t, right_t, NT)
            totals[2 * n + 1] += dot(had, left_t, NT)
        return carry

    lax.fori_loop(0, kt_ref.shape[1] // sub, columns, 0)
    for n in range(2 * count):
        scale = 2.0 * weight_ref[(first + pl.program_id(0)) * count + n // 2]
        out_ref[:, n * occ : (n + 1) * occ] = (totals[n] * scale).astype(BF16)


def pair_gradients(weights, kernel_t, lrp, lrq, row_at, pairs=None, after=()):
    size_b, rows, count = kernel_t.shape[1], lrq.shape[0], weights.shape[0] // 2
    first, last = pairs or (0, count)
    width = lrp.shape[0] // count
    occ = width // 4
    at, sub = row_at // rows, tile_of(size_b, 512)
    return pl.pallas_call(
        functools.partial(pair_kernel, sub, first, len(after)),
        out_shape=jax.ShapeDtypeStruct((rows, (last - first) * width), BF16),
        grid_spec=pltpu.PrefetchScalarGridSpec(
            num_scalar_prefetch=1,
            grid=(last - first,),
            in_specs=[
                pl.BlockSpec((rows, size_b), lambda p, s: (at, 0), pipeline_mode=pl.Buffered(1)),
                pl.BlockSpec((width, size_b), lambda p, s: (first + p, 0)),
                pl.BlockSpec((rows, width), lambda p, s: (0, first + p)),
            ]
            + [pl.BlockSpec(memory_space=pl.ANY)] * len(after),
            out_specs=pl.BlockSpec((rows, width), lambda p, s: (0, p)),
            scratch_shapes=[pltpu.VMEM((4, rows, occ), BF16), pltpu.VMEM((4, rows, occ), F32)],
        ),
        compiler_params=pltpu.CompilerParams(vmem_limit_bytes=VMEM_LIMIT),
        cost_estimate=cost(
            2 * 4 * (last - first) * 2 * 256 * rows * size_b, 2 * (last - first) * (rows + width) * size_b
        ),
    )(weights, kernel_t, lrp, lrq, *after)


def send(x, axes, pairs):
    return lax.ppermute(x, axes, pairs)


def masked_orbitals(bra_orbitals, ket_orbitals, walker_group, group_occupied):
    group_count, occ = group_occupied.shape[0], bra_orbitals.shape[2]
    matches = walker_group[:, None] == jnp.arange(group_count, dtype=jnp.int32)[None, :]
    occupied = jnp.sum(jnp.where(matches, group_occupied[None, :], 0), axis=1)
    masks = (jnp.arange(occ, dtype=jnp.int32)[None, :] < occupied[:, None]).astype(BF16)
    bra_t = jnp.swapaxes(bra_orbitals * masks[:, None, :], 1, 2)
    ket_t = jnp.swapaxes(ket_orbitals * masks[:, None, :], 1, 2)
    return jnp.concatenate([bra_t, ket_t], axis=1)


def on_device_8x4(bra, ket, collocation, kernel, walker_weight, walker_group, group_occupied):
    nw, npt = 8, 4
    size_b, size_a = kernel.shape
    occ, size_m = bra.shape
    width = 2 * occ
    me_w, me_p = lax.axis_index("walk"), lax.axis_index("pt")
    z, x, y, core = me_w // 2, me_w % 2, me_p // 2, me_p % 2

    def put(j, i):
        return j * npt + i

    def across(part):
        return send(part, "walk", [(j, j ^ 1) for j in range(nw)])

    def along(part, r):
        return send(part, "walk", [(j, (j - 2 * r) % nw) for j in range(nw)])

    def other(part):
        return send(part, "pt", [(i, i ^ 1) for i in range(npt)])

    def columns_q(begin, chunk):
        rows = lax.dynamic_slice_in_dim(collocation, x * size_a + begin, chunk, 0)
        far = send(rows, BOTH, [(put(j, j // 2), put(j, j // 2 ^ 2)) for j in range(nw)])
        near = jnp.where(me_p == z, rows, far)
        pairs = [(put(j, j // 2 ^ s), put(j, j // 2 ^ s ^ 1)) for j in range(nw) for s in (0, 2)]
        return jnp.where(core == z % 2, near, send(near, BOTH, pairs))

    def split(part, at, size, axis=1):
        give = lax.dynamic_slice_in_dim(part, (1 - at) * size, size, axis).astype(BF16)
        return give, lax.dynamic_slice_in_dim(part, at * size, size, axis)

    chunks = [(0, 2 * size_a // 3), (2 * size_a // 3, size_a // 3)]
    own, half = packed(bra, ket, walker_group, group_occupied, core.reshape(1), walker_weight)
    cols_q = [columns_q(*chunk) for chunk in chunks]
    z1, z3, x0 = along(half, 1), along(half, 3), across(half)
    z2 = along(half, 2)
    kernel_t = turned(kernel)
    x0, z1, z3, kernel_t = lax.optimization_barrier((x0, z1, z3, kernel_t))
    x1, x3, x2 = across(z1), across(z3), across(z2)
    near_four = [own] + [h for part in (x0, z1, z3) for h in (part, other(part))]
    far_four = [h for part in (x1, x3, z2, x2) for h in (part, other(part))]
    first = project(near_four, [width] + [occ] * 6, collocation, 2, 0)
    lrp, stack, weight_rows = project(far_four, [occ] * 8, collocation, 2, 1, first)
    weights = jnp.concatenate([weight_rows[:4, 0], weight_rows[8:12, 0]])

    def rows_q(c):
        return dot(cols_q[c], stack, NT).astype(BF16)

    half_m, quarter, eighth = size_m // 2, size_m // 4, size_m // 8
    swap_y = [(i, i ^ 2) for i in range(npt)]

    def to_place(part):
        pieces = [lax.dynamic_slice_in_dim(part, (x ^ t) * eighth, eighth, 1) for t in (0, 1)]
        came = []
        for t in (0, 1):
            pairs = []
            for j in range(nw):
                for i in range(npt):
                    quarter_of = 2 * (i % 2) + i // 2
                    pairs.append((put(j, i), put(2 * quarter_of + (j % 2 ^ t), j // 2)))
            came.append(send(pieces[t], BOTH, pairs))
        return pieces, came

    def over_cores(grads):
        give, keep = split(dot(grads, stack), core, half_m)
        return split(keep + other(give).astype(F32), y, quarter)

    grads = pair_gradients(weights, kernel_t, lrp, rows_q(0), chunks[0][0])
    lrq = rows_q(1)
    give, keep = over_cores(grads)
    got = send(give, "pt", swap_y)
    early = pair_gradients(weights, kernel_t, lrp, lrq, chunks[1][0], (0, 2), (give[:16, :128],))
    pieces, came_0 = to_place((keep + got.astype(F32)).astype(BF16))
    late = pair_gradients(weights, kernel_t, lrp, lrq, chunks[1][0], (2, 4), (early, *pieces))
    give, keep = over_cores(jnp.concatenate([early, late], axis=1))
    _, came_1 = to_place((keep + send(give, "pt", swap_y).astype(F32)).astype(BF16))

    ordered = [jnp.where(x == side, came[0], came[1]) for side in (0, 1) for came in (came_0, came_1)]
    return jnp.concatenate(ordered, axis=0).astype(F32) / jnp.sum(weights)


def on_device_any(nw, own, collocation, kernel, walker_weight):
    size_b, size_a = kernel.shape
    size_m = collocation.shape[1]
    me_w, me_p = lax.axis_index("walk"), lax.axis_index("pt")
    weights = lax.all_gather(walker_weight, "walk", axis=0, tiled=True)
    orbitals = lax.all_gather(own, "walk", axis=0, tiled=True)
    all_rows = lax.all_gather(collocation, "pt", axis=0, tiled=True)
    col_q = lax.dynamic_slice_in_dim(all_rows, me_w * size_a, size_a, 0)
    lrp = dot(orbitals, collocation, NT).astype(BF16)
    lrq = dot(col_q, orbitals, NT).astype(BF16)
    grads = pair_gradients(weights / jnp.sum(weights), turned(kernel), lrp, lrq, 0)
    part = lax.psum(dot(grads, orbitals), "pt")
    part = jnp.where((me_w * size_a) // size_b == me_p, part, 0.0)
    wide = lax.dynamic_update_slice_in_dim(jnp.zeros((size_b, size_m), F32), part, (me_w * size_a) % size_b, 0)
    return lax.psum_scatter(wide, "walk", scatter_dimension=1, tiled=True)


def on_device(
    nw, npt, bra_orbitals, ket_orbitals, collocation, kernel, walker_weight, walker_group, group_occupied
):
    if (nw, npt, walker_weight.shape[0]) == (8, 4, 1) and kernel.shape[0] == 2 * kernel.shape[1]:
        bra, ket = bra_orbitals[0].T, ket_orbitals[0].T
        return on_device_8x4(bra, ket, collocation, kernel, walker_weight, walker_group, group_occupied)
    own = masked_orbitals(bra_orbitals, ket_orbitals, walker_group, group_occupied)
    return on_device_any(nw, own.reshape(-1, own.shape[2]), collocation, kernel, walker_weight)


def solution(mesh):
    in_specs = (
        P("walk", None, None),
        P("walk", None, None),
        P("pt", None),
        P("pt", "walk"),
        P("walk"),
        P("walk"),
        P(),
    )
    out_specs = P("pt", "walk")
    body = functools.partial(on_device, mesh.shape["walk"], mesh.shape["pt"])
    return jax.shard_map(body, mesh=mesh, in_specs=in_specs, out_specs=out_specs, check_vma=False)
```

```python
import functools

import jax
import jax.numpy as jnp
from jax import lax
from jax.experimental import pallas as pl
from jax.experimental.pallas import tpu as pltpu
from jax.sharding import PartitionSpec as P

F32 = jnp.float32
BF16 = jnp.bfloat16
BOTH = ("walk", "pt")
NT = (((1,), (1,)), ((), ()))
VMEM_LIMIT = 56 * 1024 * 1024


def tile_of(size, limit):
    return next(t for t in range(min(size, limit), 0, -128) if size % t == 0)


def dot(a, b, dims=(((1,), (0,)), ((), ()))):
    return lax.dot_general(a, b, dims, preferred_element_type=F32)


def cost(flops, nbytes):
    return pl.CostEstimate(flops=flops, bytes_accessed=nbytes, transcendentals=0)


def turn_kernel(in_ref, out_ref):
    out_ref[...] = in_ref[...].T


def turned(block):
    rows, cols = block.shape
    tr, tc = tile_of(rows, 512), tile_of(cols, 512)
    return pl.pallas_call(
        turn_kernel,
        out_shape=jax.ShapeDtypeStruct((cols, rows), block.dtype),
        grid=(cols // tc, rows // tr),
        in_specs=[pl.BlockSpec((tr, tc), lambda c, r: (r, c))],
        out_specs=pl.BlockSpec((tc, tr), lambda c, r: (c, r)),
        compiler_params=pltpu.CompilerParams(vmem_limit_bytes=VMEM_LIMIT),
        cost_estimate=cost(0, 10 * rows * cols),
    )(block)


def pack_kernel(group_ref, occupied_ref, side_ref, weight_ref, bra_ref, ket_ref, own_ref, half_ref):
    occ = bra_ref.shape[0]
    used = occupied_ref[group_ref[0]]
    kept = lax.broadcasted_iota(jnp.int32, bra_ref.shape, 0) < used
    bra_t = jnp.where(kept, bra_ref[...].astype(F32), 0.0).astype(BF16)
    ket_t = jnp.where(kept, ket_ref[...].astype(F32), 0.0).astype(BF16)
    own_ref[:occ, :] = bra_t
    own_ref[occ : 2 * occ, :] = ket_t

    @pl.when(side_ref[0] == 0)
    def _():
        half_ref[:occ, :] = bra_t

    @pl.when(side_ref[0] != 0)
    def _():
        half_ref[:occ, :] = ket_t

    shape = (half_ref.shape[0] - occ, half_ref.shape[1])
    row = lax.broadcasted_iota(jnp.int32, shape, 0)
    rest, rows = jnp.full(shape, weight_ref[0], F32), jnp.zeros(shape, F32)
    for part in range(3):
        near = rest.astype(BF16).astype(F32)
        rows = jnp.where(row == part, near, rows)
        rest = rest - near
    half_ref[occ:, :] = rows.astype(BF16)
    own_ref[2 * occ :, :] = rows.astype(BF16)


def packed(bra, ket, group, occupied, side, weight):
    occ, size_m = bra.shape
    smem = pl.BlockSpec(memory_space=pltpu.SMEM)
    return pl.pallas_call(
        pack_kernel,
        out_shape=[
            jax.ShapeDtypeStruct((2 * occ + 16, size_m), BF16),
            jax.ShapeDtypeStruct((occ + 16, size_m), BF16),
        ],
        in_specs=[smem] * 4 + [pl.BlockSpec(memory_space=pltpu.VMEM)] * 2,
        compiler_params=pltpu.CompilerParams(vmem_limit_bytes=VMEM_LIMIT),
        cost_estimate=cost(0, 12 * size_m * occ),
    )(group, occupied, side, weight, bra, ket)


def project_kernel(rows_each, waits, *refs):
    count = len(rows_each)
    items, col_ref = refs[:count], refs[count]
    out_ref, stack_out, weight_out, stack = refs[count + 1 + waits :]
    occ = min(rows_each)

    @pl.when(pl.program_id(0) == 0)
    def _():
        at = 0
        weight_out[...] = jnp.zeros_like(weight_out)
        for ref, rows in zip(items, rows_each):
            stack[at : at + rows, :] = ref[:rows, :]
            if at % (2 * occ) == 0:
                s = at // (2 * occ)
                weight_out[s : s + 1, :] = jnp.sum(ref[rows : rows + 16, :128].astype(F32), axis=0, keepdims=True)
            at += rows
        stack_out[...] = stack[...]

    out_ref[...] = dot(stack[...], col_ref[...], NT).astype(BF16)


def project(items, rows_each, col, groups, index, before=()):
    size_m, size, total = col.shape[1], col.shape[0], sum(rows_each)
    tile = tile_of(size, 512)
    return pl.pallas_call(
        functools.partial(project_kernel, tuple(rows_each), len(before)),
        out_shape=[
            jax.ShapeDtypeStruct((groups * total, size), BF16),
            jax.ShapeDtypeStruct((groups * total, size_m), BF16),
            jax.ShapeDtypeStruct((groups * 8, 128), F32),
        ],
        grid=(size // tile,),
        in_specs=[pl.BlockSpec(x.shape, lambda b: (0, 0), pipeline_mode=pl.Buffered(1)) for x in items]
        + [pl.BlockSpec((tile, size_m), lambda b: (b, 0))]
        + [pl.BlockSpec(memory_space=pl.ANY)] * len(before),
        out_specs=[
            pl.BlockSpec((total, tile), lambda b: (index, b)),
            pl.BlockSpec((total, size_m), lambda b: (index, 0), pipeline_mode=pl.Buffered(1)),
            pl.BlockSpec((8, 128), lambda b: (index, 0)),
        ],
        scratch_shapes=[pltpu.VMEM((total, size_m), BF16)],
        input_output_aliases={len(items) + 1 + n: n for n in range(len(before))},
        compiler_params=pltpu.CompilerParams(vmem_limit_bytes=VMEM_LIMIT),
        cost_estimate=cost(2 * (total + 640) * size_m * size, 2 * size_m * size),
    )(*items, col, *before)


def pair_kernel(sub, first, weight_ref, kt_ref, lrp_ref, lrq_ref, out_ref, sides):
    item, occ = first + pl.program_id(0), sides.shape[2]
    size_b = kt_ref.shape[1]

    for odd in (0, 1):

        @pl.when(item % 2 == odd)
        def _():
            for side in (0, 1):
                at = (2 * odd + side) * occ
                sides[side] = lrq_ref[:, at : at + occ]

    total_l = jnp.zeros(sides.shape[1:], F32)
    total_r = jnp.zeros(sides.shape[1:], F32)
    for at in range(0, size_b, sub):
        left_t = lrp_ref[:occ, at : at + sub]
        right_t = lrp_ref[occ:, at : at + sub]
        kern = kt_ref[:, at : at + sub]
        had_t = kern * dot(sides[1], left_t).astype(BF16)
        had = kern * dot(sides[0], right_t).astype(BF16)
        total_l += dot(had_t, right_t, NT)
        total_r += dot(had, left_t, NT)
    scale = 2.0 * weight_ref[item]
    sides[0] = (total_l * scale).astype(BF16)
    sides[1] = (total_r * scale).astype(BF16)

    for odd in (0, 1):

        @pl.when(item % 2 == odd)
        def _():
            for side in (0, 1):
                at = (2 * odd + side) * occ
                out_ref[:, at : at + occ] = sides[side]


def pair_gradients(weights, kernel_t, lrp, lrq, row_at, items=None):
    size_b, rows, count = kernel_t.shape[1], lrq.shape[0], weights.shape[0]
    first, last = items or (0, count)
    width = lrp.shape[0] // count
    at, sub = row_at // rows, tile_of(size_b, 512)
    return pl.pallas_call(
        functools.partial(pair_kernel, sub, first),
        out_shape=jax.ShapeDtypeStruct((rows, (last - first) * width), BF16),
        grid_spec=pltpu.PrefetchScalarGridSpec(
            num_scalar_prefetch=1,
            grid=(last - first,),
            in_specs=[
                pl.BlockSpec((rows, size_b), lambda w, s: (at, 0), pipeline_mode=pl.Buffered(1)),
                pl.BlockSpec((width, size_b), lambda w, s: (first + w, 0)),
                pl.BlockSpec((rows, 2 * width), lambda w, s: (0, (first + w) // 2)),
            ],
            out_specs=pl.BlockSpec((rows, 2 * width), lambda w, s: (0, w // 2)),
            scratch_shapes=[pltpu.VMEM((2, rows, width // 2), BF16)],
        ),
        compiler_params=pltpu.CompilerParams(vmem_limit_bytes=VMEM_LIMIT),
        cost_estimate=cost(
            2 * 4 * (last - first) * 256 * rows * size_b, 2 * (last - first) * (rows + width) * size_b
        ),
    )(weights, kernel_t, lrp, lrq)


def send(x, axes, pairs):
    return lax.ppermute(x, axes, pairs)


def masked_orbitals(bra_orbitals, ket_orbitals, walker_group, group_occupied):
    group_count, occ = group_occupied.shape[0], bra_orbitals.shape[2]
    matches = walker_group[:, None] == jnp.arange(group_count, dtype=jnp.int32)[None, :]
    occupied = jnp.sum(jnp.where(matches, group_occupied[None, :], 0), axis=1)
    masks = (jnp.arange(occ, dtype=jnp.int32)[None, :] < occupied[:, None]).astype(BF16)
    bra_t = jnp.swapaxes(bra_orbitals * masks[:, None, :], 1, 2)
    ket_t = jnp.swapaxes(ket_orbitals * masks[:, None, :], 1, 2)
    return jnp.concatenate([bra_t, ket_t], axis=1)


def on_device_8x4(bra, ket, collocation, kernel, walker_weight, walker_group, group_occupied):
    nw, npt = 8, 4
    size_b, size_a = kernel.shape
    occ, size_m = bra.shape
    width = 2 * occ
    me_w, me_p = lax.axis_index("walk"), lax.axis_index("pt")
    z, x, y, core = me_w // 2, me_w % 2, me_p // 2, me_p % 2

    def put(j, i):
        return j * npt + i

    def across(part):
        return send(part, "walk", [(j, j ^ 1) for j in range(nw)])

    def along(part, r):
        return send(part, "walk", [(j, (j - 2 * r) % nw) for j in range(nw)])

    def other(part):
        return send(part, "pt", [(i, i ^ 1) for i in range(npt)])

    def columns_q(begin, chunk):
        rows = lax.dynamic_slice_in_dim(collocation, x * size_a + begin, chunk, 0)
        far = send(rows, BOTH, [(put(j, j // 2), put(j, j // 2 ^ 2)) for j in range(nw)])
        near = jnp.where(me_p == z, rows, far)
        pairs = [(put(j, j // 2 ^ s), put(j, j // 2 ^ s ^ 1)) for j in range(nw) for s in (0, 2)]
        return jnp.where(core == z % 2, near, send(near, BOTH, pairs))

    def split(part, at, size, axis=1):
        give = lax.dynamic_slice_in_dim(part, (1 - at) * size, size, axis).astype(BF16)
        return give, lax.dynamic_slice_in_dim(part, at * size, size, axis)

    tie = lax.optimization_barrier
    chunks = [(0, 2 * size_a // 3), (2 * size_a // 3, size_a // 3)]
    own, half = packed(bra, ket, walker_group, group_occupied, core.reshape(1), walker_weight)
    cols_q = [columns_q(*chunk) for chunk in chunks]
    z1, z3, x0 = along(half, 1), along(half, 3), across(half)
    z2 = along(half, 2)
    kernel_t = turned(kernel)
    x0, z1, z3, kernel_t = tie((x0, z1, z3, kernel_t))
    x1, x3 = across(z1), across(z3)
    near_four = [own] + [h for part in (x0, z1, z3) for h in (part, other(part))]
    lrp, stack, weight_rows = project(near_four, [width] + [occ] * 6, collocation, 2, 0)
    z2, weight_rows = tie((z2, weight_rows))
    far_four = [h for part in (x1, x3, z2, across(z2)) for h in (part, other(part))]
    first = (lrp, stack, weight_rows)
    lrp, stack, weight_rows = project(far_four, [occ] * 8, collocation, 2, 1, first)
    weights = jnp.concatenate([weight_rows[:4, 0], weight_rows[8:12, 0]])

    def rows_q(c):
        return dot(cols_q[c], stack, NT).astype(BF16)

    half_m, quarter, eighth = size_m // 2, size_m // 4, size_m // 8
    swap_y = [(i, i ^ 2) for i in range(npt)]

    def to_place(part, *later):
        pieces = [lax.dynamic_slice_in_dim(part, (x ^ t) * eighth, eighth, 1) for t in (0, 1)]
        pieces = tie((*pieces, *later))
        came = []
        for t in (0, 1):
            pairs = []
            for j in range(nw):
                for i in range(npt):
                    quarter_of = 2 * (i % 2) + i // 2
                    pairs.append((put(j, i), put(2 * quarter_of + (j % 2 ^ t), j // 2)))
            came.append(send(pieces[t], BOTH, pairs))
        return pieces, came

    def over_cores(grads):
        give, keep = split(dot(grads, stack), core, half_m)
        return split(keep + other(give).astype(F32), y, quarter)

    grads = pair_gradients(weights, kernel_t, lrp, rows_q(0), chunks[0][0])
    lrq = rows_q(1)
    give, keep = over_cores(grads)
    give, lrq = tie((give, lrq))
    got = send(give, "pt", swap_y)
    early = pair_gradients(weights, kernel_t, lrp, lrq, chunks[1][0], (0, 4))
    early, got = tie((early, got))
    pieces, came_0 = to_place((keep + got.astype(F32)).astype(BF16), lrq)
    late = pair_gradients(weights, kernel_t, lrp, pieces[2], chunks[1][0], (4, 8))
    late, *came_0 = tie((late, *came_0))
    give, keep = over_cores(jnp.concatenate([early, late], axis=1))
    _, came_1 = to_place((keep + send(give, "pt", swap_y).astype(F32)).astype(BF16))

    ordered = [jnp.where(x == side, came[0], came[1]) for side in (0, 1) for came in (came_0, came_1)]
    return jnp.concatenate(ordered, axis=0).astype(F32) / jnp.sum(weights)


def on_device_any(nw, own, collocation, kernel, walker_weight):
    size_b, size_a = kernel.shape
    size_m = collocation.shape[1]
    me_w, me_p = lax.axis_index("walk"), lax.axis_index("pt")
    weights = lax.all_gather(walker_weight, "walk", axis=0, tiled=True)
    orbitals = lax.all_gather(own, "walk", axis=0, tiled=True)
    all_rows = lax.all_gather(collocation, "pt", axis=0, tiled=True)
    col_q = lax.dynamic_slice_in_dim(all_rows, me_w * size_a, size_a, 0)
    lrp = dot(orbitals, collocation, NT).astype(BF16)
    lrq = dot(col_q, orbitals, NT).astype(BF16)
    grads = pair_gradients(weights / jnp.sum(weights), turned(kernel), lrp, lrq, 0)
    part = lax.psum(dot(grads, orbitals), "pt")
    part = jnp.where((me_w * size_a) // size_b == me_p, part, 0.0)
    wide = lax.dynamic_update_slice_in_dim(jnp.zeros((size_b, size_m), F32), part, (me_w * size_a) % size_b, 0)
    return lax.psum_scatter(wide, "walk", scatter_dimension=1, tiled=True)


def on_device(
    nw, npt, bra_orbitals, ket_orbitals, collocation, kernel, walker_weight, walker_group, group_occupied
):
    if (nw, npt, walker_weight.shape[0]) == (8, 4, 1) and kernel.shape[0] == 2 * kernel.shape[1]:
        bra, ket = bra_orbitals[0].T, ket_orbitals[0].T
        return on_device_8x4(bra, ket, collocation, kernel, walker_weight, walker_group, group_occupied)
    own = masked_orbitals(bra_orbitals, ket_orbitals, walker_group, group_occupied)
    return on_device_any(nw, own.reshape(-1, own.shape[2]), collocation, kernel, walker_weight)


def solution(mesh):
    in_specs = (
        P("walk", None, None),
        P("walk", None, None),
        P("pt", None),
        P("pt", "walk"),
        P("walk"),
        P("walk"),
        P(),
    )
    out_specs = P("pt", "walk")
    body = functools.partial(on_device, mesh.shape["walk"], mesh.shape["pt"])
    return jax.shard_map(body, mesh=mesh, in_specs=in_specs, out_specs=out_specs, check_vma=False)
```

```python
import functools

import jax
import jax.numpy as jnp
from jax import lax
from jax.experimental import pallas as pl
from jax.experimental.pallas import tpu as pltpu
from jax.sharding import PartitionSpec as P

F32 = jnp.float32
BF16 = jnp.bfloat16
BOTH = ("walk", "pt")
NT = (((1,), (1,)), ((), ()))
VMEM_LIMIT = 56 * 1024 * 1024


def tile_of(size, limit):
    return next(t for t in range(min(size, limit), 0, -128) if size % t == 0)


def dot(a, b, dims=(((1,), (0,)), ((), ()))):
    return lax.dot_general(a, b, dims, preferred_element_type=F32)


def cost(flops, nbytes):
    return pl.CostEstimate(flops=flops, bytes_accessed=nbytes, transcendentals=0)


def turn_kernel(in_ref, out_ref):
    out_ref[...] = in_ref[...].T


def turned(block):
    rows, cols = block.shape
    tr, tc = tile_of(rows, 512), tile_of(cols, 512)
    return pl.pallas_call(
        turn_kernel,
        out_shape=jax.ShapeDtypeStruct((cols, rows), block.dtype),
        grid=(cols // tc, rows // tr),
        in_specs=[pl.BlockSpec((tr, tc), lambda c, r: (r, c))],
        out_specs=pl.BlockSpec((tc, tr), lambda c, r: (c, r)),
        compiler_params=pltpu.CompilerParams(vmem_limit_bytes=VMEM_LIMIT),
        cost_estimate=cost(0, 10 * rows * cols),
    )(block)


def pack_kernel(group_ref, occupied_ref, side_ref, weight_ref, bra_ref, ket_ref, own_ref, half_ref):
    occ = bra_ref.shape[0]
    used = occupied_ref[group_ref[0]]
    kept = lax.broadcasted_iota(jnp.int32, bra_ref.shape, 0) < used
    bra_t = jnp.where(kept, bra_ref[...].astype(F32), 0.0).astype(BF16)
    ket_t = jnp.where(kept, ket_ref[...].astype(F32), 0.0).astype(BF16)
    own_ref[:occ, :] = bra_t
    own_ref[occ : 2 * occ, :] = ket_t

    @pl.when(side_ref[0] == 0)
    def _():
        half_ref[:occ, :] = bra_t

    @pl.when(side_ref[0] != 0)
    def _():
        half_ref[:occ, :] = ket_t

    shape = (half_ref.shape[0] - occ, half_ref.shape[1])
    row = lax.broadcasted_iota(jnp.int32, shape, 0)
    rest, rows = jnp.full(shape, weight_ref[0], F32), jnp.zeros(shape, F32)
    for part in range(3):
        near = rest.astype(BF16).astype(F32)
        rows = jnp.where(row == part, near, rows)
        rest = rest - near
    half_ref[occ:, :] = rows.astype(BF16)
    own_ref[2 * occ :, :] = rows.astype(BF16)


def packed(bra, ket, group, occupied, side, weight):
    occ, size_m = bra.shape
    smem = pl.BlockSpec(memory_space=pltpu.SMEM)
    return pl.pallas_call(
        pack_kernel,
        out_shape=[
            jax.ShapeDtypeStruct((2 * occ + 16, size_m), BF16),
            jax.ShapeDtypeStruct((occ + 16, size_m), BF16),
        ],
        in_specs=[smem] * 4 + [pl.BlockSpec(memory_space=pltpu.VMEM)] * 2,
        compiler_params=pltpu.CompilerParams(vmem_limit_bytes=VMEM_LIMIT),
        cost_estimate=cost(0, 12 * size_m * occ),
    )(group, occupied, side, weight, bra, ket)


def project_kernel(rows_each, waits, *refs):
    count = len(rows_each)
    items, col_ref = refs[:count], refs[count]
    out_ref, stack_out, weight_out, stack = refs[count + 1 + waits :]
    occ = min(rows_each)

    @pl.when(pl.program_id(0) == 0)
    def _():
        at = 0
        weight_out[...] = jnp.zeros_like(weight_out)
        for ref, rows in zip(items, rows_each):
            stack[at : at + rows, :] = ref[:rows, :]
            if at % (2 * occ) == 0:
                s = at // (2 * occ)
                weight_out[s : s + 1, :] = jnp.sum(ref[rows : rows + 16, :128].astype(F32), axis=0, keepdims=True)
            at += rows
        stack_out[...] = stack[...]

    out_ref[...] = dot(stack[...], col_ref[...], NT).astype(BF16)


def project(items, rows_each, col, groups, index, before=()):
    size_m, size, total = col.shape[1], col.shape[0], sum(rows_each)
    tile = tile_of(size, 512)
    return pl.pallas_call(
        functools.partial(project_kernel, tuple(rows_each), len(before)),
        out_shape=[
            jax.ShapeDtypeStruct((groups * total, size), BF16),
            jax.ShapeDtypeStruct((groups * total, size_m), BF16),
            jax.ShapeDtypeStruct((groups * 8, 128), F32),
        ],
        grid=(size // tile,),
        in_specs=[pl.BlockSpec(x.shape, lambda b: (0, 0), pipeline_mode=pl.Buffered(1)) for x in items]
        + [pl.BlockSpec((tile, size_m), lambda b: (b, 0))]
        + [pl.BlockSpec(memory_space=pl.ANY)] * len(before),
        out_specs=[
            pl.BlockSpec((total, tile), lambda b: (index, b)),
            pl.BlockSpec((total, size_m), lambda b: (index, 0), pipeline_mode=pl.Buffered(1)),
            pl.BlockSpec((8, 128), lambda b: (index, 0)),
        ],
        scratch_shapes=[pltpu.VMEM((total, size_m), BF16)],
        input_output_aliases={len(items) + 1 + n: n for n in range(len(before))},
        compiler_params=pltpu.CompilerParams(vmem_limit_bytes=VMEM_LIMIT),
        cost_estimate=cost(2 * (total + 640) * size_m * size, 2 * size_m * size),
    )(*items, col, *before)


def pair_kernel(sub, first, weight_ref, kt_ref, lrp_ref, lrq_ref, out_ref):
    rows, size_b = kt_ref.shape
    occ = lrp_ref.shape[0] // 4
    sides = [lrq_ref[:, n * occ : (n + 1) * occ] for n in range(4)]
    totals = [jnp.zeros((rows, occ), F32) for _ in range(4)]
    for at in range(0, size_b, sub):
        kern = kt_ref[:, at : at + sub].astype(F32)
        for n in (0, 2):
            left_t = lrp_ref[n * occ : (n + 1) * occ, at : at + sub]
            right_t = lrp_ref[(n + 1) * occ : (n + 2) * occ, at : at + sub]
            had_t = (kern * dot(sides[n + 1], left_t)).astype(BF16)
            had = (kern * dot(sides[n], right_t)).astype(BF16)
            totals[n] += dot(had_t, right_t, NT)
            totals[n + 1] += dot(had, left_t, NT)
    for n in range(4):
        scale = 2.0 * weight_ref[2 * (first + pl.program_id(0)) + n // 2]
        out_ref[:, n * occ : (n + 1) * occ] = (totals[n] * scale).astype(BF16)


def pair_gradients(weights, kernel_t, lrp, lrq, row_at, rows, items=None):
    size_b, count = kernel_t.shape[1], weights.shape[0]
    first, last = [n // 2 for n in items or (0, count)]
    width = 2 * lrp.shape[0] // count
    at, sub = row_at // rows, tile_of(size_b, 512)
    return pl.pallas_call(
        functools.partial(pair_kernel, sub, first),
        out_shape=jax.ShapeDtypeStruct((rows, (last - first) * width), BF16),
        grid_spec=pltpu.PrefetchScalarGridSpec(
            num_scalar_prefetch=1,
            grid=(last - first,),
            in_specs=[
                pl.BlockSpec((rows, size_b), lambda p, s: (at, 0), pipeline_mode=pl.Buffered(1)),
                pl.BlockSpec((width, size_b), lambda p, s: (first + p, 0)),
                pl.BlockSpec((rows, width), lambda p, s: (at, first + p)),
            ],
            out_specs=pl.BlockSpec((rows, width), lambda p, s: (0, p)),
        ),
        compiler_params=pltpu.CompilerParams(vmem_limit_bytes=VMEM_LIMIT),
        cost_estimate=cost(
            2 * 8 * (last - first) * 256 * rows * size_b, 2 * (last - first) * (rows + width) * size_b
        ),
    )(weights, kernel_t, lrp, lrq)


def send(x, axes, pairs):
    return lax.ppermute(x, axes, pairs)


def masked_orbitals(bra_orbitals, ket_orbitals, walker_group, group_occupied):
    group_count, occ = group_occupied.shape[0], bra_orbitals.shape[2]
    matches = walker_group[:, None] == jnp.arange(group_count, dtype=jnp.int32)[None, :]
    occupied = jnp.sum(jnp.where(matches, group_occupied[None, :], 0), axis=1)
    masks = (jnp.arange(occ, dtype=jnp.int32)[None, :] < occupied[:, None]).astype(BF16)
    bra_t = jnp.swapaxes(bra_orbitals * masks[:, None, :], 1, 2)
    ket_t = jnp.swapaxes(ket_orbitals * masks[:, None, :], 1, 2)
    return jnp.concatenate([bra_t, ket_t], axis=1)


def on_device_8x4(bra, ket, collocation, kernel, walker_weight, walker_group, group_occupied):
    nw, npt = 8, 4
    size_b, size_a = kernel.shape
    occ, size_m = bra.shape
    width = 2 * occ
    me_w, me_p = lax.axis_index("walk"), lax.axis_index("pt")
    z, x, y, core = me_w // 2, me_w % 2, me_p // 2, me_p % 2

    def put(j, i):
        return j * npt + i

    def across(part):
        return send(part, "walk", [(j, j ^ 1) for j in range(nw)])

    def along(part, r):
        return send(part, "walk", [(j, (j - 2 * r) % nw) for j in range(nw)])

    def other(part):
        return send(part, "pt", [(i, i ^ 1) for i in range(npt)])

    def columns_q(begin, chunk):
        rows = lax.dynamic_slice_in_dim(collocation, x * size_a + begin, chunk, 0)
        far = send(rows, BOTH, [(put(j, j // 2), put(j, j // 2 ^ 2)) for j in range(nw)])
        near = jnp.where(me_p == z, rows, far)
        pairs = [(put(j, j // 2 ^ s), put(j, j // 2 ^ s ^ 1)) for j in range(nw) for s in (0, 2)]
        return jnp.where(core == z % 2, near, send(near, BOTH, pairs))

    def split(part, at, size, axis=1):
        give = lax.dynamic_slice_in_dim(part, (1 - at) * size, size, axis).astype(BF16)
        return give, lax.dynamic_slice_in_dim(part, at * size, size, axis)

    tie = lax.optimization_barrier
    chunks = [(0, 2 * size_a // 3), (2 * size_a // 3, size_a // 3)]
    own, half = packed(bra, ket, walker_group, group_occupied, core.reshape(1), walker_weight)
    cols_q = [columns_q(*chunk) for chunk in chunks]
    z1, z3, x0 = along(half, 1), along(half, 3), across(half)
    kernel_t = turned(kernel)
    x0, z1, z3, kernel_t = tie((x0, z1, z3, kernel_t))
    z2, x1, x3 = along(z1, 1), across(z1), across(z3)
    z2, z1, z3 = tie((z2, z1, z3))
    x2 = across(z2)
    near_four = [own] + [h for part in (x0, z1, z3) for h in (part, other(part))]
    lrp, stack, weight_rows = project(near_four, [width] + [occ] * 6, collocation, 2, 0)
    first = (lrp, stack, weight_rows)
    x2, *first = tie((x2, *first))
    far_four = [h for part in (x1, x3, z2, x2) for h in (part, other(part))]
    lrp, stack, weight_rows = project(far_four, [occ] * 8, collocation, 2, 1, first)
    weights = jnp.concatenate([weight_rows[:4, 0], weight_rows[8:12, 0]])

    lrq = dot(jnp.concatenate(cols_q, axis=0), stack, NT).astype(BF16)

    half_m, quarter, eighth = size_m // 2, size_m // 4, size_m // 8
    swap_y = [(i, i ^ 2) for i in range(npt)]

    def to_place(part, *later):
        pieces = [lax.dynamic_slice_in_dim(part, (x ^ t) * eighth, eighth, 1) for t in (0, 1)]
        pieces = tie((*pieces, *later))
        came = []
        for t in (0, 1):
            pairs = []
            for j in range(nw):
                for i in range(npt):
                    quarter_of = 2 * (i % 2) + i // 2
                    pairs.append((put(j, i), put(2 * quarter_of + (j % 2 ^ t), j // 2)))
            came.append(send(pieces[t], BOTH, pairs))
        return pieces, came

    def over_cores(grads):
        give, keep = split(grads, core, half_m)
        return split(keep + other(give).astype(F32), y, quarter)

    (at_0, rows_0), (at_1, rows_1) = chunks
    middle = stack.shape[0] // 2
    grads = pair_gradients(weights, kernel_t, lrp, lrq, at_0, rows_0)
    give, keep = over_cores(dot(grads, stack))
    give, lrq = tie((give, lrq))
    got = send(give, "pt", swap_y)
    early = pair_gradients(weights, kernel_t, lrp, lrq, at_1, rows_1, (0, 4))
    part = dot(early, stack[:middle])
    part, got = tie((part, got))
    pieces, came_0 = to_place((keep + got.astype(F32)).astype(BF16), lrq)
    late = pair_gradients(weights, kernel_t, lrp, pieces[2], at_1, rows_1, (4, 8))
    late, *came_0 = tie((late, *came_0))
    give, keep = over_cores(part + dot(late, stack[middle:]))
    _, came_1 = to_place((keep + send(give, "pt", swap_y).astype(F32)).astype(BF16))

    ordered = [jnp.where(x == side, came[0], came[1]) for side in (0, 1) for came in (came_0, came_1)]
    return jnp.concatenate(ordered, axis=0).astype(F32) / jnp.sum(weights)


def on_device_any(nw, own, collocation, kernel, walker_weight):
    size_b, size_a = kernel.shape
    size_m = collocation.shape[1]
    me_w, me_p = lax.axis_index("walk"), lax.axis_index("pt")
    weights = lax.all_gather(walker_weight, "walk", axis=0, tiled=True)
    orbitals = lax.all_gather(own, "walk", axis=0, tiled=True)
    all_rows = lax.all_gather(collocation, "pt", axis=0, tiled=True)
    col_q = lax.dynamic_slice_in_dim(all_rows, me_w * size_a, size_a, 0)
    lrp = dot(orbitals, collocation, NT).astype(BF16)
    lrq = dot(col_q, orbitals, NT).astype(BF16)
    grads = pair_gradients(weights / jnp.sum(weights), turned(kernel), lrp, lrq, 0, size_a)
    part = lax.psum(dot(grads, orbitals), "pt")
    part = jnp.where((me_w * size_a) // size_b == me_p, part, 0.0)
    wide = lax.dynamic_update_slice_in_dim(jnp.zeros((size_b, size_m), F32), part, (me_w * size_a) % size_b, 0)
    return lax.psum_scatter(wide, "walk", scatter_dimension=1, tiled=True)


def on_device(
    nw, npt, bra_orbitals, ket_orbitals, collocation, kernel, walker_weight, walker_group, group_occupied
):
    if (nw, npt, walker_weight.shape[0]) == (8, 4, 1) and kernel.shape[0] == 2 * kernel.shape[1]:
        bra, ket = bra_orbitals[0].T, ket_orbitals[0].T
        return on_device_8x4(bra, ket, collocation, kernel, walker_weight, walker_group, group_occupied)
    own = masked_orbitals(bra_orbitals, ket_orbitals, walker_group, group_occupied)
    return on_device_any(nw, own.reshape(-1, own.shape[2]), collocation, kernel, walker_weight)


def solution(mesh):
    in_specs = (
        P("walk", None, None),
        P("walk", None, None),
        P("pt", None),
        P("pt", "walk"),
        P("walk"),
        P("walk"),
        P(),
    )
    out_specs = P("pt", "walk")
    body = functools.partial(on_device, mesh.shape["walk"], mesh.shape["pt"])
    return jax.shard_map(body, mesh=mesh, in_specs=in_specs, out_specs=out_specs, check_vma=False)
```

```python
import functools

import jax
import jax.numpy as jnp
from jax import lax
from jax.experimental import pallas as pl
from jax.experimental.layout import Layout, with_layout_constraint
from jax.experimental.pallas import tpu as pltpu
from jax.sharding import PartitionSpec as P

F32 = jnp.float32
BF16 = jnp.bfloat16
BOTH = ("walk", "pt")
NT = (((1,), (1,)), ((), ()))
VMEM_LIMIT = 56 * 1024 * 1024


def tile_of(size, limit):
    return next(t for t in range(min(size, limit), 0, -128) if size % t == 0)


def dot(a, b, dims=(((1,), (0,)), ((), ()))):
    return lax.dot_general(a, b, dims, preferred_element_type=F32)


def cost(flops, nbytes):
    return pl.CostEstimate(flops=flops, bytes_accessed=nbytes, transcendentals=0)


def turn_kernel(in_ref, out_ref):
    out_ref[...] = in_ref[...].T


def turned(block):
    rows, cols = block.shape
    tr, tc = tile_of(rows, 512), tile_of(cols, 512)
    return pl.pallas_call(
        turn_kernel,
        out_shape=jax.ShapeDtypeStruct((cols, rows), block.dtype),
        grid=(cols // tc, rows // tr),
        in_specs=[pl.BlockSpec((tr, tc), lambda c, r: (r, c))],
        out_specs=pl.BlockSpec((tc, tr), lambda c, r: (c, r)),
        compiler_params=pltpu.CompilerParams(vmem_limit_bytes=VMEM_LIMIT),
        cost_estimate=cost(0, 10 * rows * cols),
    )(block)


def pack_kernel(group_ref, occupied_ref, side_ref, weight_ref, bra_ref, ket_ref, own_ref, half_ref):
    occ = bra_ref.shape[0]
    used = occupied_ref[group_ref[0]]
    kept = lax.broadcasted_iota(jnp.int32, bra_ref.shape, 0) < used
    bra_t = jnp.where(kept, bra_ref[...].astype(F32), 0.0).astype(BF16)
    ket_t = jnp.where(kept, ket_ref[...].astype(F32), 0.0).astype(BF16)
    own_ref[:occ, :] = bra_t
    own_ref[occ : 2 * occ, :] = ket_t

    @pl.when(side_ref[0] == 0)
    def _():
        half_ref[:occ, :] = bra_t

    @pl.when(side_ref[0] != 0)
    def _():
        half_ref[:occ, :] = ket_t

    shape = (half_ref.shape[0] - occ, half_ref.shape[1])
    row = lax.broadcasted_iota(jnp.int32, shape, 0)
    rest, rows = jnp.full(shape, weight_ref[0], F32), jnp.zeros(shape, F32)
    for part in range(3):
        near = rest.astype(BF16).astype(F32)
        rows = jnp.where(row == part, near, rows)
        rest = rest - near
    half_ref[occ:, :] = rows.astype(BF16)
    own_ref[2 * occ :, :] = rows.astype(BF16)


def packed(bra, ket, group, occupied, side, weight):
    occ, size_m = bra.shape
    smem = pl.BlockSpec(memory_space=pltpu.SMEM)
    return pl.pallas_call(
        pack_kernel,
        out_shape=[
            jax.ShapeDtypeStruct((2 * occ + 16, size_m), BF16),
            jax.ShapeDtypeStruct((occ + 16, size_m), BF16),
        ],
        in_specs=[smem] * 4 + [pl.BlockSpec(memory_space=pltpu.VMEM)] * 2,
        compiler_params=pltpu.CompilerParams(vmem_limit_bytes=VMEM_LIMIT),
        cost_estimate=cost(0, 12 * size_m * occ),
    )(group, occupied, side, weight, bra, ket)


def project_kernel(rows_each, waits, *refs):
    count = len(rows_each)
    items, col_ref = refs[:count], refs[count]
    out_ref, stack_out, weight_out, stack = refs[count + 1 + waits :]
    occ = min(rows_each)

    @pl.when(pl.program_id(0) == 0)
    def _():
        at = 0
        weight_out[...] = jnp.zeros_like(weight_out)
        for ref, rows in zip(items, rows_each):
            stack[at : at + rows, :] = ref[:rows, :]
            if at % (2 * occ) == 0:
                s = at // (2 * occ)
                weight_out[s : s + 1, :] = jnp.sum(ref[rows : rows + 16, :128].astype(F32), axis=0, keepdims=True)
            at += rows
        stack_out[...] = stack[...]

    out_ref[...] = dot(stack[...], col_ref[...], NT).astype(BF16)


def project(items, rows_each, col, groups, index, before=()):
    size_m, size, total = col.shape[1], col.shape[0], sum(rows_each)
    tile = tile_of(size, 512)
    return pl.pallas_call(
        functools.partial(project_kernel, tuple(rows_each), len(before)),
        out_shape=[
            jax.ShapeDtypeStruct((groups * total, size), BF16),
            jax.ShapeDtypeStruct((groups * total, size_m), BF16),
            jax.ShapeDtypeStruct((groups * 8, 128), F32),
        ],
        grid=(size // tile,),
        in_specs=[pl.BlockSpec(x.shape, lambda b: (0, 0), pipeline_mode=pl.Buffered(1)) for x in items]
        + [pl.BlockSpec((tile, size_m), lambda b: (b, 0))]
        + [pl.BlockSpec(memory_space=pl.ANY)] * len(before),
        out_specs=[
            pl.BlockSpec((total, tile), lambda b: (index, b)),
            pl.BlockSpec((total, size_m), lambda b: (index, 0), pipeline_mode=pl.Buffered(1)),
            pl.BlockSpec((8, 128), lambda b: (index, 0)),
        ],
        scratch_shapes=[pltpu.VMEM((total, size_m), BF16)],
        input_output_aliases={len(items) + 1 + n: n for n in range(len(before))},
        compiler_params=pltpu.CompilerParams(vmem_limit_bytes=VMEM_LIMIT),
        cost_estimate=cost(2 * (total + 640) * size_m * size, 2 * size_m * size),
    )(*items, col, *before)


def pair_kernel(sub, first, weight_ref, kt_ref, lrp_ref, lrq_ref, out_ref):
    rows, size_b = kt_ref.shape
    occ = lrp_ref.shape[0] // 4
    sides = [lrq_ref[:, n * occ : (n + 1) * occ] for n in range(4)]
    totals = [jnp.zeros((rows, occ), F32) for _ in range(4)]
    for at in range(0, size_b, sub):
        kern = kt_ref[:, at : at + sub].astype(F32)
        for n in (0, 2):
            left_t = lrp_ref[n * occ : (n + 1) * occ, at : at + sub]
            right_t = lrp_ref[(n + 1) * occ : (n + 2) * occ, at : at + sub]
            had_t = (kern * dot(sides[n + 1], left_t)).astype(BF16)
            had = (kern * dot(sides[n], right_t)).astype(BF16)
            totals[n] += dot(had_t, right_t, NT)
            totals[n + 1] += dot(had, left_t, NT)
    for n in range(4):
        scale = 2.0 * weight_ref[2 * (first + pl.program_id(0)) + n // 2]
        out_ref[:, n * occ : (n + 1) * occ] = (totals[n] * scale).astype(BF16)


def pair_gradients(weights, kernel_t, lrp, lrq, row_at, rows, items=None):
    size_b, count = kernel_t.shape[1], weights.shape[0]
    first, last = [n // 2 for n in items or (0, count)]
    width = 2 * lrp.shape[0] // count
    at, sub = row_at // rows, tile_of(size_b, 512)
    return pl.pallas_call(
        functools.partial(pair_kernel, sub, first),
        out_shape=jax.ShapeDtypeStruct((rows, (last - first) * width), BF16),
        grid_spec=pltpu.PrefetchScalarGridSpec(
            num_scalar_prefetch=1,
            grid=(last - first,),
            in_specs=[
                pl.BlockSpec((rows, size_b), lambda p, s: (at, 0), pipeline_mode=pl.Buffered(1)),
                pl.BlockSpec((width, size_b), lambda p, s: (first + p, 0)),
                pl.BlockSpec((rows, width), lambda p, s: (at, first + p)),
            ],
            out_specs=pl.BlockSpec((rows, width), lambda p, s: (0, p)),
        ),
        compiler_params=pltpu.CompilerParams(vmem_limit_bytes=VMEM_LIMIT),
        cost_estimate=cost(
            2 * 8 * (last - first) * 256 * rows * size_b, 2 * (last - first) * (rows + width) * size_b
        ),
    )(weights, kernel_t, lrp, lrq)


def product_kernel(side_ref, grads_ref, orbitals_ref, give_ref, keep_ref):
    part = dot(grads_ref[...], orbitals_ref[...])
    step, half = pl.program_id(0), pl.num_programs(0) // 2

    @pl.when(step < half)
    def _():
        give_ref[...] = part.astype(BF16)

    @pl.when(step >= half)
    def _():
        keep_ref[...] = part


def product_halves(grads, orbitals, side):
    (rows, depth), size_m = grads.shape, orbitals.shape[1]
    tile = tile_of(size_m // 2, 384)
    half = size_m // 2 // tile
    return pl.pallas_call(
        product_kernel,
        out_shape=[
            jax.ShapeDtypeStruct((rows, size_m // 2), BF16),
            jax.ShapeDtypeStruct((rows, size_m // 2), F32),
        ],
        grid_spec=pltpu.PrefetchScalarGridSpec(
            num_scalar_prefetch=1,
            grid=(2 * half,),
            in_specs=[
                pl.BlockSpec((rows, depth), lambda n, s: (0, 0), pipeline_mode=pl.Buffered(1)),
                pl.BlockSpec((depth, tile), lambda n, s: (0, (n + half * (1 - s[0])) % (2 * half))),
            ],
            out_specs=[
                pl.BlockSpec((rows, tile), lambda n, s: (0, jnp.minimum(n, half - 1))),
                pl.BlockSpec((rows, tile), lambda n, s: (0, jnp.maximum(n - half, 0))),
            ],
        ),
        compiler_params=pltpu.CompilerParams(vmem_limit_bytes=VMEM_LIMIT),
        cost_estimate=cost(2 * rows * depth * size_m, 2 * (rows + size_m) * depth),
    )(side, grads, orbitals)


def send(x, axes, pairs):
    return lax.ppermute(x, axes, pairs)


def masked_orbitals(bra_orbitals, ket_orbitals, walker_group, group_occupied):
    group_count, occ = group_occupied.shape[0], bra_orbitals.shape[2]
    matches = walker_group[:, None] == jnp.arange(group_count, dtype=jnp.int32)[None, :]
    occupied = jnp.sum(jnp.where(matches, group_occupied[None, :], 0), axis=1)
    masks = (jnp.arange(occ, dtype=jnp.int32)[None, :] < occupied[:, None]).astype(BF16)
    bra_t = jnp.swapaxes(bra_orbitals * masks[:, None, :], 1, 2)
    ket_t = jnp.swapaxes(ket_orbitals * masks[:, None, :], 1, 2)
    return jnp.concatenate([bra_t, ket_t], axis=1)


def on_device_8x4(bra, ket, collocation, kernel, walker_weight, walker_group, group_occupied):
    nw, npt = 8, 4
    size_b, size_a = kernel.shape
    occ, size_m = bra.shape
    width = 2 * occ
    me_w, me_p = lax.axis_index("walk"), lax.axis_index("pt")
    z, x, y, core = me_w // 2, me_w % 2, me_p // 2, me_p % 2

    def put(j, i):
        return j * npt + i

    def across(part):
        return send(part, "walk", [(j, j ^ 1) for j in range(nw)])

    def along(part, r):
        return send(part, "walk", [(j, (j - 2 * r) % nw) for j in range(nw)])

    def other(part):
        return send(part, "pt", [(i, i ^ 1) for i in range(npt)])

    def split(part, at, size, axis=1):
        give = lax.dynamic_slice_in_dim(part, (1 - at) * size, size, axis).astype(BF16)
        return give, lax.dynamic_slice_in_dim(part, at * size, size, axis)

    tie = lax.optimization_barrier
    sixth = size_a // 6
    chunks = [(0, 3 * sixth), (4 * sixth, 2 * sixth), (3 * sixth, sixth)]
    rows = lax.dynamic_slice_in_dim(collocation, x * size_a, size_a, 0)
    far = send(rows, BOTH, [(put(j, j // 2), put(j, j // 2 ^ 2)) for j in range(nw)])
    own, half = packed(bra, ket, walker_group, group_occupied, core.reshape(1), walker_weight)
    z1, z3, x0 = along(half, 1), along(half, 3), across(half)
    kernel_t = turned(kernel)
    x0, z1, z3, kernel_t = tie((x0, z1, z3, kernel_t))
    z2, x1, x3 = along(z1, 1), across(z1), across(z3)
    z2, z1, z3 = tie((z2, z1, z3))
    x2 = across(z2)
    near_four = [own] + [h for part in (x0, z1, z3) for h in (part, other(part))]
    lrp, stack, weight_rows = project(near_four, [width] + [occ] * 6, collocation, 2, 0)
    x1, x3, x2, weight_rows = tie((x1, x3, x2, weight_rows))
    far, weight_rows = tie((far, weight_rows))
    first = (lrp, stack, weight_rows)
    far_four = [h for part in (x1, x3, z2, x2) for h in (part, other(part))]
    lrp, stack, weight_rows = project(far_four, [occ] * 8, collocation, 2, 1, first)
    weights = jnp.concatenate([weight_rows[:4, 0], weight_rows[8:12, 0]])

    near = jnp.where(me_p == z, rows, far)
    pairs = [(put(j, j // 2 ^ s), put(j, j // 2 ^ s ^ 1)) for j in range(nw) for s in (0, 2)]
    col_q = jnp.where(core == z % 2, near, send(near, BOTH, pairs))
    lrq = dot(col_q, stack, NT).astype(BF16)

    half_m, quarter, eighth = size_m // 2, size_m // 4, size_m // 8
    swap_y = [(i, i ^ 2) for i in range(npt)]

    def to_place(part, *later):
        row_major = Layout(major_to_minor=(0, 1))
        part = with_layout_constraint(with_layout_constraint(part, row_major).T, row_major)
        pieces = [lax.dynamic_slice_in_dim(part, (x ^ t) * eighth, eighth, 0) for t in (0, 1)]
        pieces = tie((*pieces, *later))
        came = []
        for t in (0, 1):
            pairs = []
            for j in range(nw):
                for i in range(npt):
                    quarter_of = 2 * (i % 2) + i // 2
                    pairs.append((put(j, i), put(2 * quarter_of + (j % 2 ^ t), j // 2)))
            came.append(send(pieces[t], BOTH, pairs))
        return pieces, came

    side = core.reshape(1)

    def over_cores(give, keep):
        return split(keep + other(give).astype(F32), y, quarter)

    grads = pair_gradients(weights, kernel_t, lrp, lrq, *chunks[0])
    give_0, keep_0 = over_cores(*product_halves(grads, stack, side))
    give_0, scale = tie((give_0, weights))
    got_0 = send(give_0, "pt", swap_y)
    grads = pair_gradients(scale, kernel_t, lrp, lrq, *chunks[1])
    give, keep = product_halves(grads, stack, side)
    keep, got_0 = tie((keep, got_0))
    pieces, came_0 = to_place((keep_0 + got_0.astype(F32)).astype(BF16), weights)
    give_1, keep_1 = over_cores(give, keep)
    give_1, scale = tie((give_1, pieces[2]))
    got_1 = send(give_1, "pt", swap_y)
    grads = pair_gradients(scale, kernel_t, lrp, lrq, *chunks[2])
    _, got_1, *came_0 = tie((grads[:16, :128], got_1, *came_0))
    pieces, came_1 = to_place((keep_1 + got_1.astype(F32)).astype(BF16), side)
    give_2, keep_2 = over_cores(*product_halves(grads, stack, pieces[2]))
    _, came_2 = to_place((keep_2 + send(give_2, "pt", swap_y).astype(F32)).astype(BF16))

    ordered = [jnp.where(x == side, came[0], came[1]) for side in (0, 1) for came in (came_0, came_2, came_1)]
    return (jnp.concatenate(ordered, axis=1).astype(F32) / jnp.sum(weights)).T


def on_device_any(nw, own, collocation, kernel, walker_weight):
    size_b, size_a = kernel.shape
    size_m = collocation.shape[1]
    me_w, me_p = lax.axis_index("walk"), lax.axis_index("pt")
    weights = lax.all_gather(walker_weight, "walk", axis=0, tiled=True)
    orbitals = lax.all_gather(own, "walk", axis=0, tiled=True)
    all_rows = lax.all_gather(collocation, "pt", axis=0, tiled=True)
    col_q = lax.dynamic_slice_in_dim(all_rows, me_w * size_a, size_a, 0)
    lrp = dot(orbitals, collocation, NT).astype(BF16)
    lrq = dot(col_q, orbitals, NT).astype(BF16)
    grads = pair_gradients(weights / jnp.sum(weights), turned(kernel), lrp, lrq, 0, size_a)
    part = lax.psum(dot(grads, orbitals), "pt")
    part = jnp.where((me_w * size_a) // size_b == me_p, part, 0.0)
    wide = lax.dynamic_update_slice_in_dim(jnp.zeros((size_b, size_m), F32), part, (me_w * size_a) % size_b, 0)
    return lax.psum_scatter(wide, "walk", scatter_dimension=1, tiled=True)


def on_device(
    nw, npt, bra_orbitals, ket_orbitals, collocation, kernel, walker_weight, walker_group, group_occupied
):
    if (nw, npt, walker_weight.shape[0]) == (8, 4, 1) and kernel.shape[0] == 2 * kernel.shape[1]:
        bra, ket = bra_orbitals[0].T, ket_orbitals[0].T
        return on_device_8x4(bra, ket, collocation, kernel, walker_weight, walker_group, group_occupied)
    own = masked_orbitals(bra_orbitals, ket_orbitals, walker_group, group_occupied)
    return on_device_any(nw, own.reshape(-1, own.shape[2]), collocation, kernel, walker_weight)


def solution(mesh):
    in_specs = (
        P("walk", None, None),
        P("walk", None, None),
        P("pt", None),
        P("pt", "walk"),
        P("walk"),
        P("walk"),
        P(),
    )
    out_specs = P("pt", "walk")
    body = functools.partial(on_device, mesh.shape["walk"], mesh.shape["pt"])
    return jax.shard_map(body, mesh=mesh, in_specs=in_specs, out_specs=out_specs, check_vma=False)
```

```python
import functools

import jax
import jax.numpy as jnp
from jax import lax
from jax.experimental import pallas as pl
from jax.experimental.pallas import tpu as pltpu
from jax.sharding import PartitionSpec as P

F32 = jnp.float32
BF16 = jnp.bfloat16
BOTH = ("walk", "pt")
NT = (((1,), (1,)), ((), ()))
VMEM_LIMIT = 56 * 1024 * 1024


def tile_of(size, limit):
    return next(t for t in range(min(size, limit), 0, -128) if size % t == 0)


def dot(a, b, dims=(((1,), (0,)), ((), ()))):
    return lax.dot_general(a, b, dims, preferred_element_type=F32)


def cost(flops, nbytes):
    return pl.CostEstimate(flops=flops, bytes_accessed=nbytes, transcendentals=0)


def turn_kernel(in_ref, out_ref):
    out_ref[...] = in_ref[...].T


def turned(block):
    rows, cols = block.shape
    tr, tc = tile_of(rows, 512), tile_of(cols, 512)
    return pl.pallas_call(
        turn_kernel,
        out_shape=jax.ShapeDtypeStruct((cols, rows), block.dtype),
        grid=(cols // tc, rows // tr),
        in_specs=[pl.BlockSpec((tr, tc), lambda c, r: (r, c))],
        out_specs=pl.BlockSpec((tc, tr), lambda c, r: (c, r)),
        compiler_params=pltpu.CompilerParams(vmem_limit_bytes=VMEM_LIMIT),
        cost_estimate=cost(0, 10 * rows * cols),
    )(block)


def pack_kernel(group_ref, occupied_ref, side_ref, weight_ref, bra_ref, ket_ref, own_ref, half_ref):
    occ = bra_ref.shape[0]
    used = occupied_ref[group_ref[0]]
    kept = lax.broadcasted_iota(jnp.int32, bra_ref.shape, 0) < used
    bra_t = jnp.where(kept, bra_ref[...].astype(F32), 0.0).astype(BF16)
    ket_t = jnp.where(kept, ket_ref[...].astype(F32), 0.0).astype(BF16)
    own_ref[:occ, :] = bra_t
    own_ref[occ : 2 * occ, :] = ket_t

    @pl.when(side_ref[0] == 0)
    def _():
        half_ref[:occ, :] = bra_t

    @pl.when(side_ref[0] != 0)
    def _():
        half_ref[:occ, :] = ket_t

    shape = (half_ref.shape[0] - occ, half_ref.shape[1])
    row = lax.broadcasted_iota(jnp.int32, shape, 0)
    rest, rows = jnp.full(shape, weight_ref[0], F32), jnp.zeros(shape, F32)
    for part in range(3):
        near = rest.astype(BF16).astype(F32)
        rows = jnp.where(row == part, near, rows)
        rest = rest - near
    half_ref[occ:, :] = rows.astype(BF16)
    own_ref[2 * occ :, :] = rows.astype(BF16)


def packed(bra, ket, group, occupied, side, weight):
    occ, size_m = bra.shape
    smem = pl.BlockSpec(memory_space=pltpu.SMEM)
    return pl.pallas_call(
        pack_kernel,
        out_shape=[
            jax.ShapeDtypeStruct((2 * occ + 16, size_m), BF16),
            jax.ShapeDtypeStruct((occ + 16, size_m), BF16),
        ],
        in_specs=[smem] * 4 + [pl.BlockSpec(memory_space=pltpu.VMEM)] * 2,
        compiler_params=pltpu.CompilerParams(vmem_limit_bytes=VMEM_LIMIT),
        cost_estimate=cost(0, 12 * size_m * occ),
    )(group, occupied, side, weight, bra, ket)


def project_kernel(rows_each, waits, *refs):
    count = len(rows_each)
    items, col_ref = refs[:count], refs[count]
    out_ref, stack_out, weight_out, stack = refs[count + 1 + waits :]
    occ = min(rows_each)

    @pl.when(pl.program_id(0) == 0)
    def _():
        at = 0
        weight_out[...] = jnp.zeros_like(weight_out)
        for ref, rows in zip(items, rows_each):
            stack[at : at + rows, :] = ref[:rows, :]
            if at % (2 * occ) == 0:
                s = at // (2 * occ)
                weight_out[s : s + 1, :] = jnp.sum(ref[rows : rows + 16, :128].astype(F32), axis=0, keepdims=True)
            at += rows
        stack_out[...] = stack[...]

    out_ref[...] = dot(stack[...], col_ref[...], NT).astype(BF16)


def project(items, rows_each, col, groups, index, before=()):
    size_m, size, total = col.shape[1], col.shape[0], sum(rows_each)
    tile = tile_of(size, 512)
    return pl.pallas_call(
        functools.partial(project_kernel, tuple(rows_each), len(before)),
        out_shape=[
            jax.ShapeDtypeStruct((groups * total, size), BF16),
            jax.ShapeDtypeStruct((groups * total, size_m), BF16),
            jax.ShapeDtypeStruct((groups * 8, 128), F32),
        ],
        grid=(size // tile,),
        in_specs=[pl.BlockSpec(x.shape, lambda b: (0, 0), pipeline_mode=pl.Buffered(1)) for x in items]
        + [pl.BlockSpec((tile, size_m), lambda b: (b, 0))]
        + [pl.BlockSpec(memory_space=pl.ANY)] * len(before),
        out_specs=[
            pl.BlockSpec((total, tile), lambda b: (index, b)),
            pl.BlockSpec((total, size_m), lambda b: (index, 0), pipeline_mode=pl.Buffered(1)),
            pl.BlockSpec((8, 128), lambda b: (index, 0)),
        ],
        scratch_shapes=[pltpu.VMEM((total, size_m), BF16)],
        input_output_aliases={len(items) + 1 + n: n for n in range(len(before))},
        compiler_params=pltpu.CompilerParams(vmem_limit_bytes=VMEM_LIMIT),
        cost_estimate=cost(2 * (total + 640) * size_m * size, 2 * size_m * size),
    )(*items, col, *before)


def pair_kernel(sub, first, weight_ref, kt_ref, lrp_ref, lrq_ref, out_ref):
    rows, size_b = kt_ref.shape
    occ = lrp_ref.shape[0] // 4
    sides = [lrq_ref[:, n * occ : (n + 1) * occ] for n in range(4)]
    totals = [jnp.zeros((rows, occ), F32) for _ in range(4)]
    for at in range(0, size_b, sub):
        kern = kt_ref[:, at : at + sub].astype(F32)
        for n in (0, 2):
            left_t = lrp_ref[n * occ : (n + 1) * occ, at : at + sub]
            right_t = lrp_ref[(n + 1) * occ : (n + 2) * occ, at : at + sub]
            had_t = (kern * dot(sides[n + 1], left_t)).astype(BF16)
            had = (kern * dot(sides[n], right_t)).astype(BF16)
            totals[n] += dot(had_t, right_t, NT)
            totals[n + 1] += dot(had, left_t, NT)
    for n in range(4):
        scale = 2.0 * weight_ref[2 * (first + pl.program_id(0)) + n // 2]
        out_ref[:, n * occ : (n + 1) * occ] = (totals[n] * scale).astype(BF16)


def pair_gradients(weights, kernel_t, lrp, lrq, row_at, rows, items=None):
    size_b, count = kernel_t.shape[1], weights.shape[0]
    first, last = [n // 2 for n in items or (0, count)]
    width = 2 * lrp.shape[0] // count
    at, sub = row_at // rows, tile_of(size_b, 512)
    return pl.pallas_call(
        functools.partial(pair_kernel, sub, first),
        out_shape=jax.ShapeDtypeStruct((rows, (last - first) * width), BF16),
        grid_spec=pltpu.PrefetchScalarGridSpec(
            num_scalar_prefetch=1,
            grid=(last - first,),
            in_specs=[
                pl.BlockSpec((rows, size_b), lambda p, s: (at, 0), pipeline_mode=pl.Buffered(1)),
                pl.BlockSpec((width, size_b), lambda p, s: (first + p, 0)),
                pl.BlockSpec((rows, width), lambda p, s: (at, first + p)),
            ],
            out_specs=pl.BlockSpec((rows, width), lambda p, s: (0, p)),
        ),
        compiler_params=pltpu.CompilerParams(vmem_limit_bytes=VMEM_LIMIT),
        cost_estimate=cost(
            2 * 8 * (last - first) * 256 * rows * size_b, 2 * (last - first) * (rows + width) * size_b
        ),
    )(weights, kernel_t, lrp, lrq)


def send(x, axes, pairs):
    return lax.ppermute(x, axes, pairs)


def masked_orbitals(bra_orbitals, ket_orbitals, walker_group, group_occupied):
    group_count, occ = group_occupied.shape[0], bra_orbitals.shape[2]
    matches = walker_group[:, None] == jnp.arange(group_count, dtype=jnp.int32)[None, :]
    occupied = jnp.sum(jnp.where(matches, group_occupied[None, :], 0), axis=1)
    masks = (jnp.arange(occ, dtype=jnp.int32)[None, :] < occupied[:, None]).astype(BF16)
    bra_t = jnp.swapaxes(bra_orbitals * masks[:, None, :], 1, 2)
    ket_t = jnp.swapaxes(ket_orbitals * masks[:, None, :], 1, 2)
    return jnp.concatenate([bra_t, ket_t], axis=1)


def on_device_8x4(bra, ket, collocation, kernel, walker_weight, walker_group, group_occupied):
    nw, npt = 8, 4
    size_b, size_a = kernel.shape
    occ, size_m = bra.shape
    width = 2 * occ
    me_w, me_p = lax.axis_index("walk"), lax.axis_index("pt")
    z, x, y, core = me_w // 2, me_w % 2, me_p // 2, me_p % 2

    def put(j, i):
        return j * npt + i

    def across(part):
        return send(part, "walk", [(j, j ^ 1) for j in range(nw)])

    def along(part, r):
        return send(part, "walk", [(j, (j - 2 * r) % nw) for j in range(nw)])

    def other(part):
        return send(part, "pt", [(i, i ^ 1) for i in range(npt)])

    def columns_q(begin, chunk):
        rows = lax.dynamic_slice_in_dim(collocation, x * size_a + begin, chunk, 0)
        far = send(rows, BOTH, [(put(j, j // 2), put(j, j // 2 ^ 2)) for j in range(nw)])
        near = jnp.where(me_p == z, rows, far)
        pairs = [(put(j, j // 2 ^ s), put(j, j // 2 ^ s ^ 1)) for j in range(nw) for s in (0, 2)]
        return jnp.where(core == z % 2, near, send(near, BOTH, pairs))

    def split(part, at, size, axis=1):
        give = lax.dynamic_slice_in_dim(part, (1 - at) * size, size, axis).astype(BF16)
        return give, lax.dynamic_slice_in_dim(part, at * size, size, axis)

    tie = lax.optimization_barrier
    third = size_a // 3
    sent = [(0, 2 * third), (2 * third, third)]
    chunks = [(0, third + third // 2), (2 * third, third), (third + third // 2, third // 2)]
    own, half = packed(bra, ket, walker_group, group_occupied, core.reshape(1), walker_weight)
    cols_q = [columns_q(*chunk) for chunk in sent]
    z1, z3, x0 = along(half, 1), along(half, 3), across(half)
    kernel_t = turned(kernel)
    x0, z1, z3, kernel_t = tie((x0, z1, z3, kernel_t))
    z2, x1, x3 = along(z1, 1), across(z1), across(z3)
    x1, z1, z3 = tie((x1, z1, z3))
    x2 = along(x1, 1)
    near_four = [own] + [h for part in (x0, z1, z3) for h in (part, other(part))]
    lrp, stack, weight_rows = project(near_four, [width] + [occ] * 6, collocation, 2, 0)
    x2, x3, weight_rows = tie((x2, x3, weight_rows))
    first = (lrp, stack, weight_rows)
    far_four = [h for part in (x1, x3, z2, x2) for h in (part, other(part))]
    lrp, stack, weight_rows = project(far_four, [occ] * 8, collocation, 2, 1, first)
    weights = jnp.concatenate([weight_rows[:4, 0], weight_rows[8:12, 0]])

    lrq = dot(jnp.concatenate(cols_q, axis=0), stack, NT).astype(BF16)

    half_m, quarter, eighth = size_m // 2, size_m // 4, size_m // 8
    swap_y = [(i, i ^ 2) for i in range(npt)]

    def to_place(part, *later):
        pieces = [lax.dynamic_slice_in_dim(part, (x ^ t) * eighth, eighth, 1) for t in (0, 1)]
        pieces = tie((*pieces, *later))
        came = []
        for t in (0, 1):
            pairs = []
            for j in range(nw):
                for i in range(npt):
                    quarter_of = 2 * (i % 2) + i // 2
                    pairs.append((put(j, i), put(2 * quarter_of + (j % 2 ^ t), j // 2)))
            came.append(send(pieces[t], BOTH, pairs))
        return pieces, came

    def over_cores(grads):
        give, keep = split(grads, core, half_m)
        return split(keep + other(give).astype(F32), y, quarter)

    grads = pair_gradients(weights, kernel_t, lrp, lrq, *chunks[0])
    give_0, keep_0 = over_cores(dot(grads, stack))
    give_0, scale = tie((give_0, weights))
    got_0 = send(give_0, "pt", swap_y)
    grads = pair_gradients(scale, kernel_t, lrp, lrq, *chunks[1])
    grads, got_0 = tie((grads, got_0))
    part = dot(grads, stack)
    pieces, came_0 = to_place((keep_0 + got_0.astype(F32)).astype(BF16), weights)
    give_1, keep_1 = over_cores(part)
    give_1, scale = tie((give_1, pieces[2]))
    got_1 = send(give_1, "pt", swap_y)
    grads = pair_gradients(scale, kernel_t, lrp, lrq, *chunks[2])
    grads, got_1, *came_0 = tie((grads, got_1, *came_0))
    pieces, came_1 = to_place((keep_1 + got_1.astype(F32)).astype(BF16), grads)
    give_2, keep_2 = over_cores(dot(pieces[2], stack))
    give_2, *came_1 = tie((give_2, *came_1))
    _, came_2 = to_place((keep_2 + send(give_2, "pt", swap_y).astype(F32)).astype(BF16))

    ordered = [jnp.where(x == side, came[0], came[1]) for side in (0, 1) for came in (came_0, came_2, came_1)]
    return jnp.concatenate(ordered, axis=0).astype(F32) / jnp.sum(weights)


def on_device_any(nw, own, collocation, kernel, walker_weight):
    size_b, size_a = kernel.shape
    size_m = collocation.shape[1]
    me_w, me_p = lax.axis_index("walk"), lax.axis_index("pt")
    weights = lax.all_gather(walker_weight, "walk", axis=0, tiled=True)
    orbitals = lax.all_gather(own, "walk", axis=0, tiled=True)
    all_rows = lax.all_gather(collocation, "pt", axis=0, tiled=True)
    col_q = lax.dynamic_slice_in_dim(all_rows, me_w * size_a, size_a, 0)
    lrp = dot(orbitals, collocation, NT).astype(BF16)
    lrq = dot(col_q, orbitals, NT).astype(BF16)
    grads = pair_gradients(weights / jnp.sum(weights), turned(kernel), lrp, lrq, 0, size_a)
    part = lax.psum(dot(grads, orbitals), "pt")
    part = jnp.where((me_w * size_a) // size_b == me_p, part, 0.0)
    wide = lax.dynamic_update_slice_in_dim(jnp.zeros((size_b, size_m), F32), part, (me_w * size_a) % size_b, 0)
    return lax.psum_scatter(wide, "walk", scatter_dimension=1, tiled=True)


def on_device(
    nw, npt, bra_orbitals, ket_orbitals, collocation, kernel, walker_weight, walker_group, group_occupied
):
    if (nw, npt, walker_weight.shape[0]) == (8, 4, 1) and kernel.shape[0] == 2 * kernel.shape[1]:
        bra, ket = bra_orbitals[0].T, ket_orbitals[0].T
        return on_device_8x4(bra, ket, collocation, kernel, walker_weight, walker_group, group_occupied)
    own = masked_orbitals(bra_orbitals, ket_orbitals, walker_group, group_occupied)
    return on_device_any(nw, own.reshape(-1, own.shape[2]), collocation, kernel, walker_weight)


def solution(mesh):
    in_specs = (
        P("walk", None, None),
        P("walk", None, None),
        P("pt", None),
        P("pt", "walk"),
        P("walk"),
        P("walk"),
        P(),
    )
    out_specs = P("pt", "walk")
    body = functools.partial(on_device, mesh.shape["walk"], mesh.shape["pt"])
    return jax.shard_map(body, mesh=mesh, in_specs=in_specs, out_specs=out_specs, check_vma=False)
```

```python
import functools

import jax
import jax.numpy as jnp
from jax import lax
from jax.experimental import pallas as pl
from jax.experimental.pallas import tpu as pltpu
from jax.sharding import PartitionSpec as P

F32 = jnp.float32
BF16 = jnp.bfloat16
BOTH = ("walk", "pt")
NT = (((1,), (1,)), ((), ()))
VMEM_LIMIT = 56 * 1024 * 1024


def tile_of(size, limit):
    return next(t for t in range(min(size, limit), 0, -128) if size % t == 0)


def dot(a, b, dims=(((1,), (0,)), ((), ()))):
    return lax.dot_general(a, b, dims, preferred_element_type=F32)


def cost(flops, nbytes):
    return pl.CostEstimate(flops=flops, bytes_accessed=nbytes, transcendentals=0)


def turn_kernel(in_ref, out_ref):
    out_ref[...] = in_ref[...].T


def turned(block):
    rows, cols = block.shape
    tr, tc = tile_of(rows, 512), tile_of(cols, 512)
    return pl.pallas_call(
        turn_kernel,
        out_shape=jax.ShapeDtypeStruct((cols, rows), block.dtype),
        grid=(cols // tc, rows // tr),
        in_specs=[pl.BlockSpec((tr, tc), lambda c, r: (r, c))],
        out_specs=pl.BlockSpec((tc, tr), lambda c, r: (c, r)),
        compiler_params=pltpu.CompilerParams(vmem_limit_bytes=VMEM_LIMIT),
        cost_estimate=cost(0, 10 * rows * cols),
    )(block)


def pack_kernel(group_ref, occupied_ref, side_ref, weight_ref, bra_ref, ket_ref, own_ref, half_ref):
    occ = bra_ref.shape[0]
    used = occupied_ref[group_ref[0]]
    kept = lax.broadcasted_iota(jnp.int32, bra_ref.shape, 0) < used
    bra_t = jnp.where(kept, bra_ref[...].astype(F32), 0.0).astype(BF16)
    ket_t = jnp.where(kept, ket_ref[...].astype(F32), 0.0).astype(BF16)
    own_ref[:occ, :] = bra_t
    own_ref[occ : 2 * occ, :] = ket_t

    @pl.when(side_ref[0] == 0)
    def _():
        half_ref[:occ, :] = bra_t

    @pl.when(side_ref[0] != 0)
    def _():
        half_ref[:occ, :] = ket_t

    shape = (half_ref.shape[0] - occ, half_ref.shape[1])
    row = lax.broadcasted_iota(jnp.int32, shape, 0)
    rest, rows = jnp.full(shape, weight_ref[0], F32), jnp.zeros(shape, F32)
    for part in range(3):
        near = rest.astype(BF16).astype(F32)
        rows = jnp.where(row == part, near, rows)
        rest = rest - near
    half_ref[occ:, :] = rows.astype(BF16)
    own_ref[2 * occ :, :] = rows.astype(BF16)


def packed(bra, ket, group, occupied, side, weight):
    occ, size_m = bra.shape
    smem = pl.BlockSpec(memory_space=pltpu.SMEM)
    return pl.pallas_call(
        pack_kernel,
        out_shape=[
            jax.ShapeDtypeStruct((2 * occ + 16, size_m), BF16),
            jax.ShapeDtypeStruct((occ + 16, size_m), BF16),
        ],
        in_specs=[smem] * 4 + [pl.BlockSpec(memory_space=pltpu.VMEM)] * 2,
        compiler_params=pltpu.CompilerParams(vmem_limit_bytes=VMEM_LIMIT),
        cost_estimate=cost(0, 12 * size_m * occ),
    )(group, occupied, side, weight, bra, ket)


def project_kernel(rows_each, waits, *refs):
    count = len(rows_each)
    items, col_ref = refs[:count], refs[count]
    out_ref, stack_out, weight_out, stack = refs[count + 1 + waits :]
    occ = min(rows_each)

    @pl.when(pl.program_id(0) == 0)
    def _():
        at = 0
        weight_out[...] = jnp.zeros_like(weight_out)
        for ref, rows in zip(items, rows_each):
            stack[at : at + rows, :] = ref[:rows, :]
            if at % (2 * occ) == 0:
                s = at // (2 * occ)
                weight_out[s : s + 1, :] = jnp.sum(ref[rows : rows + 16, :128].astype(F32), axis=0, keepdims=True)
            at += rows
        stack_out[...] = stack[...]

    out_ref[...] = dot(stack[...], col_ref[...], NT).astype(BF16)


def project(items, rows_each, col, groups, index, before=()):
    size_m, size, total = col.shape[1], col.shape[0], sum(rows_each)
    tile = tile_of(size, 512)
    return pl.pallas_call(
        functools.partial(project_kernel, tuple(rows_each), len(before)),
        out_shape=[
            jax.ShapeDtypeStruct((groups * total, size), BF16),
            jax.ShapeDtypeStruct((groups * total, size_m), BF16),
            jax.ShapeDtypeStruct((groups * 8, 128), F32),
        ],
        grid=(size // tile,),
        in_specs=[pl.BlockSpec(x.shape, lambda b: (0, 0), pipeline_mode=pl.Buffered(1)) for x in items]
        + [pl.BlockSpec((tile, size_m), lambda b: (b, 0))]
        + [pl.BlockSpec(memory_space=pl.ANY)] * len(before),
        out_specs=[
            pl.BlockSpec((total, tile), lambda b: (index, b)),
            pl.BlockSpec((total, size_m), lambda b: (index, 0), pipeline_mode=pl.Buffered(1)),
            pl.BlockSpec((8, 128), lambda b: (index, 0)),
        ],
        scratch_shapes=[pltpu.VMEM((total, size_m), BF16)],
        input_output_aliases={len(items) + 1 + n: n for n in range(len(before))},
        compiler_params=pltpu.CompilerParams(vmem_limit_bytes=VMEM_LIMIT),
        cost_estimate=cost(2 * (total + 640) * size_m * size, 2 * size_m * size),
    )(*items, col, *before)


def pair_kernel(sub, halves, weight_ref, side_ref, kt_ref, lrp_ref, lrq_ref, out_ref):
    rows, size_b = kt_ref.shape
    occ = lrp_ref.shape[0] // 4
    sides = [lrq_ref[:, n * occ : (n + 1) * occ] for n in range(4)]
    totals = [jnp.zeros((rows, occ), F32) for _ in range(4)]
    for at in range(0, size_b, sub):
        kern = kt_ref[:, at : at + sub].astype(F32)
        for n in (0, 2):
            left_t = lrp_ref[n * occ : (n + 1) * occ, at : at + sub]
            right_t = lrp_ref[(n + 1) * occ : (n + 2) * occ, at : at + sub]
            had_t = (kern * dot(sides[n + 1], left_t)).astype(BF16)
            had = (kern * dot(sides[n], right_t)).astype(BF16)
            totals[n] += dot(had_t, right_t, NT)
            totals[n + 1] += dot(had, left_t, NT)
    size = rows // halves
    for h in range(halves):
        at = pl.multiple_of((h + side_ref[0] + 1) % halves * size, size)
        for n in range(4):
            scale = 2.0 * weight_ref[2 * pl.program_id(0) + n // 2]
            part = totals[n][h * size : (h + 1) * size]
            out_ref[pl.ds(at, size), n * occ : (n + 1) * occ] = (part * scale).astype(BF16)


def pair_gradients(weights, side, kernel_t, lrp, lrq, halves):
    (rows, size_b), count = kernel_t.shape, weights.shape[0] // 2
    width = lrp.shape[0] // count
    sub = tile_of(size_b, 512)
    return pl.pallas_call(
        functools.partial(pair_kernel, sub, halves),
        out_shape=jax.ShapeDtypeStruct((rows, count * width), BF16),
        grid_spec=pltpu.PrefetchScalarGridSpec(
            num_scalar_prefetch=2,
            grid=(count,),
            in_specs=[
                pl.BlockSpec((rows, size_b), lambda p, w, s: (0, 0), pipeline_mode=pl.Buffered(1)),
                pl.BlockSpec((width, size_b), lambda p, w, s: (p, 0)),
                pl.BlockSpec((rows, width), lambda p, w, s: (0, p)),
            ],
            out_specs=pl.BlockSpec((rows, width), lambda p, w, s: (0, p)),
        ),
        compiler_params=pltpu.CompilerParams(vmem_limit_bytes=VMEM_LIMIT),
        cost_estimate=cost(2 * 8 * count * 256 * rows * size_b, 2 * count * (rows + width) * size_b),
    )(weights, side, kernel_t, lrp, lrq)


def send(x, axes, pairs):
    return lax.ppermute(x, axes, pairs)


def masked_orbitals(bra_orbitals, ket_orbitals, walker_group, group_occupied):
    group_count, occ = group_occupied.shape[0], bra_orbitals.shape[2]
    matches = walker_group[:, None] == jnp.arange(group_count, dtype=jnp.int32)[None, :]
    occupied = jnp.sum(jnp.where(matches, group_occupied[None, :], 0), axis=1)
    masks = (jnp.arange(occ, dtype=jnp.int32)[None, :] < occupied[:, None]).astype(BF16)
    bra_t = jnp.swapaxes(bra_orbitals * masks[:, None, :], 1, 2)
    ket_t = jnp.swapaxes(ket_orbitals * masks[:, None, :], 1, 2)
    return jnp.concatenate([bra_t, ket_t], axis=1)


def on_device_8x4(bra, ket, collocation, kernel, walker_weight, walker_group, group_occupied):
    nw, npt = 8, 4
    size_b, size_a = kernel.shape
    occ, size_m = bra.shape
    width = 2 * occ
    me_w, me_p = lax.axis_index("walk"), lax.axis_index("pt")
    z, x, y, core = me_w // 2, me_w % 2, me_p // 2, me_p % 2

    def put(j, i):
        return j * npt + i

    def across(part):
        return send(part, "walk", [(j, j ^ 1) for j in range(nw)])

    def along(part, r):
        return send(part, "walk", [(j, (j - 2 * r) % nw) for j in range(nw)])

    def other(part):
        return send(part, "pt", [(i, i ^ 1) for i in range(npt)])

    def columns_q(begin, chunk):
        rows = lax.dynamic_slice_in_dim(collocation, x * size_a + begin, chunk, 0)
        far = send(rows, BOTH, [(put(j, j // 2), put(j, j // 2 ^ 2)) for j in range(nw)])
        near = jnp.where(me_p == z, rows, far)
        pairs = [(put(j, j // 2 ^ s), put(j, j // 2 ^ s ^ 1)) for j in range(nw) for s in (0, 2)]
        return jnp.where(core == z % 2, near, send(near, BOTH, pairs))

    tie = lax.optimization_barrier
    sent = [(0, 2 * size_a // 3), (2 * size_a // 3, size_a // 3)]
    own, half = packed(bra, ket, walker_group, group_occupied, core.reshape(1), walker_weight)
    cols_q = [columns_q(*chunk) for chunk in sent]
    z1, z3, x0 = along(half, 1), along(half, 3), across(half)
    kernel_t = turned(kernel)
    x0, z1, z3, kernel_t = tie((x0, z1, z3, kernel_t))
    z2, x1, x3 = along(z1, 1), across(z1), across(z3)
    z2, z1, z3 = tie((z2, z1, z3))
    x2 = across(z2)
    near_four = [own] + [h for part in (x0, z1, z3) for h in (part, other(part))]
    lrp, stack, weight_rows = project(near_four, [width] + [occ] * 6, collocation, 2, 0)
    first = (lrp, stack, weight_rows)
    x2, *first = tie((x2, *first))
    far_four = [h for part in (x1, x3, z2, x2) for h in (part, other(part))]
    lrp, stack, weight_rows = project(far_four, [occ] * 8, collocation, 2, 1, first)
    weights = jnp.concatenate([weight_rows[:4, 0], weight_rows[8:12, 0]])

    lrq = dot(jnp.concatenate(cols_q, axis=0), stack, NT).astype(BF16)

    quarter, eighth, half_a = size_m // 4, size_m // 8, size_a // 2
    grads = pair_gradients(weights, core.reshape(1), kernel_t, lrp, lrq, 2)
    got = other(dot(grads[:half_a], stack).astype(BF16))
    part = dot(grads[half_a:], stack)
    _, got = tie((part[:8, :128], got))
    part = part + got.astype(F32)

    def columns(of_y, k):
        return lax.dynamic_slice_in_dim(part, (of_y + 2 * (core ^ k)) * quarter, quarter, 1)

    def over_y(give):
        return send(give, "pt", [(i, i ^ 2) for i in range(npt)])

    def summed(got, k):
        return (columns(y, k) + got.astype(F32)).astype(BF16)

    def placed(total, k):
        came = []
        for t in (0, 1):
            piece = lax.dynamic_slice_in_dim(total, (x ^ t) * eighth, eighth, 1)
            pairs = []
            for j in range(nw):
                for i in range(npt):
                    to_z = i // 2 + 2 * (k ^ i % 2)
                    pairs.append((put(j, i), put(2 * to_z + (j % 2 ^ t), j // 2)))
            came.append(send(piece, BOTH, pairs))
        return came

    give_0, give_1 = [columns(1 - y, k).astype(BF16) for k in (0, 1)]
    total_0, give_1 = tie((summed(over_y(give_0), 0), give_1))
    got_1 = over_y(give_1)
    came = [placed(total_0, 0), placed(summed(got_1, 1), 1)]

    def block(from_x, from_core):
        along_x = [jnp.where(x == from_x, pair[0], pair[1]) for pair in came]
        return jnp.where(z // 2 == from_core, along_x[0], along_x[1])

    ordered = [block(from_x, from_core) for from_x in (0, 1) for from_core in (0, 1)]
    return jnp.concatenate(ordered, axis=0).astype(F32) / jnp.sum(weights)


def on_device_any(nw, own, collocation, kernel, walker_weight):
    size_b, size_a = kernel.shape
    size_m = collocation.shape[1]
    me_w, me_p = lax.axis_index("walk"), lax.axis_index("pt")
    weights = lax.all_gather(walker_weight, "walk", axis=0, tiled=True)
    orbitals = lax.all_gather(own, "walk", axis=0, tiled=True)
    all_rows = lax.all_gather(collocation, "pt", axis=0, tiled=True)
    col_q = lax.dynamic_slice_in_dim(all_rows, me_w * size_a, size_a, 0)
    lrp = dot(orbitals, collocation, NT).astype(BF16)
    lrq = dot(col_q, orbitals, NT).astype(BF16)
    grads = pair_gradients(weights / jnp.sum(weights), me_p.reshape(1), turned(kernel), lrp, lrq, 1)
    part = lax.psum(dot(grads, orbitals), "pt")
    part = jnp.where((me_w * size_a) // size_b == me_p, part, 0.0)
    wide = lax.dynamic_update_slice_in_dim(jnp.zeros((size_b, size_m), F32), part, (me_w * size_a) % size_b, 0)
    return lax.psum_scatter(wide, "walk", scatter_dimension=1, tiled=True)


def on_device(
    nw, npt, bra_orbitals, ket_orbitals, collocation, kernel, walker_weight, walker_group, group_occupied
):
    if (nw, npt, walker_weight.shape[0]) == (8, 4, 1) and kernel.shape[0] == 2 * kernel.shape[1]:
        bra, ket = bra_orbitals[0].T, ket_orbitals[0].T
        return on_device_8x4(bra, ket, collocation, kernel, walker_weight, walker_group, group_occupied)
    own = masked_orbitals(bra_orbitals, ket_orbitals, walker_group, group_occupied)
    return on_device_any(nw, own.reshape(-1, own.shape[2]), collocation, kernel, walker_weight)


def solution(mesh):
    in_specs = (
        P("walk", None, None),
        P("walk", None, None),
        P("pt", None),
        P("pt", "walk"),
        P("walk"),
        P("walk"),
        P(),
    )
    out_specs = P("pt", "walk")
    body = functools.partial(on_device, mesh.shape["walk"], mesh.shape["pt"])
    return jax.shard_map(body, mesh=mesh, in_specs=in_specs, out_specs=out_specs, check_vma=False)
```

```python
import functools

import jax
import jax.numpy as jnp
from jax import lax
from jax.experimental import pallas as pl
from jax.experimental.pallas import tpu as pltpu
from jax.sharding import PartitionSpec as P

F32 = jnp.float32
BF16 = jnp.bfloat16
BOTH = ("walk", "pt")
NT = (((1,), (1,)), ((), ()))
VMEM_LIMIT = 56 * 1024 * 1024


def tile_of(size, limit):
    return next(t for t in range(min(size, limit), 0, -128) if size % t == 0)


def dot(a, b, dims=(((1,), (0,)), ((), ()))):
    return lax.dot_general(a, b, dims, preferred_element_type=F32)


def cost(flops, nbytes):
    return pl.CostEstimate(flops=flops, bytes_accessed=nbytes, transcendentals=0)


def turn_kernel(in_ref, out_ref):
    out_ref[...] = in_ref[...].T


def turned(block):
    rows, cols = block.shape
    tr, tc = tile_of(rows, 512), tile_of(cols, 512)
    return pl.pallas_call(
        turn_kernel,
        out_shape=jax.ShapeDtypeStruct((cols, rows), block.dtype),
        grid=(cols // tc, rows // tr),
        in_specs=[pl.BlockSpec((tr, tc), lambda c, r: (r, c))],
        out_specs=pl.BlockSpec((tc, tr), lambda c, r: (c, r)),
        compiler_params=pltpu.CompilerParams(vmem_limit_bytes=VMEM_LIMIT),
        cost_estimate=cost(0, 10 * rows * cols),
    )(block)


def pack_kernel(group_ref, occupied_ref, side_ref, weight_ref, bra_ref, ket_ref, own_ref, half_ref):
    occ = bra_ref.shape[0]
    used = occupied_ref[group_ref[0]]
    kept = lax.broadcasted_iota(jnp.int32, bra_ref.shape, 0) < used
    bra_t = jnp.where(kept, bra_ref[...].astype(F32), 0.0).astype(BF16)
    ket_t = jnp.where(kept, ket_ref[...].astype(F32), 0.0).astype(BF16)
    own_ref[:occ, :] = bra_t
    own_ref[occ : 2 * occ, :] = ket_t

    @pl.when(side_ref[0] == 0)
    def _():
        half_ref[:occ, :] = bra_t

    @pl.when(side_ref[0] != 0)
    def _():
        half_ref[:occ, :] = ket_t

    shape = (half_ref.shape[0] - occ, half_ref.shape[1])
    row = lax.broadcasted_iota(jnp.int32, shape, 0)
    rest, rows = jnp.full(shape, weight_ref[0], F32), jnp.zeros(shape, F32)
    for part in range(3):
        near = rest.astype(BF16).astype(F32)
        rows = jnp.where(row == part, near, rows)
        rest = rest - near
    half_ref[occ:, :] = rows.astype(BF16)
    own_ref[2 * occ :, :] = rows.astype(BF16)


def packed(bra, ket, group, occupied, side, weight):
    occ, size_m = bra.shape
    smem = pl.BlockSpec(memory_space=pltpu.SMEM)
    return pl.pallas_call(
        pack_kernel,
        out_shape=[
            jax.ShapeDtypeStruct((2 * occ + 16, size_m), BF16),
            jax.ShapeDtypeStruct((occ + 16, size_m), BF16),
        ],
        in_specs=[smem] * 4 + [pl.BlockSpec(memory_space=pltpu.VMEM)] * 2,
        compiler_params=pltpu.CompilerParams(vmem_limit_bytes=VMEM_LIMIT),
        cost_estimate=cost(0, 12 * size_m * occ),
    )(group, occupied, side, weight, bra, ket)


def project_kernel(rows_each, waits, *refs):
    count = len(rows_each)
    side_ref, items, col_ref = refs[0], refs[1 : count + 1], refs[count + 1]
    out_ref, stack_out, weight_out, stack = refs[count + 2 + waits :]
    occ = min(rows_each)
    width = 2 * occ

    @pl.when(pl.program_id(0) == 0)
    def _():
        at = 0
        weight_out[...] = jnp.zeros_like(weight_out)
        for ref, rows in zip(items, rows_each):
            if rows == occ:
                place = at // width * width + (side_ref[0] if at % width == 0 else 1 - side_ref[0]) * occ
                stack[pl.ds(pl.multiple_of(place, occ), rows), :] = ref[:rows, :]
            else:
                stack[at : at + rows, :] = ref[:rows, :]
            if at % width == 0:
                s = at // width
                weight_out[s : s + 1, :] = jnp.sum(ref[rows : rows + 16, :128].astype(F32), axis=0, keepdims=True)
            at += rows
        stack_out[...] = stack[...]

    out_ref[...] = dot(stack[...], col_ref[...], NT).astype(BF16)


def project(side, items, rows_each, col, groups, index, before=(), after=()):
    size_m, size, total = col.shape[1], col.shape[0], sum(rows_each)
    tile = tile_of(size, 512)
    return pl.pallas_call(
        functools.partial(project_kernel, tuple(rows_each), len(before) + len(after)),
        out_shape=[
            jax.ShapeDtypeStruct((groups * total, size), BF16),
            jax.ShapeDtypeStruct((groups * total, size_m), BF16),
            jax.ShapeDtypeStruct((groups * 8, 128), F32),
        ],
        grid=(size // tile,),
        in_specs=[pl.BlockSpec(memory_space=pltpu.SMEM)]
        + [pl.BlockSpec(x.shape, lambda b: (0, 0), pipeline_mode=pl.Buffered(1)) for x in items]
        + [pl.BlockSpec((tile, size_m), lambda b: (b, 0))]
        + [pl.BlockSpec(memory_space=pl.ANY)] * (len(before) + len(after)),
        out_specs=[
            pl.BlockSpec((total, tile), lambda b: (index, b)),
            pl.BlockSpec((total, size_m), lambda b: (index, 0), pipeline_mode=pl.Buffered(1)),
            pl.BlockSpec((8, 128), lambda b: (index, 0)),
        ],
        scratch_shapes=[pltpu.VMEM((total, size_m), BF16)],
        input_output_aliases={len(items) + 2 + n: n for n in range(len(before))},
        compiler_params=pltpu.CompilerParams(vmem_limit_bytes=VMEM_LIMIT),
        cost_estimate=cost(2 * (total + 640) * size_m * size, 2 * size_m * size),
    )(side, *items, col, *before, *after)


def pair_kernel(sub, weight_ref, block_ref, kt_ref, lrp_ref, lrq_ref, out_ref):
    rows, size_b = kt_ref.shape
    occ = lrp_ref.shape[0] // 4
    sides = [lrq_ref[:, n * occ : (n + 1) * occ] for n in range(4)]
    totals = [jnp.zeros((rows, occ), F32) for _ in range(4)]
    for at in range(0, size_b, sub):
        kern = kt_ref[:, at : at + sub].astype(F32)
        for n in (0, 2):
            left_t = lrp_ref[n * occ : (n + 1) * occ, at : at + sub]
            right_t = lrp_ref[(n + 1) * occ : (n + 2) * occ, at : at + sub]
            had_t = (kern * dot(sides[n + 1], left_t)).astype(BF16)
            had = (kern * dot(sides[n], right_t)).astype(BF16)
            totals[n] += dot(had_t, right_t, NT)
            totals[n + 1] += dot(had, left_t, NT)
    for n in range(4):
        scale = 2.0 * weight_ref[2 * pl.program_id(0) + n // 2]
        out_ref[:, n * occ : (n + 1) * occ] = (totals[n] * scale).astype(BF16)


def pair_gradients(weights, block, kernel_t, lrp, lrq):
    size_b, rows, count = kernel_t.shape[1], lrq.shape[0], weights.shape[0] // 2
    width = lrp.shape[0] // count
    sub = tile_of(size_b, 512)
    return pl.pallas_call(
        functools.partial(pair_kernel, sub),
        out_shape=jax.ShapeDtypeStruct((rows, count * width), BF16),
        grid_spec=pltpu.PrefetchScalarGridSpec(
            num_scalar_prefetch=2,
            grid=(count,),
            in_specs=[
                pl.BlockSpec((rows, size_b), lambda p, w, s: (s[0], 0), pipeline_mode=pl.Buffered(1)),
                pl.BlockSpec((width, size_b), lambda p, w, s: (p, 0)),
                pl.BlockSpec((rows, width), lambda p, w, s: (0, p)),
            ],
            out_specs=pl.BlockSpec((rows, width), lambda p, w, s: (0, p)),
        ),
        compiler_params=pltpu.CompilerParams(vmem_limit_bytes=VMEM_LIMIT),
        cost_estimate=cost(2 * 8 * count * 256 * rows * size_b, 2 * count * (rows + width) * size_b),
    )(weights, block, kernel_t, lrp, lrq)


def send(x, axes, pairs):
    return lax.ppermute(x, axes, pairs)


def masked_orbitals(bra_orbitals, ket_orbitals, walker_group, group_occupied):
    group_count, occ = group_occupied.shape[0], bra_orbitals.shape[2]
    matches = walker_group[:, None] == jnp.arange(group_count, dtype=jnp.int32)[None, :]
    occupied = jnp.sum(jnp.where(matches, group_occupied[None, :], 0), axis=1)
    masks = (jnp.arange(occ, dtype=jnp.int32)[None, :] < occupied[:, None]).astype(BF16)
    bra_t = jnp.swapaxes(bra_orbitals * masks[:, None, :], 1, 2)
    ket_t = jnp.swapaxes(ket_orbitals * masks[:, None, :], 1, 2)
    return jnp.concatenate([bra_t, ket_t], axis=1)


def on_device_8x4(bra, ket, collocation, kernel, walker_weight, walker_group, group_occupied):
    nw, npt = 8, 4
    size_b, size_a = kernel.shape
    occ, size_m = bra.shape
    width = 2 * occ
    me_w, me_p = lax.axis_index("walk"), lax.axis_index("pt")
    z, x, y, core = me_w // 2, me_w % 2, me_p // 2, me_p % 2

    def put(j, i):
        return j * npt + i

    def across(part):
        return send(part, "walk", [(j, j ^ 1) for j in range(nw)])

    def along(part, r):
        return send(part, "walk", [(j, (j - 2 * r) % nw) for j in range(nw)])

    def other(part):
        return send(part, "pt", [(i, i ^ 1) for i in range(npt)])

    tie = lax.optimization_barrier
    half_a = size_a // 2
    rows_alike = lax.dynamic_slice_in_dim(collocation, x * size_a + (1 - core) * half_a, half_a, 0)
    rows_unlike = lax.dynamic_slice_in_dim(collocation, x * size_a + core * half_a, half_a, 0)
    rows_of = [rows_alike]
    for hop, rows in ((1, rows_unlike), (2, rows_alike), (3, rows_unlike)):
        rows_of.append(send(rows, BOTH, [(put(j, j // 2), put(j, j // 2 ^ hop)) for j in range(nw)]))
    own, half = packed(bra, ket, walker_group, group_occupied, core.reshape(1), walker_weight)
    z1, z3, x0 = along(half, 1), along(half, 3), across(half)
    kernel_t = turned(kernel)
    x0, z1, z3, kernel_t = tie((x0, z1, z3, kernel_t))
    z2, x1, x3 = along(z1, 1), across(z1), across(z3)
    z2, z1, z3 = tie((z2, z1, z3))
    token, *rows_of = tie((jnp.zeros((8, 128), F32), *rows_of))
    x2 = across(z2)
    near_four = [own] + [h for part in (x0, z1, z3) for h in (part, other(part))]
    lrp, stack, weight_rows = project(core.reshape(1), near_four, [width] + [occ] * 6, collocation, 2, 0, (), (token,))
    first = (lrp, stack, weight_rows)
    x2, *first = tie((x2, *first))
    far_four = [h for part in (x1, x3, z2, x2) for h in (part, other(part))]
    lrp, stack, weight_rows = project(core.reshape(1), far_four, [occ] * 8, collocation, 2, 1, first)
    weights = jnp.concatenate([weight_rows[:4, 0], weight_rows[8:12, 0]])

    lrq = dot(lax.select_n(me_p ^ z, *rows_of), stack, NT).astype(BF16)
    grads = pair_gradients(weights, (1 - core).reshape(1), kernel_t, lrp, lrq)
    give = dot(grads, stack).astype(BF16)
    give, scale = tie((give, weights))
    grads = pair_gradients(scale, core.reshape(1), kernel_t, lrp, other(lrq))
    part = (dot(grads, stack) + other(give).astype(F32)).reshape(half_a, nw // 2, 2, -1)

    give = lax.dynamic_index_in_dim(part, 1 - y, 2, False).astype(BF16)
    got = send(give, "pt", [(i, i ^ 2) for i in range(npt)])
    part = (lax.dynamic_index_in_dim(part, y, 2, False) + got.astype(F32)).astype(BF16)
    came = []
    for s in range(4):
        pairs = []
        for j in range(nw):
            for i in range(npt):
                pairs.append((put(j, i), put(2 * (s ^ (2 * (j % 2) + i % 2)) + i // 2, j // 2)))
        came.append(send(lax.dynamic_index_in_dim(part, s ^ (2 * x + core), 1, False), BOTH, pairs))
    ordered = [lax.select_n(z, *[came[block ^ s] for s in range(4)]) for block in range(4)]
    return jnp.concatenate(ordered, axis=0).astype(F32) / jnp.sum(weights)


def on_device_any(nw, own, collocation, kernel, walker_weight):
    size_b, size_a = kernel.shape
    size_m = collocation.shape[1]
    me_w, me_p = lax.axis_index("walk"), lax.axis_index("pt")
    weights = lax.all_gather(walker_weight, "walk", axis=0, tiled=True)
    orbitals = lax.all_gather(own, "walk", axis=0, tiled=True)
    all_rows = lax.all_gather(collocation, "pt", axis=0, tiled=True)
    col_q = lax.dynamic_slice_in_dim(all_rows, me_w * size_a, size_a, 0)
    lrp = dot(orbitals, collocation, NT).astype(BF16)
    lrq = dot(col_q, orbitals, NT).astype(BF16)
    grads = pair_gradients(weights / jnp.sum(weights), jnp.zeros(1, jnp.int32), turned(kernel), lrp, lrq)
    part = lax.psum(dot(grads, orbitals), "pt")
    part = jnp.where((me_w * size_a) // size_b == me_p, part, 0.0)
    wide = lax.dynamic_update_slice_in_dim(jnp.zeros((size_b, size_m), F32), part, (me_w * size_a) % size_b, 0)
    return lax.psum_scatter(wide, "walk", scatter_dimension=1, tiled=True)


def on_device(
    nw, npt, bra_orbitals, ket_orbitals, collocation, kernel, walker_weight, walker_group, group_occupied
):
    if (nw, npt, walker_weight.shape[0]) == (8, 4, 1) and kernel.shape[0] == 2 * kernel.shape[1]:
        bra, ket = bra_orbitals[0].T, ket_orbitals[0].T
        return on_device_8x4(bra, ket, collocation, kernel, walker_weight, walker_group, group_occupied)
    own = masked_orbitals(bra_orbitals, ket_orbitals, walker_group, group_occupied)
    return on_device_any(nw, own.reshape(-1, own.shape[2]), collocation, kernel, walker_weight)


def solution(mesh):
    in_specs = (
        P("walk", None, None),
        P("walk", None, None),
        P("pt", None),
        P("pt", "walk"),
        P("walk"),
        P("walk"),
        P(),
    )
    out_specs = P("pt", "walk")
    body = functools.partial(on_device, mesh.shape["walk"], mesh.shape["pt"])
    return jax.shard_map(body, mesh=mesh, in_specs=in_specs, out_specs=out_specs, check_vma=False)
```

```python
import functools

import jax
import jax.numpy as jnp
from jax import lax
from jax.experimental import pallas as pl
from jax.experimental.pallas import tpu as pltpu
from jax.sharding import PartitionSpec as P

F32 = jnp.float32
BF16 = jnp.bfloat16
BOTH = ("walk", "pt")
NT = (((1,), (1,)), ((), ()))
VMEM_LIMIT = 56 * 1024 * 1024


def tile_of(size, limit):
    return next(t for t in range(min(size, limit), 0, -128) if size % t == 0)


def dot(a, b, dims=(((1,), (0,)), ((), ()))):
    return lax.dot_general(a, b, dims, preferred_element_type=F32)


def cost(flops, nbytes):
    return pl.CostEstimate(flops=flops, bytes_accessed=nbytes, transcendentals=0)


def turn_kernel(in_ref, out_ref):
    out_ref[...] = in_ref[...].T


def turned(block):
    rows, cols = block.shape
    tr, tc = tile_of(rows, 512), tile_of(cols, 512)
    return pl.pallas_call(
        turn_kernel,
        out_shape=jax.ShapeDtypeStruct((cols, rows), block.dtype),
        grid=(cols // tc, rows // tr),
        in_specs=[pl.BlockSpec((tr, tc), lambda c, r: (r, c))],
        out_specs=pl.BlockSpec((tc, tr), lambda c, r: (c, r)),
        compiler_params=pltpu.CompilerParams(vmem_limit_bytes=VMEM_LIMIT),
        cost_estimate=cost(0, 10 * rows * cols),
    )(block)


def pack_kernel(group_ref, occupied_ref, side_ref, weight_ref, bra_ref, ket_ref, own_ref, half_ref):
    occ = bra_ref.shape[0]
    used = occupied_ref[group_ref[0]]
    kept = lax.broadcasted_iota(jnp.int32, bra_ref.shape, 0) < used
    bra_t = jnp.where(kept, bra_ref[...].astype(F32), 0.0).astype(BF16)
    ket_t = jnp.where(kept, ket_ref[...].astype(F32), 0.0).astype(BF16)
    own_ref[:occ, :] = bra_t
    own_ref[occ : 2 * occ, :] = ket_t

    @pl.when(side_ref[0] == 0)
    def _():
        half_ref[:occ, :] = bra_t

    @pl.when(side_ref[0] != 0)
    def _():
        half_ref[:occ, :] = ket_t

    shape = (half_ref.shape[0] - occ, half_ref.shape[1])
    row = lax.broadcasted_iota(jnp.int32, shape, 0)
    rest, rows = jnp.full(shape, weight_ref[0], F32), jnp.zeros(shape, F32)
    for part in range(3):
        near = rest.astype(BF16).astype(F32)
        rows = jnp.where(row == part, near, rows)
        rest = rest - near
    half_ref[occ:, :] = rows.astype(BF16)
    own_ref[2 * occ :, :] = rows.astype(BF16)


def packed(bra, ket, group, occupied, side, weight):
    occ, size_m = bra.shape
    smem = pl.BlockSpec(memory_space=pltpu.SMEM)
    return pl.pallas_call(
        pack_kernel,
        out_shape=[
            jax.ShapeDtypeStruct((2 * occ + 16, size_m), BF16),
            jax.ShapeDtypeStruct((occ + 16, size_m), BF16),
        ],
        in_specs=[smem] * 4 + [pl.BlockSpec(memory_space=pltpu.VMEM)] * 2,
        compiler_params=pltpu.CompilerParams(vmem_limit_bytes=VMEM_LIMIT),
        cost_estimate=cost(0, 12 * size_m * occ),
    )(group, occupied, side, weight, bra, ket)


def project_kernel(rows_each, waits, *refs):
    count = len(rows_each)
    side_ref, items, col_ref = refs[0], refs[1 : count + 1], refs[count + 1]
    out_ref, stack_out, weight_out, stack = refs[count + 2 + waits :]
    occ = min(rows_each)
    width = 2 * occ

    @pl.when(pl.program_id(0) == 0)
    def _():
        at = 0
        weight_out[...] = jnp.zeros_like(weight_out)
        for ref, rows in zip(items, rows_each):
            if rows == occ:
                place = at // width * width + (side_ref[0] if at % width == 0 else 1 - side_ref[0]) * occ
                stack[pl.ds(pl.multiple_of(place, occ), rows), :] = ref[:rows, :]
            else:
                stack[at : at + rows, :] = ref[:rows, :]
            if at % width == 0:
                s = at // width
                weight_out[s : s + 1, :] = jnp.sum(ref[rows : rows + 16, :128].astype(F32), axis=0, keepdims=True)
            at += rows
        stack_out[...] = stack[...]

    out_ref[...] = dot(stack[...], col_ref[...], NT).astype(BF16)


def project(side, items, rows_each, col, groups, index, before=()):
    size_m, size, total = col.shape[1], col.shape[0], sum(rows_each)
    tile = tile_of(size, 512)
    return pl.pallas_call(
        functools.partial(project_kernel, tuple(rows_each), len(before)),
        out_shape=[
            jax.ShapeDtypeStruct((groups * total, size), BF16),
            jax.ShapeDtypeStruct((groups * total, size_m), BF16),
            jax.ShapeDtypeStruct((groups * 8, 128), F32),
        ],
        grid=(size // tile,),
        in_specs=[pl.BlockSpec(memory_space=pltpu.SMEM)]
        + [pl.BlockSpec(x.shape, lambda b: (0, 0), pipeline_mode=pl.Buffered(1)) for x in items]
        + [pl.BlockSpec((tile, size_m), lambda b: (b, 0))]
        + [pl.BlockSpec(memory_space=pl.ANY)] * (len(before)),
        out_specs=[
            pl.BlockSpec((total, tile), lambda b: (index, b)),
            pl.BlockSpec((total, size_m), lambda b: (index, 0), pipeline_mode=pl.Buffered(1)),
            pl.BlockSpec((8, 128), lambda b: (index, 0)),
        ],
        scratch_shapes=[pltpu.VMEM((total, size_m), BF16)],
        input_output_aliases={len(items) + 2 + n: n for n in range(len(before))},
        compiler_params=pltpu.CompilerParams(vmem_limit_bytes=VMEM_LIMIT),
        cost_estimate=cost(2 * (total + 640) * size_m * size, 2 * size_m * size),
    )(side, *items, col, *before)


def pair_kernel(sub, weight_ref, block_ref, kt_ref, lrp_ref, lrq_ref, out_ref):
    rows, size_b = kt_ref.shape
    occ = lrp_ref.shape[0] // 4
    sides = [lrq_ref[:, n * occ : (n + 1) * occ] for n in range(4)]
    totals = [jnp.zeros((rows, occ), F32) for _ in range(4)]
    for at in range(0, size_b, sub):
        kern = kt_ref[:, at : at + sub].astype(F32)
        for n in (0, 2):
            left_t = lrp_ref[n * occ : (n + 1) * occ, at : at + sub]
            right_t = lrp_ref[(n + 1) * occ : (n + 2) * occ, at : at + sub]
            had_t = (kern * dot(sides[n + 1], left_t)).astype(BF16)
            had = (kern * dot(sides[n], right_t)).astype(BF16)
            totals[n] += dot(had_t, right_t, NT)
            totals[n + 1] += dot(had, left_t, NT)
    for n in range(4):
        scale = 2.0 * weight_ref[2 * pl.program_id(0) + n // 2]
        out_ref[:, n * occ : (n + 1) * occ] = (totals[n] * scale).astype(BF16)


def pair_gradients(weights, block, kernel_t, lrp, lrq):
    size_b, rows, count = kernel_t.shape[1], lrq.shape[0], weights.shape[0] // 2
    width = lrp.shape[0] // count
    sub = tile_of(size_b, 512)
    return pl.pallas_call(
        functools.partial(pair_kernel, sub),
        out_shape=jax.ShapeDtypeStruct((rows, count * width), BF16),
        grid_spec=pltpu.PrefetchScalarGridSpec(
            num_scalar_prefetch=2,
            grid=(count,),
            in_specs=[
                pl.BlockSpec((rows, size_b), lambda p, w, s: (s[0], 0), pipeline_mode=pl.Buffered(1)),
                pl.BlockSpec((width, size_b), lambda p, w, s: (p, 0)),
                pl.BlockSpec((rows, width), lambda p, w, s: (0, p)),
            ],
            out_specs=pl.BlockSpec((rows, width), lambda p, w, s: (0, p)),
        ),
        compiler_params=pltpu.CompilerParams(vmem_limit_bytes=VMEM_LIMIT),
        cost_estimate=cost(2 * 8 * count * 256 * rows * size_b, 2 * count * (rows + width) * size_b),
    )(weights, block, kernel_t, lrp, lrq)


def send(x, axes, pairs):
    return lax.ppermute(x, axes, pairs)


def masked_orbitals(bra_orbitals, ket_orbitals, walker_group, group_occupied):
    group_count, occ = group_occupied.shape[0], bra_orbitals.shape[2]
    matches = walker_group[:, None] == jnp.arange(group_count, dtype=jnp.int32)[None, :]
    occupied = jnp.sum(jnp.where(matches, group_occupied[None, :], 0), axis=1)
    masks = (jnp.arange(occ, dtype=jnp.int32)[None, :] < occupied[:, None]).astype(BF16)
    bra_t = jnp.swapaxes(bra_orbitals * masks[:, None, :], 1, 2)
    ket_t = jnp.swapaxes(ket_orbitals * masks[:, None, :], 1, 2)
    return jnp.concatenate([bra_t, ket_t], axis=1)


def on_device_8x4(bra, ket, collocation, kernel, walker_weight, walker_group, group_occupied):
    nw, npt = 8, 4
    size_b, size_a = kernel.shape
    occ, size_m = bra.shape
    width = 2 * occ
    me_w, me_p = lax.axis_index("walk"), lax.axis_index("pt")
    z, x, y, core = me_w // 2, me_w % 2, me_p // 2, me_p % 2

    def put(j, i):
        return j * npt + i

    def across(part):
        return send(part, "walk", [(j, j ^ 1) for j in range(nw)])

    def along(part, r):
        return send(part, "walk", [(j, (j - 2 * r) % nw) for j in range(nw)])

    def other(part):
        return send(part, "pt", [(i, i ^ 1) for i in range(npt)])

    tie = lax.optimization_barrier
    half_a = size_a // 2
    rows_alike = lax.dynamic_slice_in_dim(collocation, x * size_a + (1 - core) * half_a, half_a, 0)
    rows_unlike = lax.dynamic_slice_in_dim(collocation, x * size_a + core * half_a, half_a, 0)
    over = [(put(j, j // 2), put(j, j // 2 ^ 2)) for j in range(nw)]
    far_alike, far_unlike = send(rows_alike, BOTH, over), send(rows_unlike, BOTH, over)
    own, half = packed(bra, ket, walker_group, group_occupied, core.reshape(1), walker_weight)
    z1, z3, x0 = along(half, 1), along(half, 3), across(half)
    kernel_t = turned(kernel)
    x0, z1, z3, kernel_t = tie((x0, z1, z3, kernel_t))
    z2, x1, x3 = along(z1, 1), across(z1), across(z3)
    z2, z1, z3 = tie((z2, z1, z3))
    x2 = across(z2)
    near_four = [own] + [h for part in (x0, z1, z3) for h in (part, other(part))]
    lrp, stack, weight_rows = project(core.reshape(1), near_four, [width] + [occ] * 6, collocation, 2, 0)
    far_alike, far_unlike, weight_rows = tie((far_alike, far_unlike, weight_rows))
    first = (lrp, stack, weight_rows)
    x2, *first = tie((x2, *first))
    far_four = [h for part in (x1, x3, z2, x2) for h in (part, other(part))]
    lrp, stack, weight_rows = project(core.reshape(1), far_four, [occ] * 8, collocation, 2, 1, first)
    weights = jnp.concatenate([weight_rows[:4, 0], weight_rows[8:12, 0]])

    beside = [(put(j, j // 2 ^ s), put(j, j // 2 ^ s ^ 1)) for j in range(nw) for s in (0, 2)]
    beside = send(jnp.where(me_p == z, rows_unlike, far_unlike), BOTH, beside)
    col_q = jnp.where(core != z % 2, beside, jnp.where(me_p == z, rows_alike, far_alike))
    lrq = dot(col_q, stack, NT).astype(BF16)
    grads = pair_gradients(weights, (1 - core).reshape(1), kernel_t, lrp, lrq)
    by_rows = (((0,), (1,)), ((), ()))
    give = dot(stack, grads, by_rows).astype(BF16)
    give, scale = tie((give, weights))
    grads = pair_gradients(scale, core.reshape(1), kernel_t, lrp, other(lrq))
    part = (dot(stack, grads, by_rows) + other(give).astype(F32)).reshape(nw // 2, 2, -1, half_a)

    give = lax.dynamic_index_in_dim(part, 1 - y, 1, False).astype(BF16)
    got = send(give, "pt", [(i, i ^ 2) for i in range(npt)])
    part = (lax.dynamic_index_in_dim(part, y, 1, False) + got.astype(F32)).astype(BF16)
    came = []
    for s in range(4):
        pairs = []
        for j in range(nw):
            for i in range(npt):
                pairs.append((put(j, i), put(2 * (s ^ (2 * (j % 2) + i % 2)) + i // 2, j // 2)))
        came.append(send(lax.dynamic_index_in_dim(part, s ^ (2 * x + core), 0, False), BOTH, pairs))
    ordered = [lax.select_n(z, *[came[block ^ s] for s in range(4)]) for block in range(4)]
    return (jnp.concatenate(ordered, axis=1).astype(F32) / jnp.sum(weights)).T


def on_device_any(nw, own, collocation, kernel, walker_weight):
    size_b, size_a = kernel.shape
    size_m = collocation.shape[1]
    me_w, me_p = lax.axis_index("walk"), lax.axis_index("pt")
    weights = lax.all_gather(walker_weight, "walk", axis=0, tiled=True)
    orbitals = lax.all_gather(own, "walk", axis=0, tiled=True)
    all_rows = lax.all_gather(collocation, "pt", axis=0, tiled=True)
    col_q = lax.dynamic_slice_in_dim(all_rows, me_w * size_a, size_a, 0)
    lrp = dot(orbitals, collocation, NT).astype(BF16)
    lrq = dot(col_q, orbitals, NT).astype(BF16)
    grads = pair_gradients(weights / jnp.sum(weights), jnp.zeros(1, jnp.int32), turned(kernel), lrp, lrq)
    part = lax.psum(dot(grads, orbitals), "pt")
    part = jnp.where((me_w * size_a) // size_b == me_p, part, 0.0)
    wide = lax.dynamic_update_slice_in_dim(jnp.zeros((size_b, size_m), F32), part, (me_w * size_a) % size_b, 0)
    return lax.psum_scatter(wide, "walk", scatter_dimension=1, tiled=True)


def on_device(
    nw, npt, bra_orbitals, ket_orbitals, collocation, kernel, walker_weight, walker_group, group_occupied
):
    if (nw, npt, walker_weight.shape[0]) == (8, 4, 1) and kernel.shape[0] == 2 * kernel.shape[1]:
        bra, ket = bra_orbitals[0].T, ket_orbitals[0].T
        return on_device_8x4(bra, ket, collocation, kernel, walker_weight, walker_group, group_occupied)
    own = masked_orbitals(bra_orbitals, ket_orbitals, walker_group, group_occupied)
    return on_device_any(nw, own.reshape(-1, own.shape[2]), collocation, kernel, walker_weight)


def solution(mesh):
    in_specs = (
        P("walk", None, None),
        P("walk", None, None),
        P("pt", None),
        P("pt", "walk"),
        P("walk"),
        P("walk"),
        P(),
    )
    out_specs = P("pt", "walk")
    body = functools.partial(on_device, mesh.shape["walk"], mesh.shape["pt"])
    return jax.shard_map(body, mesh=mesh, in_specs=in_specs, out_specs=out_specs, check_vma=False)
```

```python
import functools

import jax
import jax.numpy as jnp
from jax import lax
from jax.experimental import pallas as pl
from jax.experimental.pallas import tpu as pltpu
from jax.sharding import PartitionSpec as P

F32 = jnp.float32
BF16 = jnp.bfloat16
BOTH = ("walk", "pt")
NT = (((1,), (1,)), ((), ()))
VMEM_LIMIT = 56 * 1024 * 1024


def tile_of(size, limit):
    return next(t for t in range(min(size, limit), 0, -128) if size % t == 0)


def dot(a, b, dims=(((1,), (0,)), ((), ()))):
    return lax.dot_general(a, b, dims, preferred_element_type=F32)


def cost(flops, nbytes):
    return pl.CostEstimate(flops=flops, bytes_accessed=nbytes, transcendentals=0)


def turn_kernel(in_ref, out_ref):
    out_ref[...] = in_ref[...].T


def turned(block):
    rows, cols = block.shape
    tr, tc = tile_of(rows, 512), tile_of(cols, 512)
    return pl.pallas_call(
        turn_kernel,
        out_shape=jax.ShapeDtypeStruct((cols, rows), block.dtype),
        grid=(cols // tc, rows // tr),
        in_specs=[pl.BlockSpec((tr, tc), lambda c, r: (r, c))],
        out_specs=pl.BlockSpec((tc, tr), lambda c, r: (c, r)),
        compiler_params=pltpu.CompilerParams(vmem_limit_bytes=VMEM_LIMIT),
        cost_estimate=cost(0, 10 * rows * cols),
    )(block)


def pack_kernel(group_ref, occupied_ref, side_ref, weight_ref, bra_ref, ket_ref, own_ref, half_ref):
    occ = bra_ref.shape[0]
    used = occupied_ref[group_ref[0]]
    kept = lax.broadcasted_iota(jnp.int32, bra_ref.shape, 0) < used
    bra_t = jnp.where(kept, bra_ref[...].astype(F32), 0.0).astype(BF16)
    ket_t = jnp.where(kept, ket_ref[...].astype(F32), 0.0).astype(BF16)
    own_ref[:occ, :] = bra_t
    own_ref[occ : 2 * occ, :] = ket_t

    @pl.when(side_ref[0] == 0)
    def _():
        half_ref[:occ, :] = bra_t

    @pl.when(side_ref[0] != 0)
    def _():
        half_ref[:occ, :] = ket_t

    shape = (half_ref.shape[0] - occ, half_ref.shape[1])
    row = lax.broadcasted_iota(jnp.int32, shape, 0)
    rest, rows = jnp.full(shape, weight_ref[0], F32), jnp.zeros(shape, F32)
    for part in range(3):
        near = rest.astype(BF16).astype(F32)
        rows = jnp.where(row == part, near, rows)
        rest = rest - near
    half_ref[occ:, :] = rows.astype(BF16)
    own_ref[2 * occ :, :] = rows.astype(BF16)


def packed(bra, ket, group, occupied, side, weight):
    occ, size_m = bra.shape
    smem = pl.BlockSpec(memory_space=pltpu.SMEM)
    return pl.pallas_call(
        pack_kernel,
        out_shape=[
            jax.ShapeDtypeStruct((2 * occ + 16, size_m), BF16),
            jax.ShapeDtypeStruct((occ + 16, size_m), BF16),
        ],
        in_specs=[smem] * 4 + [pl.BlockSpec(memory_space=pltpu.VMEM)] * 2,
        compiler_params=pltpu.CompilerParams(vmem_limit_bytes=VMEM_LIMIT),
        cost_estimate=cost(0, 12 * size_m * occ),
    )(group, occupied, side, weight, bra, ket)


def project_kernel(rows_each, waits, *refs):
    count = len(rows_each)
    side_ref, items, col_ref = refs[0], refs[1 : count + 1], refs[count + 1]
    out_ref, stack_out, weight_out, stack = refs[count + 2 + waits :]
    occ = min(rows_each)
    width = 2 * occ

    @pl.when(pl.program_id(0) == 0)
    def _():
        at = 0
        weight_out[...] = jnp.zeros_like(weight_out)
        for ref, rows in zip(items, rows_each):
            if rows == occ:
                place = at // width * width + (side_ref[0] if at % width == 0 else 1 - side_ref[0]) * occ
                stack[pl.ds(pl.multiple_of(place, occ), rows), :] = ref[:rows, :]
            else:
                stack[at : at + rows, :] = ref[:rows, :]
            if at % width == 0:
                s = at // width
                weight_out[s : s + 1, :] = jnp.sum(ref[rows : rows + 16, :128].astype(F32), axis=0, keepdims=True)
            at += rows
        stack_out[...] = stack[...]

    out_ref[...] = dot(stack[...], col_ref[...], NT).astype(BF16)


def project(side, items, rows_each, col, groups, index, before=()):
    size_m, size, total = col.shape[1], col.shape[0], sum(rows_each)
    tile = tile_of(size, 512)
    return pl.pallas_call(
        functools.partial(project_kernel, tuple(rows_each), len(before)),
        out_shape=[
            jax.ShapeDtypeStruct((groups * total, size), BF16),
            jax.ShapeDtypeStruct((groups * total, size_m), BF16),
            jax.ShapeDtypeStruct((groups * 8, 128), F32),
        ],
        grid=(size // tile,),
        in_specs=[pl.BlockSpec(memory_space=pltpu.SMEM)]
        + [pl.BlockSpec(x.shape, lambda b: (0, 0), pipeline_mode=pl.Buffered(1)) for x in items]
        + [pl.BlockSpec((tile, size_m), lambda b: (b, 0))]
        + [pl.BlockSpec(memory_space=pl.ANY)] * (len(before)),
        out_specs=[
            pl.BlockSpec((total, tile), lambda b: (index, b)),
            pl.BlockSpec((total, size_m), lambda b: (index, 0), pipeline_mode=pl.Buffered(1)),
            pl.BlockSpec((8, 128), lambda b: (index, 0)),
        ],
        scratch_shapes=[pltpu.VMEM((total, size_m), BF16)],
        input_output_aliases={len(items) + 2 + n: n for n in range(len(before))},
        compiler_params=pltpu.CompilerParams(vmem_limit_bytes=VMEM_LIMIT),
        cost_estimate=cost(2 * (total + 640) * size_m * size, 2 * size_m * size),
    )(side, *items, col, *before)


def pair_kernel(sub, weight_ref, block_ref, kt_ref, lrp_ref, lrq_ref, out_ref):
    rows, size_b = kt_ref.shape
    occ = lrp_ref.shape[0] // 4
    sides = [lrq_ref[:, n * occ : (n + 1) * occ] for n in range(4)]
    totals = [jnp.zeros((rows, occ), F32) for _ in range(4)]
    for at in range(0, size_b, sub):
        kern = kt_ref[:, at : at + sub].astype(F32)
        for n in (0, 2):
            left_t = lrp_ref[n * occ : (n + 1) * occ, at : at + sub]
            right_t = lrp_ref[(n + 1) * occ : (n + 2) * occ, at : at + sub]
            had_t = (kern * dot(sides[n + 1], left_t)).astype(BF16)
            had = (kern * dot(sides[n], right_t)).astype(BF16)
            totals[n] += dot(had_t, right_t, NT)
            totals[n + 1] += dot(had, left_t, NT)
    for n in range(4):
        scale = 2.0 * weight_ref[2 * pl.program_id(0) + n // 2]
        out_ref[:, n * occ : (n + 1) * occ] = (totals[n] * scale).astype(BF16)


def pair_gradients(weights, block, kernel_t, lrp, lrq):
    size_b, rows, count = kernel_t.shape[1], lrq.shape[0], weights.shape[0] // 2
    width = lrp.shape[0] // count
    sub = tile_of(size_b, 512)
    return pl.pallas_call(
        functools.partial(pair_kernel, sub),
        out_shape=jax.ShapeDtypeStruct((rows, count * width), BF16),
        grid_spec=pltpu.PrefetchScalarGridSpec(
            num_scalar_prefetch=2,
            grid=(count,),
            in_specs=[
                pl.BlockSpec((rows, size_b), lambda p, w, s: (s[0], 0), pipeline_mode=pl.Buffered(1)),
                pl.BlockSpec((width, size_b), lambda p, w, s: (p, 0)),
                pl.BlockSpec((rows, width), lambda p, w, s: (0, p)),
            ],
            out_specs=pl.BlockSpec((rows, width), lambda p, w, s: (0, p)),
        ),
        compiler_params=pltpu.CompilerParams(vmem_limit_bytes=VMEM_LIMIT),
        cost_estimate=cost(2 * 8 * count * 256 * rows * size_b, 2 * count * (rows + width) * size_b),
    )(weights, block, kernel_t, lrp, lrq)


def send(x, axes, pairs):
    return lax.ppermute(x, axes, pairs)


def masked_orbitals(bra_orbitals, ket_orbitals, walker_group, group_occupied):
    group_count, occ = group_occupied.shape[0], bra_orbitals.shape[2]
    matches = walker_group[:, None] == jnp.arange(group_count, dtype=jnp.int32)[None, :]
    occupied = jnp.sum(jnp.where(matches, group_occupied[None, :], 0), axis=1)
    masks = (jnp.arange(occ, dtype=jnp.int32)[None, :] < occupied[:, None]).astype(BF16)
    bra_t = jnp.swapaxes(bra_orbitals * masks[:, None, :], 1, 2)
    ket_t = jnp.swapaxes(ket_orbitals * masks[:, None, :], 1, 2)
    return jnp.concatenate([bra_t, ket_t], axis=1)


def on_device_8x4(bra, ket, collocation, kernel, walker_weight, walker_group, group_occupied):
    nw, npt = 8, 4
    size_b, size_a = kernel.shape
    occ, size_m = bra.shape
    width = 2 * occ
    me_w, me_p = lax.axis_index("walk"), lax.axis_index("pt")
    z, x, y, core = me_w // 2, me_w % 2, me_p // 2, me_p % 2

    def put(j, i):
        return j * npt + i

    def across(part):
        return send(part, "walk", [(j, j ^ 1) for j in range(nw)])

    def along(part, r):
        return send(part, "walk", [(j, (j - 2 * r) % nw) for j in range(nw)])

    def other(part):
        return send(part, "pt", [(i, i ^ 1) for i in range(npt)])

    tie = lax.optimization_barrier
    half_a = size_a // 2
    rows_alike = lax.dynamic_slice_in_dim(collocation, x * size_a + (1 - core) * half_a, half_a, 0)
    rows_unlike = lax.dynamic_slice_in_dim(collocation, x * size_a + core * half_a, half_a, 0)
    over = [(put(j, j // 2), put(j, j // 2 ^ 2)) for j in range(nw)]
    far_alike, far_unlike = send(rows_alike, BOTH, over), send(rows_unlike, BOTH, over)
    own, half = packed(bra, ket, walker_group, group_occupied, core.reshape(1), walker_weight)
    z1, z3, x0 = along(half, 1), along(half, 3), across(half)
    kernel_t = turned(kernel)
    x0, z1, z3, kernel_t = tie((x0, z1, z3, kernel_t))
    z2, x1, x3 = along(z1, 1), across(z1), across(z3)
    z2, z1, z3 = tie((z2, z1, z3))
    x2 = across(z2)
    near_four = [own] + [h for part in (x0, z1, z3) for h in (part, other(part))]
    side, far_unlike = tie((core.reshape(1), far_unlike))
    lrp, stack, weight_rows = project(side, near_four, [width] + [occ] * 6, collocation, 2, 0)
    far_alike, weight_rows = tie((far_alike, weight_rows))
    first = (lrp, stack, weight_rows)
    x2, *first = tie((x2, *first))
    far_four = [h for part in (x1, x3, z2, x2) for h in (part, other(part))]
    lrp, stack, weight_rows = project(core.reshape(1), far_four, [occ] * 8, collocation, 2, 1, first)
    weights = jnp.concatenate([weight_rows[:4, 0], weight_rows[8:12, 0]])

    beside = [(put(j, j // 2 ^ s), put(j, j // 2 ^ s ^ 1)) for j in range(nw) for s in (0, 2)]
    beside = send(jnp.where(me_p == z, rows_unlike, far_unlike), BOTH, beside)
    col_q = jnp.where(core != z % 2, beside, jnp.where(me_p == z, rows_alike, far_alike))
    lrq = dot(col_q, stack, NT).astype(BF16)
    grads = pair_gradients(weights, (1 - core).reshape(1), kernel_t, lrp, lrq)
    by_rows = (((0,), (1,)), ((), ()))
    give = dot(stack, grads, by_rows).astype(BF16)
    give, scale = tie((give, weights))
    grads = pair_gradients(scale, core.reshape(1), kernel_t, lrp, other(lrq))
    part = (dot(stack, grads, by_rows) + other(give).astype(F32)).reshape(nw // 2, 2, -1, half_a)

    give = lax.dynamic_index_in_dim(part, 1 - y, 1, False).astype(BF16)
    got = send(give, "pt", [(i, i ^ 2) for i in range(npt)])
    part = (lax.dynamic_index_in_dim(part, y, 1, False) + got.astype(F32)).astype(BF16)
    came = []
    for s in range(4):
        pairs = []
        for j in range(nw):
            for i in range(npt):
                pairs.append((put(j, i), put(2 * (s ^ (2 * (j % 2) + i % 2)) + i // 2, j // 2)))
        came.append(send(lax.dynamic_index_in_dim(part, s ^ (2 * x + core), 0, False), BOTH, pairs))
    ordered = [lax.select_n(z, *[came[block ^ s] for s in range(4)]) for block in range(4)]
    return (jnp.concatenate(ordered, axis=1).astype(F32) / jnp.sum(weights)).T


def on_device_any(nw, own, collocation, kernel, walker_weight):
    size_b, size_a = kernel.shape
    size_m = collocation.shape[1]
    me_w, me_p = lax.axis_index("walk"), lax.axis_index("pt")
    weights = lax.all_gather(walker_weight, "walk", axis=0, tiled=True)
    orbitals = lax.all_gather(own, "walk", axis=0, tiled=True)
    all_rows = lax.all_gather(collocation, "pt", axis=0, tiled=True)
    col_q = lax.dynamic_slice_in_dim(all_rows, me_w * size_a, size_a, 0)
    lrp = dot(orbitals, collocation, NT).astype(BF16)
    lrq = dot(col_q, orbitals, NT).astype(BF16)
    grads = pair_gradients(weights / jnp.sum(weights), jnp.zeros(1, jnp.int32), turned(kernel), lrp, lrq)
    part = lax.psum(dot(grads, orbitals), "pt")
    part = jnp.where((me_w * size_a) // size_b == me_p, part, 0.0)
    wide = lax.dynamic_update_slice_in_dim(jnp.zeros((size_b, size_m), F32), part, (me_w * size_a) % size_b, 0)
    return lax.psum_scatter(wide, "walk", scatter_dimension=1, tiled=True)


def on_device(
    nw, npt, bra_orbitals, ket_orbitals, collocation, kernel, walker_weight, walker_group, group_occupied
):
    if (nw, npt, walker_weight.shape[0]) == (8, 4, 1) and kernel.shape[0] == 2 * kernel.shape[1]:
        bra, ket = bra_orbitals[0].T, ket_orbitals[0].T
        return on_device_8x4(bra, ket, collocation, kernel, walker_weight, walker_group, group_occupied)
    own = masked_orbitals(bra_orbitals, ket_orbitals, walker_group, group_occupied)
    return on_device_any(nw, own.reshape(-1, own.shape[2]), collocation, kernel, walker_weight)


def solution(mesh):
    in_specs = (
        P("walk", None, None),
        P("walk", None, None),
        P("pt", None),
        P("pt", "walk"),
        P("walk"),
        P("walk"),
        P(),
    )
    out_specs = P("pt", "walk")
    body = functools.partial(on_device, mesh.shape["walk"], mesh.shape["pt"])
    return jax.shard_map(body, mesh=mesh, in_specs=in_specs, out_specs=out_specs, check_vma=False)
```

```python
import functools

import jax
import jax.numpy as jnp
from jax import lax
from jax.experimental import pallas as pl
from jax.experimental.pallas import tpu as pltpu
from jax.sharding import PartitionSpec as P

F32 = jnp.float32
BF16 = jnp.bfloat16
BOTH = ("walk", "pt")
NT = (((1,), (1,)), ((), ()))
VMEM_LIMIT = 56 * 1024 * 1024


def tile_of(size, limit):
    return next(t for t in range(min(size, limit), 0, -128) if size % t == 0)


def dot(a, b, dims=(((1,), (0,)), ((), ()))):
    return lax.dot_general(a, b, dims, preferred_element_type=F32)


def cost(flops, nbytes):
    return pl.CostEstimate(flops=flops, bytes_accessed=nbytes, transcendentals=0)


def turn_kernel(in_ref, out_ref):
    out_ref[...] = in_ref[...].T


def turned(block):
    rows, cols = block.shape
    tr, tc = tile_of(rows, 512), tile_of(cols, 512)
    return pl.pallas_call(
        turn_kernel,
        out_shape=jax.ShapeDtypeStruct((cols, rows), block.dtype),
        grid=(cols // tc, rows // tr),
        in_specs=[pl.BlockSpec((tr, tc), lambda c, r: (r, c))],
        out_specs=pl.BlockSpec((tc, tr), lambda c, r: (c, r)),
        compiler_params=pltpu.CompilerParams(vmem_limit_bytes=VMEM_LIMIT),
        cost_estimate=cost(0, 10 * rows * cols),
    )(block)


def pack_kernel(group_ref, occupied_ref, side_ref, weight_ref, bra_ref, ket_ref, own_ref, half_ref):
    occ = bra_ref.shape[0]
    used = occupied_ref[group_ref[0]]
    kept = lax.broadcasted_iota(jnp.int32, bra_ref.shape, 0) < used
    bra_t = jnp.where(kept, bra_ref[...].astype(F32), 0.0).astype(BF16)
    ket_t = jnp.where(kept, ket_ref[...].astype(F32), 0.0).astype(BF16)
    own_ref[:occ, :] = bra_t
    own_ref[occ : 2 * occ, :] = ket_t

    @pl.when(side_ref[0] == 0)
    def _():
        half_ref[:occ, :] = bra_t

    @pl.when(side_ref[0] != 0)
    def _():
        half_ref[:occ, :] = ket_t

    shape = (half_ref.shape[0] - occ, half_ref.shape[1])
    row = lax.broadcasted_iota(jnp.int32, shape, 0)
    rest, rows = jnp.full(shape, weight_ref[0], F32), jnp.zeros(shape, F32)
    for part in range(3):
        near = rest.astype(BF16).astype(F32)
        rows = jnp.where(row == part, near, rows)
        rest = rest - near
    half_ref[occ:, :] = rows.astype(BF16)
    own_ref[2 * occ :, :] = rows.astype(BF16)


def packed(bra, ket, group, occupied, side, weight):
    occ, size_m = bra.shape
    smem = pl.BlockSpec(memory_space=pltpu.SMEM)
    return pl.pallas_call(
        pack_kernel,
        out_shape=[
            jax.ShapeDtypeStruct((2 * occ + 16, size_m), BF16),
            jax.ShapeDtypeStruct((occ + 16, size_m), BF16),
        ],
        in_specs=[smem] * 4 + [pl.BlockSpec(memory_space=pltpu.VMEM)] * 2,
        compiler_params=pltpu.CompilerParams(vmem_limit_bytes=VMEM_LIMIT),
        cost_estimate=cost(0, 12 * size_m * occ),
    )(group, occupied, side, weight, bra, ket)


def project_kernel(rows_each, waits, *refs):
    count = len(rows_each)
    side_ref, items, col_ref = refs[0], refs[1 : count + 1], refs[count + 1]
    out_ref, stack_out, weight_out, stack = refs[count + 2 + waits :]
    occ = min(rows_each)
    width = 2 * occ

    @pl.when(pl.program_id(0) == 0)
    def _():
        at = 0
        weight_out[...] = jnp.zeros_like(weight_out)
        for ref, rows in zip(items, rows_each):
            if rows == occ:
                place = at // width * width + (side_ref[0] if at % width == 0 else 1 - side_ref[0]) * occ
                stack[pl.ds(pl.multiple_of(place, occ), rows), :] = ref[:rows, :]
            else:
                stack[at : at + rows, :] = ref[:rows, :]
            if at % width == 0:
                s = at // width
                weight_out[s : s + 1, :] = jnp.sum(ref[rows : rows + 16, :128].astype(F32), axis=0, keepdims=True)
            at += rows
        stack_out[...] = stack[...]

    out_ref[...] = dot(stack[...], col_ref[...], NT).astype(BF16)


def project(side, items, rows_each, col, groups, index, before=()):
    size_m, size, total = col.shape[1], col.shape[0], sum(rows_each)
    tile = tile_of(size, 512)
    return pl.pallas_call(
        functools.partial(project_kernel, tuple(rows_each), len(before)),
        out_shape=[
            jax.ShapeDtypeStruct((groups * total, size), BF16),
            jax.ShapeDtypeStruct((groups * total, size_m), BF16),
            jax.ShapeDtypeStruct((groups * 8, 128), F32),
        ],
        grid=(size // tile,),
        in_specs=[pl.BlockSpec(memory_space=pltpu.SMEM)]
        + [pl.BlockSpec(x.shape, lambda b: (0, 0), pipeline_mode=pl.Buffered(1)) for x in items]
        + [pl.BlockSpec((tile, size_m), lambda b: (b, 0))]
        + [pl.BlockSpec(memory_space=pl.ANY)] * (len(before)),
        out_specs=[
            pl.BlockSpec((total, tile), lambda b: (index, b)),
            pl.BlockSpec((total, size_m), lambda b: (index, 0), pipeline_mode=pl.Buffered(1)),
            pl.BlockSpec((8, 128), lambda b: (index, 0)),
        ],
        scratch_shapes=[pltpu.VMEM((total, size_m), BF16)],
        input_output_aliases={len(items) + 2 + n: n for n in range(len(before))},
        compiler_params=pltpu.CompilerParams(vmem_limit_bytes=VMEM_LIMIT),
        cost_estimate=cost(2 * (total + 640) * size_m * size, 2 * size_m * size),
    )(side, *items, col, *before)


def pair_kernel(sub, weight_ref, block_ref, kt_ref, lrp_ref, lrq_ref, out_ref):
    rows, size_b = kt_ref.shape
    occ = lrp_ref.shape[0] // 4
    sides = [lrq_ref[:, n * occ : (n + 1) * occ] for n in range(4)]
    totals = [jnp.zeros((rows, occ), F32) for _ in range(4)]
    for at in range(0, size_b, sub):
        kern = kt_ref[:, at : at + sub].astype(F32)
        for n in (0, 2):
            left_t = lrp_ref[n * occ : (n + 1) * occ, at : at + sub]
            right_t = lrp_ref[(n + 1) * occ : (n + 2) * occ, at : at + sub]
            had_t = (kern * dot(sides[n + 1], left_t)).astype(BF16)
            had = (kern * dot(sides[n], right_t)).astype(BF16)
            totals[n] += dot(had_t, right_t, NT)
            totals[n + 1] += dot(had, left_t, NT)
    for n in range(4):
        scale = 2.0 * weight_ref[2 * pl.program_id(0) + n // 2]
        out_ref[:, n * occ : (n + 1) * occ] = (totals[n] * scale).astype(BF16)


def pair_gradients(weights, block, kernel_t, lrp, lrq):
    size_b, rows, count = kernel_t.shape[1], lrq.shape[0], weights.shape[0] // 2
    width = lrp.shape[0] // count
    sub = tile_of(size_b, 512)
    return pl.pallas_call(
        functools.partial(pair_kernel, sub),
        out_shape=jax.ShapeDtypeStruct((rows, count * width), BF16),
        grid_spec=pltpu.PrefetchScalarGridSpec(
            num_scalar_prefetch=2,
            grid=(count,),
            in_specs=[
                pl.BlockSpec((rows, size_b), lambda p, w, s: (s[0], 0), pipeline_mode=pl.Buffered(1)),
                pl.BlockSpec((width, size_b), lambda p, w, s: (p, 0)),
                pl.BlockSpec((rows, width), lambda p, w, s: (0, p)),
            ],
            out_specs=pl.BlockSpec((rows, width), lambda p, w, s: (0, p)),
        ),
        compiler_params=pltpu.CompilerParams(vmem_limit_bytes=VMEM_LIMIT),
        cost_estimate=cost(2 * 8 * count * 256 * rows * size_b, 2 * count * (rows + width) * size_b),
    )(weights, block, kernel_t, lrp, lrq)


def send(x, axes, pairs):
    return lax.ppermute(x, axes, pairs)


def masked_orbitals(bra_orbitals, ket_orbitals, walker_group, group_occupied):
    group_count, occ = group_occupied.shape[0], bra_orbitals.shape[2]
    matches = walker_group[:, None] == jnp.arange(group_count, dtype=jnp.int32)[None, :]
    occupied = jnp.sum(jnp.where(matches, group_occupied[None, :], 0), axis=1)
    masks = (jnp.arange(occ, dtype=jnp.int32)[None, :] < occupied[:, None]).astype(BF16)
    bra_t = jnp.swapaxes(bra_orbitals * masks[:, None, :], 1, 2)
    ket_t = jnp.swapaxes(ket_orbitals * masks[:, None, :], 1, 2)
    return jnp.concatenate([bra_t, ket_t], axis=1)


def on_device_8x4(bra, ket, collocation, kernel, walker_weight, walker_group, group_occupied):
    nw, npt = 8, 4
    size_b, size_a = kernel.shape
    occ, size_m = bra.shape
    width = 2 * occ
    me_w, me_p = lax.axis_index("walk"), lax.axis_index("pt")
    z, x, y, core = me_w // 2, me_w % 2, me_p // 2, me_p % 2

    def put(j, i):
        return j * npt + i

    def across(part):
        return send(part, "walk", [(j, j ^ 1) for j in range(nw)])

    def along(part, r):
        return send(part, "walk", [(j, (j - 2 * r) % nw) for j in range(nw)])

    def other(part):
        return send(part, "pt", [(i, i ^ 1) for i in range(npt)])

    tie = lax.optimization_barrier
    half_a = size_a // 2
    rows_alike = lax.dynamic_slice_in_dim(collocation, x * size_a + (1 - core) * half_a, half_a, 0)
    rows_unlike = lax.dynamic_slice_in_dim(collocation, x * size_a + core * half_a, half_a, 0)
    over = [(put(j, j // 2), put(j, j // 2 ^ 2)) for j in range(nw)]
    far_alike, far_unlike = send(rows_alike, BOTH, over), send(rows_unlike, BOTH, over)
    own, half = packed(bra, ket, walker_group, group_occupied, core.reshape(1), walker_weight)
    z1, z3, x0 = along(half, 1), along(half, 3), across(half)
    kernel_t = turned(kernel)
    x0, z1, z3, kernel_t = tie((x0, z1, z3, kernel_t))
    z2, x1, x3 = along(z1, 1), across(z1), across(z3)
    z2, z1, z3 = tie((z2, z1, z3))
    x2 = across(z2)
    near_four = [own] + [h for part in (x0, z1, z3) for h in (part, other(part))]
    side, far_unlike = tie((core.reshape(1), far_unlike))
    lrp, stack, weight_rows = project(side, near_four, [width] + [occ] * 6, collocation, 2, 0)
    far_alike, weight_rows = tie((far_alike, weight_rows))
    first = (lrp, stack, weight_rows)
    x1, x3, x2, *first = tie((x1, x3, x2, *first))
    far_four = [h for part in (x1, x3, z2, x2) for h in (part, other(part))]
    lrp, stack, weight_rows = project(core.reshape(1), far_four, [occ] * 8, collocation, 2, 1, first)
    weights = jnp.concatenate([weight_rows[:4, 0], weight_rows[8:12, 0]])

    beside = [(put(j, j // 2 ^ s), put(j, j // 2 ^ s ^ 1)) for j in range(nw) for s in (0, 2)]
    beside = send(jnp.where(me_p == z, rows_unlike, far_unlike), BOTH, beside)
    col_q = jnp.where(core != z % 2, beside, jnp.where(me_p == z, rows_alike, far_alike))
    lrq = dot(col_q, stack, NT).astype(BF16)
    grads = pair_gradients(weights, (1 - core).reshape(1), kernel_t, lrp, lrq)
    by_rows = (((0,), (1,)), ((), ()))
    give = dot(stack, grads, by_rows).astype(BF16)
    give, scale = tie((give, weights))
    grads = pair_gradients(scale, core.reshape(1), kernel_t, lrp, other(lrq))
    part = (dot(stack, grads, by_rows) + other(give).astype(F32)).reshape(nw // 2, 2, -1, half_a)

    give = lax.dynamic_index_in_dim(part, 1 - y, 1, False).astype(BF16)
    got = send(give, "pt", [(i, i ^ 2) for i in range(npt)])
    part = (lax.dynamic_index_in_dim(part, y, 1, False) + got.astype(F32)).astype(BF16)
    came = []
    for s in range(4):
        pairs = []
        for j in range(nw):
            for i in range(npt):
                pairs.append((put(j, i), put(2 * (s ^ (2 * (j % 2) + i % 2)) + i // 2, j // 2)))
        came.append(send(lax.dynamic_index_in_dim(part, s ^ (2 * x + core), 0, False), BOTH, pairs))
    ordered = [lax.select_n(z, *[came[block ^ s] for s in range(4)]) for block in range(4)]
    return (jnp.concatenate(ordered, axis=1).astype(F32) / jnp.sum(weights)).T


def on_device_any(nw, own, collocation, kernel, walker_weight):
    size_b, size_a = kernel.shape
    size_m = collocation.shape[1]
    me_w, me_p = lax.axis_index("walk"), lax.axis_index("pt")
    weights = lax.all_gather(walker_weight, "walk", axis=0, tiled=True)
    orbitals = lax.all_gather(own, "walk", axis=0, tiled=True)
    all_rows = lax.all_gather(collocation, "pt", axis=0, tiled=True)
    col_q = lax.dynamic_slice_in_dim(all_rows, me_w * size_a, size_a, 0)
    lrp = dot(orbitals, collocation, NT).astype(BF16)
    lrq = dot(col_q, orbitals, NT).astype(BF16)
    grads = pair_gradients(weights / jnp.sum(weights), jnp.zeros(1, jnp.int32), turned(kernel), lrp, lrq)
    part = lax.psum(dot(grads, orbitals), "pt")
    part = jnp.where((me_w * size_a) // size_b == me_p, part, 0.0)
    wide = lax.dynamic_update_slice_in_dim(jnp.zeros((size_b, size_m), F32), part, (me_w * size_a) % size_b, 0)
    return lax.psum_scatter(wide, "walk", scatter_dimension=1, tiled=True)


def on_device(
    nw, npt, bra_orbitals, ket_orbitals, collocation, kernel, walker_weight, walker_group, group_occupied
):
    if (nw, npt, walker_weight.shape[0]) == (8, 4, 1) and kernel.shape[0] == 2 * kernel.shape[1]:
        bra, ket = bra_orbitals[0].T, ket_orbitals[0].T
        return on_device_8x4(bra, ket, collocation, kernel, walker_weight, walker_group, group_occupied)
    own = masked_orbitals(bra_orbitals, ket_orbitals, walker_group, group_occupied)
    return on_device_any(nw, own.reshape(-1, own.shape[2]), collocation, kernel, walker_weight)


def solution(mesh):
    in_specs = (
        P("walk", None, None),
        P("walk", None, None),
        P("pt", None),
        P("pt", "walk"),
        P("walk"),
        P("walk"),
        P(),
    )
    out_specs = P("pt", "walk")
    body = functools.partial(on_device, mesh.shape["walk"], mesh.shape["pt"])
    return jax.shard_map(body, mesh=mesh, in_specs=in_specs, out_specs=out_specs, check_vma=False)
```
